256 devices in a mesh: gx: 16 (over z, core), gy: 16 (over y, x).
Axes of the slice: x: 4, y: 4, z: 8, core: 2. Of those that a mesh axis runs over, the one named last changes fastest.
Arguments:
- initial: float32 [2048, 4096], P(('gx', 'gy')), may hold values from -3 to 3
- source: float32 [2048, 4096], P(('gx', 'gy')), may hold values from -6 to 6
- permeability: float32 [2048, 4096], P(('gx', 'gy')), may hold values from 0.5 to 4
- migrate_x: int32 [2048], P(('gx', 'gy')), may hold values from 0 to 15, as said below
- migrate_y: int32 [2048], P(('gx', 'gy')), may hold values from 0 to 15, as said below
- neighbours: int32 [2048, 6], P(('gx', 'gy')), may hold values from -1 to 39, as said below
- children: int32 [2048], P(('gx', 'gy')), may hold values from 0 to 23, as said below
- parents: int32 [2048], P(('gx', 'gy')), may hold values from 0 to 23, as said below
Outputs:
- solution: float32 [2048, 4096], P(('gx', 'gy'))
- residual: float32 [2048, 4096], P(('gx', 'gy'))
The draws below stay inside these ranges and needn't reach their ends.
Inputs may be any that keep to these rules, and one draw needn't show every extreme that they name: `migrate_x`: within each pair of devices whose gx index differs in the lowest bit, every block of the pair lands in exactly one slot; a device takes at most 2 blocks from its partner, and some device takes exactly 2. `migrate_y`: refers to the layout after the gx migration; within each pair of devices whose gy index differs in the lowest bit, every block lands in exactly one slot; a device takes at most 2 blocks from its partner, and some device takes exactly 2. `neighbours`: refers to the layout after both migrations; never names a device outside the mesh; on each device at most 6 entries name one given neighbouring device, and exactly 6 wherever that device exists. `children`: refers to the layout after both migrations; every block of every device is named by exactly one position; on each device exactly 1 entries name the gx partner and exactly 1 the gy partner. `parents`: the inverse of children: the position whose entry names the block, as src * 8 + position with src 0 own device, 1 the gx partner, 2 the gy partner; on each device exactly 1 entries have src 1 and exactly 1 src 2.
All inputs are finite; a program needn't handle non-finite values.
Results may differ from the reference program's by a relative error of at most 0.00002.
Values sent between devices are 32-bit elements; how exact they have to be, the bound alone decides.
A program may use at most 192 MiB of HBM per device.

```python
import math
import jax
import jax.numpy as jnp

BLK_DEV = 8
CELLS = 4096
INNER = 3
COARSE = 4
MOVE = 2
CROSS = 1
BLOCKS = 2048
N_GX = 16
N_GY = 16


def pair_tables(key, along):
    if along == 0:
        pairs = (N_GX // 2, N_GY)
    else:
        pairs = (N_GX, N_GY // 2)
    count = pairs[0] * pairs[1]
    keys = jax.random.split(key, 5)

    def orders(base_key):
        return jax.vmap(lambda single: jax.random.permutation(single, BLK_DEV).astype(jnp.int32))(jax.random.split(base_key, count))
    first_out, second_out, first_in, second_in = (orders(keys[0]), orders(keys[1]), orders(keys[2]), orders(keys[3]))
    moved = jax.random.randint(keys[4], (count,), MOVE // 2, MOVE + 1).astype(jnp.int32).at[0].set(MOVE)
    early = jnp.arange(BLK_DEV, dtype=jnp.int32)[None, :] < moved[:, None]
    first_vals = jnp.where(early, BLK_DEV + second_out, first_out)
    second_vals = jnp.where(early, BLK_DEV + first_out, second_out)
    place = jax.vmap(lambda order, vals: jnp.zeros((BLK_DEV,), jnp.int32).at[order].set(vals))
    first_table = place(first_in, first_vals).reshape(pairs + (BLK_DEV,))
    second_table = place(second_in, second_vals).reshape(pairs + (BLK_DEV,))
    if along == 0:
        whole = jnp.stack([first_table, second_table], 1).reshape(N_GX, N_GY, BLK_DEV)
    else:
        whole = jnp.stack([first_table, second_table], 2).reshape(N_GX, N_GY, BLK_DEV)
    return whole.reshape(-1).astype(jnp.int32)


def chosen_positions(key, pool, count):
    half = pool.shape[0]
    orders = jax.vmap(lambda single: jax.random.permutation(single, half).astype(jnp.int32))(jax.random.split(key, count))
    picks = pool[orders[:, :CROSS]]
    rows = jnp.arange(count, dtype=jnp.int32)[:, None]
    return jnp.zeros((count, BLK_DEV), jnp.int32).at[rows, picks].set(1)


def family_tables(key):
    keys = jax.random.split(key, 4)
    sigma = jax.vmap(lambda single: jax.random.permutation(single, BLK_DEV).astype(jnp.int32))(jax.random.split(keys[0], N_GX * N_GY)).reshape(N_GX, N_GY, BLK_DEV)
    order = jax.random.permutation(keys[1], BLK_DEV).astype(jnp.int32)
    half = BLK_DEV // 2
    flip_x = chosen_positions(keys[2], order[:half], N_GX // 2 * N_GY).reshape(N_GX // 2, N_GY, BLK_DEV)
    flip_x = jnp.repeat(flip_x, 2, axis=0)
    flip_y = chosen_positions(keys[3], order[half:], N_GX * (N_GY // 2)).reshape(N_GX, N_GY // 2, BLK_DEV)
    flip_y = jnp.repeat(flip_y, 2, axis=1)
    swap_x = flip_x == 1
    swap_y = flip_y == 1
    sigma_px = sigma.reshape(N_GX // 2, 2, N_GY, BLK_DEV)[:, ::-1].reshape(N_GX, N_GY, BLK_DEV)
    sigma_py = sigma.reshape(N_GX, N_GY // 2, 2, BLK_DEV)[:, :, ::-1].reshape(N_GX, N_GY, BLK_DEV)
    kids = jnp.where(swap_x, BLK_DEV + sigma_px, jnp.where(swap_y, 2 * BLK_DEV + sigma_py, sigma))
    inverse = jnp.argsort(sigma, axis=-1).astype(jnp.int32)
    moved_x = jnp.take_along_axis(swap_x, inverse, -1)
    moved_y = jnp.take_along_axis(swap_y, inverse, -1)
    owners = jnp.where(moved_x, BLK_DEV + inverse, jnp.where(moved_y, 2 * BLK_DEV + inverse, inverse))
    return (kids.reshape(-1).astype(jnp.int32), owners.reshape(-1).astype(jnp.int32))


def draw_migrate_x(key, part):
    key = jax.random.fold_in(key, 11)
    return pair_tables(key, 0)


def draw_migrate_y(key, part):
    key = jax.random.fold_in(key, 12)
    return pair_tables(key, 1)


def draw_neighbours(key, part):
    key = jax.random.fold_in(key, 13)
    first_key, second_key = jax.random.split(key)
    shape = (N_GX, N_GY, BLK_DEV, 6)
    total = 6 * BLK_DEV
    pattern = jnp.array([0, 0, 0, 1, 2, 3, 4, -1], jnp.int32)[jnp.arange(total, dtype=jnp.int32) * 8 // total]
    orders = jax.vmap(lambda single: jax.random.permutation(single, total).astype(jnp.int32))(jax.random.split(first_key, N_GX * N_GY))
    direction = pattern[orders].reshape(shape)
    place_x = jnp.arange(N_GX, dtype=jnp.int32)[:, None, None, None]
    place_y = jnp.arange(N_GY, dtype=jnp.int32)[None, :, None, None]
    outside = (direction == 1) & (place_x == 0) | (direction == 2) & (place_x == N_GX - 1)
    outside = outside | (direction == 3) & (place_y == 0) | (direction == 4) & (place_y == N_GY - 1)
    direction = jnp.where(outside, -1, direction)
    slot = jax.random.randint(second_key, shape, 0, BLK_DEV).astype(jnp.int32)
    code = jnp.where(direction >= 0, direction * BLK_DEV + slot, -1)
    return code.reshape(N_GX * N_GY * BLK_DEV, 6).astype(jnp.int32)


def draw_children(key, part):
    shared = family_tables(key)
    return shared[0]


def draw_parents(key, part):
    shared = family_tables(key)
    return shared[1]


def block_levels(rng, shape, shards, low, top_value):
    factor_of, own = 1.0, jax.random.fold_in(rng, 6)
    for position, blocks in shards:
        heights = jnp.exp(jax.random.uniform(jax.random.fold_in(own, position), (blocks,), jnp.float32, low / len(shards), top_value / len(shards)))
        factor_of = factor_of * jnp.repeat(heights, shape[position] // blocks).reshape([-1 if axis == position else 1 for axis in range(len(shape))])
    return factor_of


def noise(stream_key, shape, scale, most, cuts=(), kind=jnp.bfloat16):
    values = jax.random.normal(stream_key, shape, jnp.float32) * scale
    if len(cuts) > 0:
        values = block_levels(stream_key, shape, cuts, -0.22, 0.18) * values
    return jnp.clip(values, min=-most, max=most).astype(kind)


def setup_inputs(seed: int = 0) -> dict:
    arg_keys = jax.random.split(jax.random.key(seed), 9)
    return {
        "initial": noise(arg_keys[0], (BLOCKS, CELLS), 0.5, 3.0, ((0, 256),), jnp.float32),
        "source": noise(arg_keys[1], (BLOCKS, CELLS), 1.0, 6.0, ((0, 256),), jnp.float32),
        "permeability": jnp.clip(jnp.exp(math.log(4.0) - 2.0794415 * jax.random.uniform(arg_keys[2], (BLOCKS, CELLS), jnp.float32) ** block_levels(arg_keys[2], (BLOCKS, CELLS), ((0, 256),), -0.2, 0.2)), 0.5, 4.0),
        "migrate_x": draw_migrate_x(jax.random.fold_in(arg_keys[8], 71), 0),
        "migrate_y": draw_migrate_y(jax.random.fold_in(arg_keys[8], 71), 0),
        "neighbours": draw_neighbours(jax.random.fold_in(arg_keys[8], 71), 0),
        "children": draw_children(jax.random.fold_in(arg_keys[8], 71), 0),
        "parents": draw_parents(jax.random.fold_in(arg_keys[8], 71), 0),
    }


REACTION = 0.25
DAMPING = 0.8


def faces_of(values):
    return jnp.stack([values[:, 0], values[:, -1], values[:, :, 0], values[:, :, -1], values[:, :, :, 0], values[:, :, :, -1]], 1)


def operator(values, ghosts, coefficient, scale):
    beside = (
        jnp.concatenate([ghosts[:, 0:1], values[:, :-1]], 1),
        jnp.concatenate([values[:, 1:], ghosts[:, 1:2]], 1),
        jnp.concatenate([ghosts[:, 2][:, :, None], values[:, :, :-1]], 2),
        jnp.concatenate([values[:, :, 1:], ghosts[:, 3][:, :, None]], 2),
        jnp.concatenate([ghosts[:, 4][..., None], values[..., :-1]], 3),
        jnp.concatenate([values[..., 1:], ghosts[:, 5][..., None]], 3),
    )
    mobility = 0.5 + values * values
    flux_sum = jnp.zeros_like(values)
    conduct_sum = jnp.zeros_like(values)
    for other in beside:
        conduct = 0.5 * (mobility + 0.5 + other * other)
        flux_sum = flux_sum + conduct * (values - other)
        conduct_sum = conduct_sum + conduct
    image = REACTION * values + scale * coefficient * flux_sum
    diagonal = REACTION + scale * coefficient * conduct_sum
    return image, diagonal


def shrink(values):
    return values.reshape(-1, 8, 2, 8, 2, 8, 2).mean(axis=(2, 4, 6)).reshape(-1, 512)


def assemble(pieces):
    return pieces.reshape(-1, 2, 2, 2, 3, 8, 8, 8).transpose(0, 4, 1, 5, 2, 6, 3, 7).reshape(-1, 3, 16, 16, 16)


def split_octants(values):
    return values.reshape(-1, 2, 8, 2, 8, 2, 8).transpose(0, 1, 3, 5, 2, 4, 6).reshape(-1, 512)


def upsample(pieces):
    count = pieces.shape[0]
    spread = jnp.broadcast_to(pieces.reshape(count, 8, 1, 8, 1, 8, 1), (count, 8, 2, 8, 2, 8, 2))
    return spread.reshape(count, 16, 16, 16)


def partner_x(values):
    shape = values.shape
    return values.reshape((N_GX // 2, 2) + shape[1:])[:, ::-1].reshape(shape)


def partner_y(values):
    shape = values.shape
    return values.reshape((N_GX, N_GY // 2, 2) + shape[2:])[:, :, ::-1].reshape(shape)


def migrate(fields, table, partner):
    combined = jnp.concatenate([fields, partner(fields)], 2)
    return jnp.take_along_axis(combined, table[:, :, :, None, None], 2)


def global_ghosts(values, links):
    faces = faces_of(values).reshape(-1, 256)
    present = links >= 0
    code = jnp.where(present, links, 0)
    direction = code // BLK_DEV
    slot = code % BLK_DEV
    step_x = jnp.array([0, -1, 1, 0, 0], jnp.int32)[direction]
    step_y = jnp.array([0, 0, 0, -1, 1], jnp.int32)[direction]
    row_x = jnp.arange(N_GX, dtype=jnp.int32)[:, None, None, None] + step_x
    row_y = jnp.arange(N_GY, dtype=jnp.int32)[None, :, None, None] + step_y
    opposite = jnp.array([1, 0, 3, 2, 5, 4], jnp.int32)
    indices = ((row_x * N_GY + row_y) * BLK_DEV + slot) * 6 + opposite
    ghosts = jnp.take(faces, indices.reshape(-1), axis=0).reshape(-1, 6, 16, 16)
    return jnp.where(present.reshape(-1, 6, 1, 1), ghosts, 0.0)


def reference(initial, source, permeability, migrate_x, migrate_y, neighbours, children, parents):
    layout = (N_GX, N_GY, BLK_DEV)
    fields = jnp.stack([initial, source, permeability], 1).reshape(layout + (3, 4096))
    fields = migrate(fields, migrate_x.reshape(layout), partner_x)
    fields = migrate(fields, migrate_y.reshape(layout), partner_y)
    cells = fields.reshape(-1, 3, 16, 16, 16)
    solution, forcing, perm_cells = cells[:, 0], cells[:, 1], cells[:, 2]
    links = neighbours.reshape(layout + (6,))

    def smooth(values):
        ghosts = global_ghosts(values, links)
        for repeat in range(INNER):
            image, diagonal = operator(values, ghosts, perm_cells, 1.0)
            values = values + DAMPING * (forcing - image) / diagonal
        return values

    solution = smooth(solution)
    image, unused = operator(solution, global_ghosts(solution, links), perm_cells, 1.0)
    residual = forcing - image
    pieces = jnp.stack([shrink(solution), shrink(residual), shrink(perm_cells)], 1).reshape(layout + (3, 512))
    gathered = jnp.concatenate([pieces, partner_x(pieces), partner_y(pieces)], 2)
    coarse = assemble(jnp.take_along_axis(gathered, children.reshape(layout)[:, :, :, None, None], 2).reshape(-1, 3, 512))
    coarse_sol, coarse_res, coarse_perm = coarse[:, 0], coarse[:, 1], coarse[:, 2]
    zero_ghosts = jnp.zeros((coarse_sol.shape[0], 6, 16, 16), coarse_sol.dtype)
    image, unused = operator(coarse_sol, zero_ghosts, coarse_perm, 0.25)
    coarse_force = image + coarse_res
    iterate = coarse_sol
    for repeat in range(COARSE):
        image, diagonal = operator(iterate, zero_ghosts, coarse_perm, 0.25)
        iterate = iterate + DAMPING * (coarse_force - image) / diagonal
    correction = split_octants(iterate - coarse_sol).reshape(layout + (512,))
    gathered = jnp.concatenate([correction, partner_x(correction), partner_y(correction)], 2)
    taken = jnp.take_along_axis(gathered, parents.reshape(layout)[:, :, :, None], 2).reshape(-1, 512)
    solution = smooth(solution + upsample(taken))
    return solution.reshape(-1, 4096), residual.reshape(-1, 4096)
```

```python
import functools

import jax
import jax.numpy as jnp
from jax import lax
from jax.experimental import pallas as pl
from jax.experimental.pallas import tpu as pltpu
from jax.sharding import PartitionSpec as P

INNER = 3
COARSE = 4
REACTION = 0.25
DAMPING = 0.8
OPP = (1, 0, 3, 2)

F32 = jnp.float32
I32 = jnp.int32
BF16 = jnp.bfloat16

_ROWS = lax.GatherDimensionNumbers(
    offset_dims=(),
    collapsed_slice_dims=(0,),
    start_index_map=(0,),
    operand_batching_dims=(1,),
    start_indices_batching_dims=(1,),
)


def rows(x, index):
    return lax.gather(
        x, index[..., None], _ROWS, (1, 1), mode=lax.GatherScatterMode.PROMISE_IN_BOUNDS
    )


def roll(x, shift):
    return pltpu.roll(x, shift % 128, 1) if shift % 128 else x


def split3(x):
    high = x.astype(BF16)
    rest = x - high.astype(F32)
    mid = rest.astype(BF16)
    low = (rest - mid.astype(F32)).astype(BF16)
    return high, mid, low


def exact_dot(x, matrix):
    count = x.shape[0]
    out = jnp.dot(jnp.concatenate(split3(x), 0), matrix, preferred_element_type=F32)
    return out[:count] + (out[count : 2 * count] + out[2 * count :])


def kernel(
    init_h, src_h, perm_h, mx_h, my_h, nb_h, ch_h, pa_h, sol_h, res_h,
    own, px, t_mx, t_my, t_ch, t_pa, nbv, msg_s, msg_r, yi_s, yi_r, yf_s, yf_r,
    va, vb, fr, qr, sb, sc, gb, gc, gs, gr, ps, pxr, pyr, pd_s, pd_r,
    ea, eb, e0, ef, eq, cor, zz, restrict_m, upsample_m, sol_v, res_v,
    lsem, ssem, rsem,
):
    i, j = lax.axis_index("gx"), lax.axis_index("gy")
    nx, ny = lax.axis_size("gx"), lax.axis_size("gy")
    xp = (i + 1 - 2 * (i % 2), j)
    yp = (i, j + 1 - 2 * (j % 2))
    diag = (xp[0], yp[1])
    around = (((i + nx - 1) % nx, j), ((i + 1) % nx, j), (i, (j + ny - 1) % ny), (i, (j + 1) % ny))

    barrier = pltpu.get_barrier_semaphore()
    for peer in around + (diag,):
        pl.semaphore_signal(barrier, inc=1, device_id=peer, device_id_type=pl.DeviceIdType.MESH)

    tables = [
        pltpu.make_async_copy(a, b, lsem.at[n])
        for n, (a, b) in enumerate(
            ((mx_h, t_mx), (my_h, t_my), (ch_h, t_ch), (pa_h, t_pa), (nb_h, nbv))
        )
    ]
    for copy in tables:
        copy.start()
    fields = [
        pltpu.make_async_copy(a, own.at[n], lsem.at[5 + n])
        for n, a in enumerate((init_h, src_h, perm_h))
    ]
    for copy in fields:
        copy.start()

    used = [0]

    def push(source, target, peer, there=None):
        n = used[0]
        if there is None:
            there = n
            used[0] += 1
        return pltpu.make_async_remote_copy(
            src_ref=source,
            dst_ref=target,
            send_sem=ssem.at[n if there == n else n],
            recv_sem=rsem.at[there],
            device_id=peer,
            device_id_type=pl.DeviceIdType.MESH,
        )

    def push_around(sources, target):
        base = used[0]
        used[0] += 4
        return [
            pltpu.make_async_remote_copy(
                src_ref=sources(d),
                dst_ref=target(OPP[d]),
                send_sem=ssem.at[base + d],
                recv_sem=rsem.at[base + OPP[d]],
                device_id=around[d],
                device_id_type=pl.DeviceIdType.MESH,
            )
            for d in range(4)
        ]

    pl.semaphore_wait(barrier, 5)
    x_copies = [push(a, px.at[n], xp) for n, a in enumerate((init_h, src_h, perm_h))]
    for copy in x_copies:
        copy.start()

    lane = lax.broadcasted_iota(I32, (8, 128), 1)
    sub = lax.broadcasted_iota(I32, (8, 128), 0)
    zero = jnp.zeros((8, 128), F32)

    for copy in tables:
        copy.wait()

    def column(ref):
        out = jnp.full((8, 128), ref[0], I32)
        for k in range(1, 8):
            out = jnp.where(sub == k, ref[k], out)
        return out

    mx, my, ch, pa = column(t_mx), column(t_my), column(t_ch), column(t_pa)

    links = [jnp.broadcast_to(nbv[:, f : f + 1], (8, 128)) for f in range(6)]
    away = [jnp.where(c >= 0, c // 8, 7) for c in links]
    slot = [jnp.where(c >= 0, c % 8, 0) for c in links]
    marks = jnp.concatenate([(lane == d).astype(F32) for d in away], 0)
    before = (
        lax.broadcasted_iota(I32, (48, 48), 1) < lax.broadcasted_iota(I32, (48, 48), 0)
    ).astype(F32)
    counts = jnp.dot(before, marks, preferred_element_type=F32)
    rank = []
    wanted = zero
    for f in range(6):
        mine = jnp.where(lane == away[f], counts[8 * f : 8 * f + 8], 0.0)
        place = jnp.broadcast_to(jnp.sum(mine, axis=1, keepdims=True), (8, 128)).astype(I32)
        place = jnp.minimum(place, 7)
        rank.append(place)
        remote = (away[f] >= 1) & (away[f] <= 4)
        hit = (lane == away[f] * 8 + place) & remote
        wanted = wanted + jnp.where(hit, ((f ^ 1) * 8 + slot[f]).astype(F32), 0.0)
    msg_s[0:8, :] = jnp.broadcast_to(jnp.sum(wanted, axis=0, keepdims=True), (8, 128))
    msg_s[8:16, :] = ch.astype(F32)
    msgs = push_around(lambda d: msg_s, lambda d: msg_r.at[d])
    for copy in msgs:
        copy.start()

    named = sub == t_my[0]
    for k in range(1, 8):
        named = named | (sub == t_my[k])
    free = jnp.where(named, 8.0, sub.astype(F32))
    first = jnp.min(free, axis=0, keepdims=True)
    last = jnp.max(jnp.where(named, 0.0, sub.astype(F32)), axis=0, keepdims=True)
    leave = jnp.where(sub % 2 == 0, jnp.broadcast_to(first, (8, 128)), jnp.broadcast_to(last, (8, 128)))
    leave = jnp.minimum(leave, 7.0).astype(I32)
    leave_e = rows(mx, leave)
    leave_own, leave_row = leave_e < 8, leave_e % 8
    stay = my < 8
    final_e = rows(mx, my % 8)
    final_own, final_row = final_e < 8, final_e % 8
    order = jnp.zeros((8, 128), I32)
    for k in range(8):
        entry = t_my[k]
        order = order + jnp.where((entry >= 8) & (my > entry), 1, 0)
    final_first = order == 0

    fine = lax.broadcasted_iota(I32, (256, 128), 0)
    small = lax.broadcasted_iota(I32, (256, 128), 1)
    same = (fine // 32 == small // 16) & ((fine % 16) // 2 == small % 8)
    restrict_m[...] = jnp.where(same, 0.125, 0.0).astype(BF16)
    fine = lax.broadcasted_iota(I32, (128, 256), 1)
    small = lax.broadcasted_iota(I32, (128, 256), 0)
    same = (fine // 32 == small // 16) & ((fine % 16) // 2 == small % 16)
    upsample_m[...] = jnp.where(same, 1.0, 0.0).astype(BF16)

    def leaving(n, c):
        cols = pl.ds(128 * c, 128)
        return jnp.where(leave_own, rows(own[n, :, cols], leave_row), rows(px[n, :, cols], leave_row))

    fields[0].wait()
    x_copies[0].wait_recv()
    for c in range(32):
        yi_s[c] = leaving(0, c)[0:2]
    y_first = push(yi_s, yi_r, yp)
    y_first.start()
    for n in (1, 2):
        fields[n].wait()
        x_copies[n].wait_recv()
    for c in range(32):
        yf_s[c] = jnp.where(sub < 2, leaving(1, c), leaving(2, c))[0:4]
    y_second = push(yf_s, yf_r, yp)
    y_second.start()

    for copy in msgs:
        copy.wait_recv()
    give = []
    for d in range(4):
        code = jnp.where(lane == (OPP[d] + 1) * 8 + sub, msg_r[d, 0:8, :], 0.0)
        code = jnp.broadcast_to(jnp.sum(code, axis=1, keepdims=True), (8, 128)).astype(I32)
        give.append((code // 8, code % 8))
    ch_x = msg_r[1 - i % 2, 8:16, :].astype(I32)
    ch_y = msg_r[3 - j % 2, 8:16, :].astype(I32)

    def arrived(n, ref, top, c):
        cols = pl.ds(128 * c, 128)
        kept = jnp.where(final_own, rows(own[n, :, cols], final_row), rows(px[n, :, cols], final_row))
        one = jnp.broadcast_to(ref[c, top : top + 1, :], (8, 128))
        two = jnp.broadcast_to(ref[c, top + 1 : top + 2, :], (8, 128))
        return jnp.where(stay, kept, jnp.where(final_first, one, two))

    low_b, high_b = lane < 16, lane >= 112
    low_c, high_c = lane % 16 == 0, lane % 16 == 15
    left_half, left_c = lane < 64, lane % 16 < 8
    group, inside = lane // 16, lane % 16
    row_b = jnp.where(left_half, slot[2], slot[3])
    here_b = jnp.where(left_half, away[2], away[3]) == 0
    row_c = jnp.where(left_c, slot[4], slot[5])
    here_c = jnp.where(left_c, away[4], away[5]) == 0

    def send_faces(g, v):
        packed = [[v[1, :, 0:128], v[1, :, 128:256]], [v[16, :, 0:128], v[16, :, 128:256]]]
        for _ in range(4):
            packed.append([zero, zero])
        for a in range(16):
            both = jnp.where(left_half, roll(v[a + 1, :, 128:256], 16), roll(v[a + 1, :, 0:128], -16))
            sb[a] = both
            moved = roll(both, 16 * (a % 8))
            packed[3][a // 8] = jnp.where(group == a % 8, moved, packed[3][a // 8])
            packed[2][a // 8] = jnp.where(group == (a + 7) % 8, moved, packed[2][a // 8])
            for h in range(2):
                half = v[a + 1, :, 128 * h : 128 * h + 128]
                both = jnp.where(left_c, roll(half, -15), roll(half, 15))
                sc[a, :, 128 * h : 128 * h + 128] = both
                m, k = (2 * a + h) % 16, (2 * a + h) // 16
                moved = roll(both, m)
                packed[5][k] = jnp.where(inside == m, moved, packed[5][k])
                packed[4][k] = jnp.where(inside == (m + 15) % 16, moved, packed[4][k])
        for d in range(4):
            face, row = give[d]
            for k in range(2):
                out = rows(packed[0][k], row)
                for f in range(1, 6):
                    out = jnp.where(face == f, rows(packed[f][k], row), out)
                gs[g, d, :, 128 * k : 128 * k + 128] = out
        copies = push_around(lambda d: gs.at[g, d], lambda d: gr.at[g, d])
        for copy in copies:
            copy.start()
        return copies

    def take_faces(g, v, ends, copies):
        for copy in copies:
            copy.wait_recv()
        came = [[zero, zero] for _ in range(6)]
        for f in range(6):
            for k in range(2):
                for d in range(4):
                    got = rows(gr[g, d, :, 128 * k : 128 * k + 128], rank[f])
                    came[f][k] = jnp.where(away[f] == d + 1, got, came[f][k])
        for k in range(2):
            cols = slice(128 * k, 128 * k + 128)
            low = jnp.where(away[0] == 0, rows(v[16, :, cols], slot[0]), came[0][k])
            high = jnp.where(away[1] == 0, rows(v[1, :, cols], slot[1]), came[1][k])
            for end in ends:
                end[0, :, cols] = low
                end[17, :, cols] = high
        for a in range(16):
            both = jnp.where(group == a % 8, came[2][a // 8], came[3][a // 8])
            gb[a] = jnp.where(here_b, rows(sb[a], row_b), roll(both, -16 * (a % 8)))
            for h in range(2):
                cols = slice(128 * h, 128 * h + 128)
                m, k = (2 * a + h) % 16, (2 * a + h) // 16
                both = jnp.where(inside == m, came[4][k], came[5][k])
                gc[a, :, cols] = jnp.where(here_c, rows(sc[a, :, cols], row_c), roll(both, -m))

    def stencil(v, a, ghost_b, ghost_c):
        x = [v[a + 1, :, 0:128], v[a + 1, :, 128:256]]
        down, up = [roll(y, 16) for y in x], [roll(y, -16) for y in x]
        beside_b = (
            (jnp.where(low_b, ghost_b, down[0]), jnp.where(high_b, up[1], up[0])),
            (jnp.where(low_b, down[0], down[1]), jnp.where(high_b, ghost_b, up[1])),
        )
        out = []
        for h in range(2):
            cols = slice(128 * h, 128 * h + 128)
            beside = beside_b[h] + (
                jnp.where(low_c, ghost_c[h], roll(x[h], 1)),
                jnp.where(high_c, ghost_c[h], roll(x[h], -1)),
                v[a, :, cols],
                v[a + 2, :, cols],
            )
            mobility = 1.0 + x[h] * x[h]
            squares, flux = 6.0 * mobility, None
            for w in beside:
                square = w * w
                squares = squares + square
                term = (mobility + square) * (x[h] - w)
                flux = term if flux is None else flux + term
            out.append((x[h], flux, squares))
        return out

    def fine_ghosts(a):
        return gb[a], (gc[a, :, 0:128], gc[a, :, 128:256])

    def over(count, step):
        lax.fori_loop(0, count, lambda a, carry: (step(a), carry)[1], 0, unroll=4)

    def jacobi(v, force, coefficient, ghosts, store, count):
        def step(a):
            parts = stencil(v, a, *ghosts(a))
            for h, (x, flux, conduct) in enumerate(parts):
                cols = slice(128 * h, 128 * h + 128)
                q = coefficient[a, :, cols]
                defect = force[a, :, cols] - (REACTION * x + q * flux)
                store(a, h, x + DAMPING * defect / (REACTION + q * conduct))

        over(count, step)

    def into(ref):
        def store(a, h, value):
            ref[a + 1, :, 128 * h : 128 * h + 128] = value

        return store

    def shrink(n, layer):
        fold = jnp.concatenate([layer(2 * a) + layer(2 * a + 1) for a in range(8)], 0)
        out = exact_dot(fold, restrict_m[...])
        for a in range(8):
            zz[n, a] = out[8 * a : 8 * a + 8]
        for m in range(4):
            dense = jnp.where(left_c, out[16 * m : 16 * m + 8], out[16 * m + 8 : 16 * m + 16])
            ps[n, m] = dense
            pd_s[n, m] = rows(dense, outward)[0:2]
        copies = [
            push(ps.at[n], pxr.at[n], xp),
            push(ps.at[n], pyr.at[n], yp),
            push(pd_s.at[n], pd_r.at[n], diag),
        ]
        for copy in copies:
            copy.start()
        return copies

    slots = sub.astype(F32)
    to_x = jnp.sum(jnp.where(pa // 8 == 1, slots, 0.0), axis=0, keepdims=True)
    to_y = jnp.sum(jnp.where(pa // 8 == 2, slots, 0.0), axis=0, keepdims=True)
    outward = jnp.where(sub == 0, jnp.broadcast_to(to_x, (8, 128)), jnp.broadcast_to(to_y, (8, 128)))
    outward = outward.astype(I32)

    y_first.wait_recv()
    for c in range(32):
        va[1 + c // 2, :, 128 * (c % 2) : 128 * (c % 2) + 128] = arrived(0, yi_r, 0, c)
    copies0 = send_faces(0, va)
    y_second.wait_recv()
    for c in range(32):
        cols = slice(128 * (c % 2), 128 * (c % 2) + 128)
        fr[c // 2, :, cols] = arrived(1, yf_r, 0, c)
        qr[c // 2, :, cols] = 0.5 * arrived(2, yf_r, 2, c)
    perm_copies = shrink(2, lambda a: qr[a])
    take_faces(0, va, (va, vb), copies0)

    for source, target in ((va, vb), (vb, va), (va, vb)):
        jacobi(source, fr, qr, fine_ghosts, into(target), 16)

    copies1 = send_faces(1, vb)
    sol_copies = shrink(0, lambda a: vb[a + 1])
    take_faces(1, vb, (vb,), copies1)

    def residual_step(a):
        for h, (x, flux, _) in enumerate(stencil(vb, a, *fine_ghosts(a))):
            cols = slice(128 * h, 128 * h + 128)
            value = fr[a, :, cols] - (REACTION * x + qr[a, :, cols] * flux)
            res_v[:, pl.ds(pl.multiple_of(256 * a + 128 * h, 128), 128)] = value

    over(16, residual_step)
    res_copies = shrink(1, lambda a: res_v[:, 256 * a : 256 * a + 256])
    res_out = pltpu.make_async_copy(res_v, res_h, lsem.at[8])
    res_out.start()

    block, half_a = sub // 2, sub % 2
    side_c = (lane // 8) % 2
    codes = []
    for t in range(2):
        at = half_a * 4 + 2 * t + side_c
        code = jnp.where(block == 1, rows(ch_x, at), jnp.where(block == 2, rows(ch_y, at), rows(ch, at)))
        source = code // 8
        place = jnp.where(
            block == 1,
            jnp.where(source == 0, 1, jnp.where(source == 1, 0, 3)),
            jnp.where(block == 2, jnp.where(source == 0, 2, jnp.where(source == 1, 3, 0)), source),
        )
        codes.append((place, code % 8))

    def unpack(dense, odd):
        if odd:
            return jnp.where(left_c, roll(dense, -8), dense)
        return jnp.where(left_c, dense, roll(dense, 8))

    def assemble(n, copies, store):
        for copy in copies:
            copy.wait_recv()
        for a in range(8):
            from_x = unpack(pxr[n, a // 2], a % 2)
            from_y = unpack(pyr[n, a // 2], a % 2)
            one = jnp.broadcast_to(pd_r[n, a // 2, 0:1, :], (8, 128))
            two = jnp.broadcast_to(pd_r[n, a // 2, 1:2, :], (8, 128))
            from_d = unpack(jnp.where(block == 1, two, one), a % 2)
            for t in range(2):
                place, row = codes[t]
                value = jnp.where(place == 0, rows(zz[n, a], row), from_d)
                value = jnp.where(place == 1, rows(from_x, row), value)
                value = jnp.where(place == 2, rows(from_y, row), value)
                store(a, t, value)

    def store_q(a, t, value):
        eq[a, :, 128 * t : 128 * t + 128] = 0.25 * value

    def store_0(a, t, value):
        cols = slice(128 * t, 128 * t + 128)
        e0[a, :, cols] = value
        ea[a + 1, :, cols] = value

    def store_f(a, t, value):
        cols = slice(128 * t, 128 * t + 128)
        ef[a, :, cols] = ef[a, :, cols] + value

    def close(e):
        for t in range(2):
            cols = slice(128 * t, 128 * t + 128)
            e[0, :, cols] = jnp.where(half_a == 1, rows(e[8, :, cols], sub - half_a + 1 - half_a), 0.0)
            e[9, :, cols] = jnp.where(half_a == 0, rows(e[1, :, cols], sub - half_a + 1 - half_a), 0.0)

    def no_ghosts(a):
        return zero, (zero, zero)

    assemble(2, perm_copies, store_q)
    assemble(0, sol_copies, store_0)
    close(ea)

    def force_step(a):
        for h, (x, flux, _) in enumerate(stencil(ea, a, *no_ghosts(a))):
            cols = slice(128 * h, 128 * h + 128)
            ef[a, :, cols] = REACTION * x + eq[a, :, cols] * flux

    over(8, force_step)
    assemble(1, res_copies, store_f)

    for n, (source, target) in enumerate(((ea, eb), (eb, ea)) * (COARSE // 2)):
        if n:
            close(source)
        jacobi(source, ef, eq, no_ghosts, into(target), 8)

    parent_row = (pa // 8) * 2 + (pa % 8) // 4
    low_ob, low_oc = (pa // 2) % 2 == 0, pa % 2 == 0
    for a in range(8):
        one = rows(ea[a + 1, :, 0:128] - e0[a, :, 0:128], parent_row)
        two = rows(ea[a + 1, :, 128:256] - e0[a, :, 128:256], parent_row)
        value = jnp.where(low_ob, one, two)
        cor[a] = jnp.where(low_oc, value, roll(value, -8))
    spread = exact_dot(jnp.concatenate([cor[a] for a in range(8)], 0), upsample_m[...])
    for a in range(16):
        part = spread[8 * (a // 2) : 8 * (a // 2) + 8]
        va[a + 1] = vb[a + 1] + part

    copies2 = send_faces(2, va)
    take_faces(2, va, (va, vb), copies2)

    def into_result(a, h, value):
        sol_v[:, pl.ds(pl.multiple_of(256 * a + 128 * h, 128), 128)] = value

    jacobi(va, fr, qr, fine_ghosts, into(vb), 16)
    jacobi(vb, fr, qr, fine_ghosts, into(va), 16)
    jacobi(va, fr, qr, fine_ghosts, into_result, 16)
    sol_out = pltpu.make_async_copy(sol_v, sol_h, lsem.at[9])
    sol_out.start()

    for copy in (
        x_copies + msgs + [y_first, y_second] + copies0 + perm_copies + copies1 + sol_copies + res_copies + copies2
    ):
        copy.wait_send()
    res_out.wait()
    sol_out.wait()


def body(*args):
    count = 30
    vmem = lambda *shape: pltpu.VMEM(shape, F32)
    any_space = pl.BlockSpec(memory_space=pl.ANY)
    shape = jax.ShapeDtypeStruct((8, 4096), F32)
    return pl.pallas_call(
        kernel,
        out_shape=(shape, shape),
        in_specs=[any_space] * 8,
        out_specs=(any_space, any_space),
        scratch_shapes=[
            vmem(3, 8, 4096), vmem(3, 8, 4096),
            pltpu.SMEM((8,), I32), pltpu.SMEM((8,), I32), pltpu.SMEM((8,), I32), pltpu.SMEM((8,), I32),
            pltpu.VMEM((8, 6), I32), vmem(16, 128), vmem(4, 16, 128),
            vmem(32, 2, 128), vmem(32, 2, 128), vmem(32, 4, 128), vmem(32, 4, 128),
            vmem(18, 8, 256), vmem(18, 8, 256), vmem(16, 8, 256), vmem(16, 8, 256),
            vmem(16, 8, 128), vmem(16, 8, 256), vmem(16, 8, 128), vmem(16, 8, 256),
            vmem(3, 4, 8, 256), vmem(3, 4, 8, 256),
            vmem(3, 4, 8, 128), vmem(3, 4, 8, 128), vmem(3, 4, 8, 128),
            vmem(3, 4, 2, 128), vmem(3, 4, 2, 128),
            vmem(10, 8, 256), vmem(10, 8, 256), vmem(8, 8, 256), vmem(8, 8, 256), vmem(8, 8, 256),
            vmem(8, 8, 128), vmem(3, 8, 8, 128),
            pltpu.VMEM((256, 128), BF16), pltpu.VMEM((128, 256), BF16),
            vmem(8, 4096), vmem(8, 4096),
            pltpu.SemaphoreType.DMA((10,)), pltpu.SemaphoreType.DMA((count,)), pltpu.SemaphoreType.DMA((count,)),
        ],
        compiler_params=pltpu.CompilerParams(
            collective_id=0, has_side_effects=True, vmem_limit_bytes=32 * 1024 * 1024
        ),
    )(*args)


def solution(mesh):
    whole, flat = P(("gx", "gy"), None), P(("gx", "gy"))
    return jax.shard_map(
        body,
        mesh=mesh,
        in_specs=(whole, whole, whole, flat, flat, whole, flat, flat),
        out_specs=(whole, whole),
        check_vma=False,
    )
```

```python
import functools

import jax
import jax.numpy as jnp
from jax import lax
from jax.experimental import pallas as pl
from jax.experimental.pallas import tpu as pltpu
from jax.sharding import PartitionSpec as P

INNER = 3
COARSE = 4
REACTION = 0.25
DAMPING = 0.8
OPP = (1, 0, 3, 2)

F32 = jnp.float32
I32 = jnp.int32
BF16 = jnp.bfloat16

_ROWS = lax.GatherDimensionNumbers(
    offset_dims=(),
    collapsed_slice_dims=(0,),
    start_index_map=(0,),
    operand_batching_dims=(1,),
    start_indices_batching_dims=(1,),
)


def rows(x, index):
    return lax.gather(
        x, index[..., None], _ROWS, (1, 1), mode=lax.GatherScatterMode.PROMISE_IN_BOUNDS
    )


def roll(x, shift):
    return pltpu.roll(x, shift % 128, 1) if shift % 128 else x


def split3(x):
    high = x.astype(BF16)
    rest = x - high.astype(F32)
    mid = rest.astype(BF16)
    low = (rest - mid.astype(F32)).astype(BF16)
    return high, mid, low


def exact_dot(x, matrix):
    count = x.shape[0]
    out = jnp.dot(jnp.concatenate(split3(x), 0), matrix, preferred_element_type=F32)
    return out[:count] + (out[count : 2 * count] + out[2 * count :])


def pairwise(x):
    return ((x[0] + x[1]) + (x[2] + x[3])) + (x[4] + x[5])


def kernel(
    init_h, src_h, perm_h, mx_h, my_h, nb_h, ch_h, pa_h, sol_v, res_v,
    own, px, t_mx, t_my, t_ch, t_pa, nbv, msg_s, msg_r, yi_s, yi_r, yf_s, yf_r,
    vv, fr, qr, sb, sc, gb, gc, gs, gr, ps, pxr, pyr, pd_s, pd_r,
    ee, e0, ef, eq, cor, zz, restrict_m, upsample_m,
    lsem, ssem, rsem,
):
    va, vb = vv.at[0], vv.at[1]
    ea, eb = ee.at[0], ee.at[1]
    i, j = lax.axis_index("gx"), lax.axis_index("gy")
    nx, ny = lax.axis_size("gx"), lax.axis_size("gy")
    xp = (i + 1 - 2 * (i % 2), j)
    yp = (i, j + 1 - 2 * (j % 2))
    diag = (xp[0], yp[1])
    around = (((i + nx - 1) % nx, j), ((i + 1) % nx, j), (i, (j + ny - 1) % ny), (i, (j + 1) % ny))

    barrier = pltpu.get_barrier_semaphore()
    for peer in around + (diag,):
        pl.semaphore_signal(barrier, inc=1, device_id=peer, device_id_type=pl.DeviceIdType.MESH)

    tables = [
        pltpu.make_async_copy(a, b, lsem.at[n])
        for n, (a, b) in enumerate(
            ((mx_h, t_mx), (my_h, t_my), (ch_h, t_ch), (pa_h, t_pa), (nb_h, nbv))
        )
    ]
    for copy in tables:
        copy.start()
    fields = [
        pltpu.make_async_copy(a, own.at[n], lsem.at[5 + n])
        for n, a in enumerate((init_h, src_h, perm_h))
    ]
    for copy in fields:
        copy.start()

    used = [0]

    def push(source, target, peer):
        n = used[0]
        used[0] += 1
        return pltpu.make_async_remote_copy(
            src_ref=source,
            dst_ref=target,
            send_sem=ssem.at[n],
            recv_sem=rsem.at[n],
            device_id=peer,
            device_id_type=pl.DeviceIdType.MESH,
        )

    def push_around(sources, target):
        base = used[0]
        used[0] += 4
        return [
            pltpu.make_async_remote_copy(
                src_ref=sources(d),
                dst_ref=target(OPP[d]),
                send_sem=ssem.at[base + d],
                recv_sem=rsem.at[base + OPP[d]],
                device_id=around[d],
                device_id_type=pl.DeviceIdType.MESH,
            )
            for d in range(4)
        ]

    lane = lax.broadcasted_iota(I32, (8, 128), 1)
    sub = lax.broadcasted_iota(I32, (8, 128), 0)
    zero = jnp.zeros((8, 128), F32)

    for copy in tables:
        copy.wait()

    def column(ref):
        out = jnp.full((8, 128), ref[0], I32)
        for k in range(1, 8):
            out = jnp.where(sub == k, ref[k], out)
        return out

    mx, my, ch, pa = column(t_mx), column(t_my), column(t_ch), column(t_pa)

    links = [jnp.broadcast_to(nbv[:, f : f + 1], (8, 128)) for f in range(6)]
    away = [jnp.where(c >= 0, c // 8, 7) for c in links]
    slot = [jnp.where(c >= 0, c % 8, 0) for c in links]
    marks = jnp.concatenate([(lane == d).astype(F32) for d in away], 0)
    before = (
        lax.broadcasted_iota(I32, (48, 48), 1) < lax.broadcasted_iota(I32, (48, 48), 0)
    ).astype(F32)
    counts = jnp.dot(before, marks, preferred_element_type=F32)
    rank = []
    wanted = zero
    for f in range(6):
        mine = jnp.where(lane == away[f], counts[8 * f : 8 * f + 8], 0.0)
        place = jnp.broadcast_to(jnp.sum(mine, axis=1, keepdims=True), (8, 128)).astype(I32)
        place = jnp.minimum(place, 7)
        rank.append(place)
        remote = (away[f] >= 1) & (away[f] <= 4)
        hit = (lane == away[f] * 8 + place) & remote
        wanted = wanted + jnp.where(hit, ((f ^ 1) * 8 + slot[f]).astype(F32), 0.0)
    msg_s[0:8, :] = jnp.broadcast_to(jnp.sum(wanted, axis=0, keepdims=True), (8, 128))
    msg_s[8:16, :] = ch.astype(F32)

    named = sub == t_my[0]
    for k in range(1, 8):
        named = named | (sub == t_my[k])
    free = jnp.where(named, 8.0, sub.astype(F32))
    first = jnp.min(free, axis=0, keepdims=True)
    last = jnp.max(jnp.where(named, 0.0, sub.astype(F32)), axis=0, keepdims=True)
    leave = jnp.where(sub % 2 == 0, jnp.broadcast_to(first, (8, 128)), jnp.broadcast_to(last, (8, 128)))
    leave = jnp.minimum(leave, 7.0).astype(I32)
    leave_e = rows(mx, leave)
    leave_own, leave_row = leave_e < 8, leave_e % 8
    stay = my < 8
    final_e = rows(mx, my % 8)
    final_own, final_row = final_e < 8, final_e % 8
    order = jnp.zeros((8, 128), I32)
    for k in range(8):
        entry = t_my[k]
        order = order + jnp.where((entry >= 8) & (my > entry), 1, 0)
    final_first = order == 0

    fine = lax.broadcasted_iota(I32, (256, 128), 0)
    small = lax.broadcasted_iota(I32, (256, 128), 1)
    same = (fine // 32 == small // 16) & ((fine % 16) // 2 == small % 8)
    restrict_m[...] = jnp.where(same, 0.125, 0.0).astype(BF16)
    fine = lax.broadcasted_iota(I32, (128, 256), 1)
    small = lax.broadcasted_iota(I32, (128, 256), 0)
    same = (fine // 32 == small // 16) & ((fine % 16) // 2 == small % 16)
    upsample_m[...] = jnp.where(same, 1.0, 0.0).astype(BF16)

    for copy in fields:
        copy.wait()
    pl.semaphore_wait(barrier, 5)
    x_copies = [push(own.at[n], px.at[n], xp) for n in range(3)]
    x_copies[0].start()
    msgs = push_around(lambda d: msg_s, lambda d: msg_r.at[d])
    for copy in msgs:
        copy.start()
    for copy in x_copies[1:]:
        copy.start()

    def leaving(n, c):
        cols = pl.ds(128 * c, 128)
        return jnp.where(leave_own, rows(own[n, :, cols], leave_row), rows(px[n, :, cols], leave_row))

    x_copies[0].wait_recv()
    for c in range(32):
        yi_s[c] = leaving(0, c)[0:2]
    y_first = push(yi_s, yi_r, yp)
    y_first.start()
    for n in (1, 2):
        x_copies[n].wait_recv()
    for c in range(32):
        yf_s[c] = jnp.where(sub < 2, leaving(1, c), leaving(2, c))[0:4]
    y_second = push(yf_s, yf_r, yp)
    y_second.start()

    for copy in msgs:
        copy.wait_recv()
    give = []
    for d in range(4):
        code = jnp.where(lane == (OPP[d] + 1) * 8 + sub, msg_r[d, 0:8, :], 0.0)
        code = jnp.broadcast_to(jnp.sum(code, axis=1, keepdims=True), (8, 128)).astype(I32)
        give.append((code // 8, code % 8))
    ch_x = msg_r[1 - i % 2, 8:16, :].astype(I32)
    ch_y = msg_r[3 - j % 2, 8:16, :].astype(I32)

    def arrived(n, ref, top, c):
        cols = pl.ds(128 * c, 128)
        kept = jnp.where(final_own, rows(own[n, :, cols], final_row), rows(px[n, :, cols], final_row))
        one = jnp.broadcast_to(ref[c, top : top + 1, :], (8, 128))
        two = jnp.broadcast_to(ref[c, top + 1 : top + 2, :], (8, 128))
        return jnp.where(stay, kept, jnp.where(final_first, one, two))

    low_b, high_b = lane < 16, lane >= 112
    low_c, high_c = lane % 16 == 0, lane % 16 == 15
    left_half, left_c = lane < 64, lane % 16 < 8
    group, inside = lane // 16, lane % 16
    row_b = jnp.where(left_half, slot[2], slot[3])
    here_b = jnp.where(left_half, away[2], away[3]) == 0
    row_c = jnp.where(left_c, slot[4], slot[5])
    here_c = jnp.where(left_c, away[4], away[5]) == 0

    def send_faces(g, v):
        packed = [[v[1, :, 0:128], v[1, :, 128:256]], [v[16, :, 0:128], v[16, :, 128:256]]]
        for _ in range(4):
            packed.append([zero, zero])
        for a in range(16):
            both = jnp.where(left_half, roll(v[a + 1, :, 128:256], 16), roll(v[a + 1, :, 0:128], -16))
            sb[a] = both
            moved = roll(both, 16 * (a % 8))
            packed[3][a // 8] = jnp.where(group == a % 8, moved, packed[3][a // 8])
            packed[2][a // 8] = jnp.where(group == (a + 7) % 8, moved, packed[2][a // 8])
            for h in range(2):
                half = v[a + 1, :, 128 * h : 128 * h + 128]
                both = jnp.where(left_c, roll(half, -15), roll(half, 15))
                sc[a, :, 128 * h : 128 * h + 128] = both
                m, k = (2 * a + h) % 16, (2 * a + h) // 16
                moved = roll(both, m)
                packed[5][k] = jnp.where(inside == m, moved, packed[5][k])
                packed[4][k] = jnp.where(inside == (m + 15) % 16, moved, packed[4][k])
        for d in range(4):
            face, row = give[d]
            for k in range(2):
                out = rows(packed[0][k], row)
                for f in range(1, 6):
                    out = jnp.where(face == f, rows(packed[f][k], row), out)
                gs[g, d, :, 128 * k : 128 * k + 128] = out
        copies = push_around(lambda d: gs.at[g, d], lambda d: gr.at[g, d])
        for copy in copies:
            copy.start()
        return copies

    def own_faces(v, ends):
        for k in range(2):
            cols = slice(128 * k, 128 * k + 128)
            low = jnp.where(away[0] == 0, rows(v[16, :, cols], slot[0]), 0.0)
            high = jnp.where(away[1] == 0, rows(v[1, :, cols], slot[1]), 0.0)
            for end in ends:
                end[0, :, cols] = low
                end[17, :, cols] = high
        for a in range(16):
            gb[a] = rows(sb[a], row_b)
            for h in range(2):
                cols = slice(128 * h, 128 * h + 128)
                gc[a, :, cols] = rows(sc[a, :, cols], row_c)

    def take_faces(g, ends, copies):
        for copy in copies:
            copy.wait_recv()
        came = [[zero, zero] for _ in range(6)]
        for f in range(6):
            for k in range(2):
                for d in range(4):
                    got = rows(gr[g, d, :, 128 * k : 128 * k + 128], rank[f])
                    came[f][k] = jnp.where(away[f] == d + 1, got, came[f][k])
        for k in range(2):
            cols = slice(128 * k, 128 * k + 128)
            low = jnp.where(away[0] == 0, ends[0][0, :, cols], came[0][k])
            high = jnp.where(away[1] == 0, ends[0][17, :, cols], came[1][k])
            for end in ends:
                end[0, :, cols] = low
                end[17, :, cols] = high
        for a in range(16):
            both = jnp.where(group == a % 8, came[2][a // 8], came[3][a // 8])
            gb[a] = jnp.where(here_b, gb[a], roll(both, -16 * (a % 8)))
            for h in range(2):
                cols = slice(128 * h, 128 * h + 128)
                m, k = (2 * a + h) % 16, (2 * a + h) // 16
                both = jnp.where(inside == m, came[4][k], came[5][k])
                gc[a, :, cols] = jnp.where(here_c, gc[a, :, cols], roll(both, -m))

    def stencil(v, a, ghost_b, ghost_c):
        x = [v[a + 1, :, 0:128], v[a + 1, :, 128:256]]
        down, up = [roll(y, 16) for y in x], [roll(y, -16) for y in x]
        beside_b = (
            (jnp.where(low_b, ghost_b, down[0]), jnp.where(high_b, up[1], up[0])),
            (jnp.where(low_b, down[0], down[1]), jnp.where(high_b, ghost_b, up[1])),
        )
        out = []
        for h in range(2):
            cols = slice(128 * h, 128 * h + 128)
            beside = beside_b[h] + (
                jnp.where(low_c, ghost_c[h], roll(x[h], 1)),
                jnp.where(high_c, ghost_c[h], roll(x[h], -1)),
                v[a, :, cols],
                v[a + 2, :, cols],
            )
            mobility = 1.0 + x[h] * x[h]
            square = [w * w for w in beside]
            term = [(mobility + y) * (x[h] - w) for y, w in zip(square, beside)]
            squares = 6.0 * mobility + pairwise(square)
            flux = pairwise(term)
            out.append((x[h], flux, squares))
        return out

    def fine_ghosts(a):
        return gb[a], (gc[a, :, 0:128], gc[a, :, 128:256])

    def jacobi(v, force, coefficient, ghosts, store, count):
        for a in range(count):
            parts = stencil(v, a, *ghosts(a))
            for h, (x, flux, conduct) in enumerate(parts):
                cols = slice(128 * h, 128 * h + 128)
                q = coefficient[a, :, cols]
                defect = force[a, :, cols] - (REACTION * x + q * flux)
                store(a, h, x + defect * (DAMPING / (REACTION + q * conduct)))

    def into(ref):
        def store(a, h, value):
            ref[a + 1, :, 128 * h : 128 * h + 128] = value

        return store

    def smooth(sweeps):
        def sweep(n, carry):
            jacobi(vv.at[n % 2], fr, qr, fine_ghosts, into(vv.at[(n + 1) % 2]), 16)
            return carry

        lax.fori_loop(0, sweeps, sweep, 0)

    def shrink(n, layer):
        fold = jnp.concatenate([layer(2 * a) + layer(2 * a + 1) for a in range(8)], 0)
        out = exact_dot(fold, restrict_m[...])
        for a in range(8):
            zz[n, a] = out[8 * a : 8 * a + 8]
        for m in range(4):
            dense = jnp.where(left_c, out[16 * m : 16 * m + 8], out[16 * m + 8 : 16 * m + 16])
            ps[n, m] = dense
            pd_s[n, m] = rows(dense, outward)[0:2]
        copies = [
            push(ps.at[n], pxr.at[n], xp),
            push(ps.at[n], pyr.at[n], yp),
            push(pd_s.at[n], pd_r.at[n], diag),
        ]
        for copy in copies:
            copy.start()
        return copies

    slots = sub.astype(F32)
    to_x = jnp.sum(jnp.where(pa // 8 == 1, slots, 0.0), axis=0, keepdims=True)
    to_y = jnp.sum(jnp.where(pa // 8 == 2, slots, 0.0), axis=0, keepdims=True)
    outward = jnp.where(sub == 0, jnp.broadcast_to(to_x, (8, 128)), jnp.broadcast_to(to_y, (8, 128)))
    outward = outward.astype(I32)

    y_first.wait_recv()
    for c in range(32):
        va[1 + c // 2, :, 128 * (c % 2) : 128 * (c % 2) + 128] = arrived(0, yi_r, 0, c)
    copies0 = send_faces(0, va)
    own_faces(va, (va, vb))
    y_second.wait_recv()
    for c in range(32):
        cols = slice(128 * (c % 2), 128 * (c % 2) + 128)
        fr[c // 2, :, cols] = arrived(1, yf_r, 0, c)
        qr[c // 2, :, cols] = 0.5 * arrived(2, yf_r, 2, c)
    perm_copies = shrink(2, lambda a: qr[a])
    take_faces(0, (va, vb), copies0)
    smooth(INNER)

    copies1 = send_faces(1, vb)
    own_faces(vb, (vb,))
    sol_copies = shrink(0, lambda a: vb[a + 1])
    take_faces(1, (vb,), copies1)

    layers = []
    for a in range(16):
        layers.append([])
        for h, (x, flux, _) in enumerate(stencil(vb, a, *fine_ghosts(a))):
            cols = slice(128 * h, 128 * h + 128)
            value = fr[a, :, cols] - (REACTION * x + qr[a, :, cols] * flux)
            res_v[:, 256 * a + 128 * h : 256 * a + 128 * h + 128] = value
            layers[a].append(value)
    res_copies = shrink(1, lambda a: jnp.concatenate(layers[a], 1))

    block, half_a = sub // 2, sub % 2
    side_c = (lane // 8) % 2
    codes = []
    for t in range(2):
        at = half_a * 4 + 2 * t + side_c
        code = jnp.where(block == 1, rows(ch_x, at), jnp.where(block == 2, rows(ch_y, at), rows(ch, at)))
        source = code // 8
        place = jnp.where(
            block == 1,
            jnp.where(source == 0, 1, jnp.where(source == 1, 0, 3)),
            jnp.where(block == 2, jnp.where(source == 0, 2, jnp.where(source == 1, 3, 0)), source),
        )
        codes.append((place, code % 8))

    def unpack(dense, odd):
        if odd:
            return jnp.where(left_c, roll(dense, -8), dense)
        return jnp.where(left_c, dense, roll(dense, 8))

    def assemble(n, copies, store):
        for copy in copies:
            copy.wait_recv()
        for a in range(8):
            from_x = unpack(pxr[n, a // 2], a % 2)
            from_y = unpack(pyr[n, a // 2], a % 2)
            one = jnp.broadcast_to(pd_r[n, a // 2, 0:1, :], (8, 128))
            two = jnp.broadcast_to(pd_r[n, a // 2, 1:2, :], (8, 128))
            from_d = unpack(jnp.where(block == 1, two, one), a % 2)
            for t in range(2):
                place, row = codes[t]
                value = jnp.where(place == 0, rows(zz[n, a], row), from_d)
                value = jnp.where(place == 1, rows(from_x, row), value)
                value = jnp.where(place == 2, rows(from_y, row), value)
                store(a, t, value)

    def store_q(a, t, value):
        eq[a, :, 128 * t : 128 * t + 128] = 0.25 * value

    def store_0(a, t, value):
        cols = slice(128 * t, 128 * t + 128)
        e0[a, :, cols] = value
        ea[a + 1, :, cols] = value

    def store_f(a, t, value):
        cols = slice(128 * t, 128 * t + 128)
        ef[a, :, cols] = ef[a, :, cols] + value

    def close(e):
        for t in range(2):
            cols = slice(128 * t, 128 * t + 128)
            e[0, :, cols] = jnp.where(half_a == 1, rows(e[8, :, cols], sub - half_a + 1 - half_a), 0.0)
            e[9, :, cols] = jnp.where(half_a == 0, rows(e[1, :, cols], sub - half_a + 1 - half_a), 0.0)

    def no_ghosts(a):
        return zero, (zero, zero)

    assemble(2, perm_copies, store_q)
    assemble(0, sol_copies, store_0)
    close(ea)

    for a in range(8):
        for h, (x, flux, _) in enumerate(stencil(ea, a, *no_ghosts(a))):
            cols = slice(128 * h, 128 * h + 128)
            ef[a, :, cols] = REACTION * x + eq[a, :, cols] * flux
    assemble(1, res_copies, store_f)

    def coarse_sweep(n, carry):
        source, target = ee.at[n % 2], ee.at[(n + 1) % 2]
        jacobi(source, ef, eq, no_ghosts, into(target), 8)
        close(target)
        return carry

    lax.fori_loop(0, COARSE, coarse_sweep, 0)

    parent_row = (pa // 8) * 2 + (pa % 8) // 4
    low_ob, low_oc = (pa // 2) % 2 == 0, pa % 2 == 0
    for a in range(8):
        one = rows(ea[a + 1, :, 0:128] - e0[a, :, 0:128], parent_row)
        two = rows(ea[a + 1, :, 128:256] - e0[a, :, 128:256], parent_row)
        value = jnp.where(low_ob, one, two)
        cor[a] = jnp.where(low_oc, value, roll(value, -8))
    spread = exact_dot(jnp.concatenate([cor[a] for a in range(8)], 0), upsample_m[...])
    for a in range(16):
        part = spread[8 * (a // 2) : 8 * (a // 2) + 8]
        va[a + 1] = vb[a + 1] + part

    copies2 = send_faces(2, va)
    own_faces(va, (va, vb))
    take_faces(2, (va, vb), copies2)

    def into_result(a, h, value):
        sol_v[:, 256 * a + 128 * h : 256 * a + 128 * h + 128] = value

    smooth(INNER - 1)
    jacobi(va, fr, qr, fine_ghosts, into_result, 16)

    for copy in (
        x_copies + msgs + [y_first, y_second] + copies0 + perm_copies + copies1 + sol_copies + res_copies + copies2
    ):
        copy.wait_send()


def body(*args):
    count = 30
    vmem = lambda *shape: pltpu.VMEM(shape, F32)
    any_space = pl.BlockSpec(memory_space=pl.ANY)
    return pl.pallas_call(
        kernel,
        out_shape=(pltpu.VMEM((8, 4096), F32), pltpu.VMEM((8, 4096), F32)),
        in_specs=[any_space] * 8,
        out_specs=(pl.BlockSpec(memory_space=pltpu.VMEM),) * 2,
        scratch_shapes=[
            vmem(3, 8, 4096), vmem(3, 8, 4096),
            pltpu.SMEM((8,), I32), pltpu.SMEM((8,), I32), pltpu.SMEM((8,), I32), pltpu.SMEM((8,), I32),
            pltpu.VMEM((8, 6), I32), vmem(16, 128), vmem(4, 16, 128),
            vmem(32, 2, 128), vmem(32, 2, 128), vmem(32, 4, 128), vmem(32, 4, 128),
            vmem(2, 18, 8, 256), vmem(16, 8, 256), vmem(16, 8, 256),
            vmem(16, 8, 128), vmem(16, 8, 256), vmem(16, 8, 128), vmem(16, 8, 256),
            vmem(3, 4, 8, 256), vmem(3, 4, 8, 256),
            vmem(3, 4, 8, 128), vmem(3, 4, 8, 128), vmem(3, 4, 8, 128),
            vmem(3, 4, 2, 128), vmem(3, 4, 2, 128),
            vmem(2, 10, 8, 256), vmem(8, 8, 256), vmem(8, 8, 256), vmem(8, 8, 256),
            vmem(8, 8, 128), vmem(3, 8, 8, 128),
            pltpu.VMEM((256, 128), BF16), pltpu.VMEM((128, 256), BF16),
            pltpu.SemaphoreType.DMA((10,)), pltpu.SemaphoreType.DMA((count,)), pltpu.SemaphoreType.DMA((count,)),
        ],
        compiler_params=pltpu.CompilerParams(
            collective_id=0, has_side_effects=True, vmem_limit_bytes=32 * 1024 * 1024
        ),
    )(*[pltpu.with_memory_space_constraint(a, pltpu.HBM) for a in args])


def solution(mesh):
    whole, flat = P(("gx", "gy"), None), P(("gx", "gy"))
    return jax.shard_map(
        body,
        mesh=mesh,
        in_specs=(whole, whole, whole, flat, flat, whole, flat, flat),
        out_specs=(whole, whole),
        check_vma=False,
    )
```

```python
import functools

import jax
import jax.numpy as jnp
from jax import lax
from jax.experimental import pallas as pl
from jax.experimental.pallas import tpu as pltpu
from jax.sharding import PartitionSpec as P

INNER = 3
COARSE = 4
REACTION = 0.25
DAMPING = 0.8
OPP = (1, 0, 3, 2)

F32 = jnp.float32
I32 = jnp.int32
BF16 = jnp.bfloat16

_ROWS = lax.GatherDimensionNumbers(
    offset_dims=(),
    collapsed_slice_dims=(0,),
    start_index_map=(0,),
    operand_batching_dims=(1,),
    start_indices_batching_dims=(1,),
)


def rows(x, index):
    return lax.gather(
        x, index[..., None], _ROWS, (1, 1), mode=lax.GatherScatterMode.PROMISE_IN_BOUNDS
    )


def roll(x, shift):
    return pltpu.roll(x, shift % 128, 1) if shift % 128 else x


def split3(x):
    high = x.astype(BF16)
    rest = x - high.astype(F32)
    mid = rest.astype(BF16)
    low = (rest - mid.astype(F32)).astype(BF16)
    return high, mid, low


def exact_dot(x, matrix):
    count = x.shape[0]
    out = jnp.dot(jnp.concatenate(split3(x), 0), matrix, preferred_element_type=F32)
    return out[:count] + (out[count : 2 * count] + out[2 * count :])


def pairwise(x):
    return ((x[0] + x[1]) + (x[2] + x[3])) + (x[4] + x[5])


def kernel(
    init_h, src_h, perm_h, mx_h, my_h, nb_h, ch_h, pa_h, both_v,
    own, px, t_mx, t_my, t_ch, t_pa, nbv, msg_s, msg_r, yi_s, yi_r, yf_s, yf_r,
    vv, fr, qr, sb, sc, gb, gc, every_s, every_r, gs, gr, ps, pxr, pyr, pd_s, pd_r,
    e0, ef, eq, cor, zz, restrict_m, upsample_m,
    ready, lsem, ssem, rsem,
):
    va, vb = vv.at[0], vv.at[1]
    i, j = lax.axis_index("gx"), lax.axis_index("gy")
    nx, ny = lax.axis_size("gx"), lax.axis_size("gy")
    xp = (i + 1 - 2 * (i % 2), j)
    yp = (i, j + 1 - 2 * (j % 2))
    diag = (xp[0], yp[1])
    beyond_x = ((i + nx - 1 + 2 * (i % 2)) % nx, j)
    beyond_y = (i, (j + ny - 1 + 2 * (j % 2)) % ny)
    around = (((i + nx - 1) % nx, j), ((i + 1) % nx, j), (i, (j + ny - 1) % ny), (i, (j + 1) % ny))

    tables = [
        pltpu.make_async_copy(a, b, lsem.at[n])
        for n, (a, b) in enumerate(
            ((mx_h, t_mx), (my_h, t_my), (ch_h, t_ch), (pa_h, t_pa), (nb_h, nbv))
        )
    ]
    for copy in tables:
        copy.start()
    fields = [
        pltpu.make_async_copy(a, own.at[n], lsem.at[5 + n])
        for n, a in enumerate((init_h, src_h, perm_h))
    ]
    for copy in fields:
        copy.start()

    even = (i + j) % 2 == 0
    odd = (i + j) % 2 == 1
    barrier = pltpu.get_barrier_semaphore()

    def signal(semaphore, peer):
        pl.semaphore_signal(semaphore, inc=1, device_id=peer, device_id_type=pl.DeviceIdType.MESH)

    @pl.when(even)
    def _():
        signal(barrier, beyond_x)
        signal(barrier, beyond_y)
        pl.semaphore_wait(barrier, 2)
        signal(ready.at[0], xp)
        signal(ready.at[1], yp)

    @pl.when(odd)
    def _():
        signal(barrier, xp)
        signal(barrier, yp)
        pl.semaphore_wait(ready.at[0], 1)

    used = [0]

    def push(source, target, peer):
        n = used[0]
        used[0] += 1
        return pltpu.make_async_remote_copy(
            src_ref=source,
            dst_ref=target,
            send_sem=ssem.at[n],
            recv_sem=rsem.at[n],
            device_id=peer,
            device_id_type=pl.DeviceIdType.MESH,
        )

    def push_around(sources, target):
        base = used[0]
        used[0] += 4
        return [
            pltpu.make_async_remote_copy(
                src_ref=sources(d),
                dst_ref=target(OPP[d]),
                send_sem=ssem.at[base + d],
                recv_sem=rsem.at[base + OPP[d]],
                device_id=around[d],
                device_id_type=pl.DeviceIdType.MESH,
            )
            for d in range(4)
        ]

    x_copies = [push(a, px.at[n], xp) for n, a in enumerate((init_h, src_h, perm_h))]
    for copy in x_copies:
        copy.start()

    lane = lax.broadcasted_iota(I32, (8, 128), 1)
    sub = lax.broadcasted_iota(I32, (8, 128), 0)
    zero = jnp.zeros((8, 128), F32)

    for copy in tables:
        copy.wait()

    def column(ref):
        out = jnp.full((8, 128), ref[0], I32)
        for k in range(1, 8):
            out = jnp.where(sub == k, ref[k], out)
        return out

    mx, my, ch, pa = column(t_mx), column(t_my), column(t_ch), column(t_pa)

    links = [jnp.broadcast_to(nbv[:, f : f + 1], (8, 128)) for f in range(6)]
    away = [jnp.where(c >= 0, c // 8, 7) for c in links]
    slot = [jnp.where(c >= 0, c % 8, 0) for c in links]
    named = sub == t_my[0]
    for k in range(1, 8):
        named = named | (sub == t_my[k])
    free = jnp.where(named, 8.0, sub.astype(F32))
    first = jnp.min(free, axis=0, keepdims=True)
    last = jnp.max(jnp.where(named, 0.0, sub.astype(F32)), axis=0, keepdims=True)
    leave = jnp.where(sub % 2 == 0, jnp.broadcast_to(first, (8, 128)), jnp.broadcast_to(last, (8, 128)))
    leave = jnp.minimum(leave, 7.0).astype(I32)
    leave_e = rows(mx, leave)
    leave_own, leave_row = leave_e < 8, leave_e % 8
    stay = my < 8
    final_e = rows(mx, my % 8)
    final_own, final_row = final_e < 8, final_e % 8
    order = jnp.zeros((8, 128), I32)
    for k in range(8):
        entry = t_my[k]
        order = order + jnp.where((entry >= 8) & (my > entry), 1, 0)
    final_first = order == 0

    def leaving(n, c):
        cols = pl.ds(128 * c, 128)
        return jnp.where(leave_own, rows(own[n, :, cols], leave_row), rows(px[n, :, cols], leave_row))

    fields[0].wait()
    x_copies[0].wait_recv()
    for c in range(32):
        yi_s[c] = leaving(0, c)[0:2]
    y_first = push(yi_s, yi_r, yp)

    @pl.when(odd)
    def _():
        pl.semaphore_wait(ready.at[1], 1)

    y_first.start()

    @pl.when(odd)
    def _():
        pl.semaphore_wait(barrier, 2)
        signal(ready.at[2], beyond_x)
        signal(ready.at[3], beyond_y)

    for n in (1, 2):
        fields[n].wait()
        x_copies[n].wait_recv()
    for c in range(32):
        yf_s[c] = jnp.where(sub < 2, leaving(1, c), leaving(2, c))[0:4]
    y_second = push(yf_s, yf_r, yp)
    y_second.start()

    def arrived(n, ref, top, c):
        cols = pl.ds(128 * c, 128)
        kept = jnp.where(final_own, rows(own[n, :, cols], final_row), rows(px[n, :, cols], final_row))
        one = jnp.broadcast_to(ref[c, top : top + 1, :], (8, 128))
        two = jnp.broadcast_to(ref[c, top + 1 : top + 2, :], (8, 128))
        return jnp.where(stay, kept, jnp.where(final_first, one, two))

    low_b, high_b = lane < 16, lane >= 112
    low_c, high_c = lane % 16 == 0, lane % 16 == 15
    left_half, left_c = lane < 64, lane % 16 < 8
    group, inside = lane // 16, lane % 16
    row_b = jnp.where(left_half, slot[2], slot[3])
    here_b = jnp.where(left_half, away[2], away[3]) == 0
    row_c = jnp.where(left_c, slot[4], slot[5])
    here_c = jnp.where(left_c, away[4], away[5]) == 0

    def pack_faces(v):
        packed = [[v[1, :, 0:128], v[1, :, 128:256]], [v[16, :, 0:128], v[16, :, 128:256]]]
        for _ in range(4):
            packed.append([zero, zero])
        for a in range(16):
            both = jnp.where(left_half, roll(v[a + 1, :, 128:256], 16), roll(v[a + 1, :, 0:128], -16))
            sb[a] = both
            moved = roll(both, 16 * (a % 8))
            packed[3][a // 8] = jnp.where(group == a % 8, moved, packed[3][a // 8])
            packed[2][a // 8] = jnp.where(group == (a + 7) % 8, moved, packed[2][a // 8])
            for h in range(2):
                half = v[a + 1, :, 128 * h : 128 * h + 128]
                both = jnp.where(left_c, roll(half, -15), roll(half, 15))
                sc[a, :, 128 * h : 128 * h + 128] = both
                m, k = (2 * a + h) % 16, (2 * a + h) // 16
                moved = roll(both, m)
                packed[5][k] = jnp.where(inside == m, moved, packed[5][k])
                packed[4][k] = jnp.where(inside == (m + 15) % 16, moved, packed[4][k])
        return packed

    def send_faces(g, v):
        packed = pack_faces(v)
        for d in range(4):
            face, row = give[d]
            for k in range(2):
                out = rows(packed[0][k], row)
                for f in range(1, 6):
                    out = jnp.where(face == f, rows(packed[f][k], row), out)
                gs[g - 1, d, :, 128 * k : 128 * k + 128] = out
        copies = push_around(lambda d: gs.at[g - 1, d], lambda d: gr.at[g - 1, d])
        for copy in copies:
            copy.start()
        return copies

    def own_faces(v, ends):
        for k in range(2):
            cols = slice(128 * k, 128 * k + 128)
            low = jnp.where(away[0] == 0, rows(v[16, :, cols], slot[0]), 0.0)
            high = jnp.where(away[1] == 0, rows(v[1, :, cols], slot[1]), 0.0)
            for end in ends:
                end[0, :, cols] = low
                end[17, :, cols] = high
        for a in range(16):
            gb[a] = rows(sb[a], row_b)
            for h in range(2):
                cols = slice(128 * h, 128 * h + 128)
                gc[a, :, cols] = rows(sc[a, :, cols], row_c)

    def take_faces(got, ends, copies):
        for copy in copies:
            copy.wait_recv()
        came = [[zero, zero] for _ in range(6)]
        for f in range(6):
            for k in range(2):
                for d in range(4):
                    came[f][k] = jnp.where(away[f] == d + 1, got(d, f, slice(128 * k, 128 * k + 128)), came[f][k])
        for k in range(2):
            cols = slice(128 * k, 128 * k + 128)
            low = jnp.where(away[0] == 0, ends[0][0, :, cols], came[0][k])
            high = jnp.where(away[1] == 0, ends[0][17, :, cols], came[1][k])
            for end in ends:
                end[0, :, cols] = low
                end[17, :, cols] = high
        for a in range(16):
            both = jnp.where(group == a % 8, came[2][a // 8], came[3][a // 8])
            gb[a] = jnp.where(here_b, gb[a], roll(both, -16 * (a % 8)))
            for h in range(2):
                cols = slice(128 * h, 128 * h + 128)
                m, k = (2 * a + h) % 16, (2 * a + h) // 16
                both = jnp.where(inside == m, came[4][k], came[5][k])
                gc[a, :, cols] = jnp.where(here_c, gc[a, :, cols], roll(both, -m))

    def halves(v, a):
        return [v[a, :, 0:128], v[a, :, 128:256]]

    def parts(before, x, after, ghost_b, ghost_c):
        down, up = [roll(y, 16) for y in x], [roll(y, -16) for y in x]
        beside_b = (
            (jnp.where(low_b, ghost_b, down[0]), jnp.where(high_b, up[1], up[0])),
            (jnp.where(low_b, down[0], down[1]), jnp.where(high_b, ghost_b, up[1])),
        )
        out = []
        for h in range(2):
            beside = beside_b[h] + (
                jnp.where(low_c, ghost_c[h], roll(x[h], 1)),
                jnp.where(high_c, ghost_c[h], roll(x[h], -1)),
                before[h],
                after[h],
            )
            mobility = 1.0 + x[h] * x[h]
            square = [w * w for w in beside]
            term = [(mobility + y) * (x[h] - w) for y, w in zip(square, beside)]
            squares = 6.0 * mobility + pairwise(square)
            flux = pairwise(term)
            out.append((x[h], flux, squares))
        return out

    def stencil(v, a, ghost_b, ghost_c):
        return parts(halves(v, a), halves(v, a + 1), halves(v, a + 2), ghost_b, ghost_c)

    def fine_ghosts(a):
        return gb[a], (gc[a, :, 0:128], gc[a, :, 128:256])

    def jacobi(v, force, coefficient, ghosts, store, count):
        for a in range(count):
            for h, (x, flux, conduct) in enumerate(stencil(v, a, *ghosts(a))):
                cols = slice(128 * h, 128 * h + 128)
                q = coefficient[a, :, cols]
                defect = force[a, :, cols] - (REACTION * x + q * flux)
                store(a, h, x + defect * (DAMPING / (REACTION + q * conduct)))

    def into(ref):
        def store(a, h, value):
            ref[a + 1, :, 128 * h : 128 * h + 128] = value

        return store

    def smooth(sweeps):
        for n in range(sweeps):
            jacobi(vv.at[n % 2], fr, qr, fine_ghosts, into(vv.at[(n + 1) % 2]), 16)

    def shrink(n, layer):
        fold = jnp.concatenate([layer(2 * a) + layer(2 * a + 1) for a in range(8)], 0)
        out = exact_dot(fold, restrict_m[...])
        for a in range(8):
            zz[n, a] = out[8 * a : 8 * a + 8]
        for m in range(4):
            dense = jnp.where(left_c, out[16 * m : 16 * m + 8], out[16 * m + 8 : 16 * m + 16])
            ps[n, m] = dense
            pd_s[n, m] = rows(dense, outward)[0:2]
        copies = [
            push(ps.at[n], pxr.at[n], xp),
            push(ps.at[n], pyr.at[n], yp),
            push(pd_s.at[n], pd_r.at[n], diag),
        ]
        for copy in copies:
            copy.start()
        return copies

    slots = sub.astype(F32)
    to_x = jnp.sum(jnp.where(pa // 8 == 1, slots, 0.0), axis=0, keepdims=True)
    to_y = jnp.sum(jnp.where(pa // 8 == 2, slots, 0.0), axis=0, keepdims=True)
    outward = jnp.where(sub == 0, jnp.broadcast_to(to_x, (8, 128)), jnp.broadcast_to(to_y, (8, 128)))
    outward = outward.astype(I32)

    y_first.wait_recv()
    for c in range(32):
        va[1 + c // 2, :, 128 * (c % 2) : 128 * (c % 2) + 128] = arrived(0, yi_r, 0, c)
    packed = pack_faces(va)
    for f in range(6):
        for k in range(2):
            every_s[f, :, 128 * k : 128 * k + 128] = packed[f][k]

    @pl.when(even)
    def _():
        pl.semaphore_wait(ready.at[2], 1)
        pl.semaphore_wait(ready.at[3], 1)

    copies0 = push_around(lambda d: every_s, lambda d: every_r.at[d])
    for copy in copies0:
        copy.start()
    own_faces(va, (va, vb))

    marks = jnp.concatenate([(lane == d).astype(F32) for d in away], 0)
    before = (
        lax.broadcasted_iota(I32, (48, 48), 1) < lax.broadcasted_iota(I32, (48, 48), 0)
    ).astype(F32)
    counts = jnp.dot(before, marks, preferred_element_type=F32)
    rank = []
    wanted = zero
    for f in range(6):
        mine = jnp.where(lane == away[f], counts[8 * f : 8 * f + 8], 0.0)
        place = jnp.broadcast_to(jnp.sum(mine, axis=1, keepdims=True), (8, 128)).astype(I32)
        place = jnp.minimum(place, 7)
        rank.append(place)
        remote = (away[f] >= 1) & (away[f] <= 4)
        hit = (lane == away[f] * 8 + place) & remote
        wanted = wanted + jnp.where(hit, ((f ^ 1) * 8 + slot[f]).astype(F32), 0.0)
    msg_s[0:8, :] = jnp.broadcast_to(jnp.sum(wanted, axis=0, keepdims=True), (8, 128))
    msg_s[8:16, :] = ch.astype(F32)

    msgs = push_around(lambda d: msg_s, lambda d: msg_r.at[d])
    for copy in msgs:
        copy.start()

    fine = lax.broadcasted_iota(I32, (256, 128), 0)
    small = lax.broadcasted_iota(I32, (256, 128), 1)
    same = (fine // 32 == small // 16) & ((fine % 16) // 2 == small % 8)
    restrict_m[...] = jnp.where(same, 0.125, 0.0).astype(BF16)
    fine = lax.broadcasted_iota(I32, (128, 256), 1)
    small = lax.broadcasted_iota(I32, (128, 256), 0)
    same = (fine // 32 == small // 16) & ((fine % 16) // 2 == small % 16)
    upsample_m[...] = jnp.where(same, 1.0, 0.0).astype(BF16)

    y_second.wait_recv()
    for c in range(32):
        cols = slice(128 * (c % 2), 128 * (c % 2) + 128)
        fr[c // 2, :, cols] = arrived(1, yf_r, 0, c)
        qr[c // 2, :, cols] = 0.5 * arrived(2, yf_r, 2, c)
    perm_copies = shrink(2, lambda a: qr[a])
    take_faces(lambda d, f, cols: rows(every_r[d, f ^ 1, :, cols], slot[f]), (va, vb), copies0)
    smooth(INNER)

    for copy in msgs:
        copy.wait_recv()
    give = []
    for d in range(4):
        code = jnp.where(lane == (OPP[d] + 1) * 8 + sub, msg_r[d, 0:8, :], 0.0)
        code = jnp.broadcast_to(jnp.sum(code, axis=1, keepdims=True), (8, 128)).astype(I32)
        give.append((code // 8, code % 8))
    ch_x = msg_r[1 - i % 2, 8:16, :].astype(I32)
    ch_y = msg_r[3 - j % 2, 8:16, :].astype(I32)

    def asked(g):
        return lambda d, f, cols: rows(gr[g - 1, d, :, cols], rank[f])

    copies1 = send_faces(1, vb)
    own_faces(vb, (vb,))
    sol_copies = shrink(0, lambda a: vb[a + 1])
    take_faces(asked(1), (vb,), copies1)

    layers = []
    for a in range(16):
        layers.append([])
        for h, (x, flux, _) in enumerate(stencil(vb, a, *fine_ghosts(a))):
            cols = slice(128 * h, 128 * h + 128)
            value = fr[a, :, cols] - (REACTION * x + qr[a, :, cols] * flux)
            both_v[8:16, 256 * a + 128 * h : 256 * a + 128 * h + 128] = value
            layers[a].append(value)
    res_copies = shrink(1, lambda a: jnp.concatenate(layers[a], 1))

    block, half_a = sub // 2, sub % 2
    side_c = (lane // 8) % 2
    codes = []
    for t in range(2):
        at = half_a * 4 + 2 * t + side_c
        code = jnp.where(block == 1, rows(ch_x, at), jnp.where(block == 2, rows(ch_y, at), rows(ch, at)))
        source = code // 8
        place = jnp.where(
            block == 1,
            jnp.where(source == 0, 1, jnp.where(source == 1, 0, 3)),
            jnp.where(block == 2, jnp.where(source == 0, 2, jnp.where(source == 1, 3, 0)), source),
        )
        codes.append((place, code % 8))

    def unpack(dense, odd):
        if odd:
            return jnp.where(left_c, roll(dense, -8), dense)
        return jnp.where(left_c, dense, roll(dense, 8))

    def assemble(n, copies, store):
        for copy in copies:
            copy.wait_recv()
        for a in range(8):
            from_x = unpack(pxr[n, a // 2], a % 2)
            from_y = unpack(pyr[n, a // 2], a % 2)
            one = jnp.broadcast_to(pd_r[n, a // 2, 0:1, :], (8, 128))
            two = jnp.broadcast_to(pd_r[n, a // 2, 1:2, :], (8, 128))
            from_d = unpack(jnp.where(block == 1, two, one), a % 2)
            for t in range(2):
                place, row = codes[t]
                value = jnp.where(place == 0, rows(zz[n, a], row), from_d)
                value = jnp.where(place == 1, rows(from_x, row), value)
                value = jnp.where(place == 2, rows(from_y, row), value)
                store(a, t, value)

    def store_q(a, t, value):
        eq[a, :, 128 * t : 128 * t + 128] = 0.25 * value

    coarse = [[None, None] for _ in range(8)]

    def store_0(a, t, value):
        coarse[a][t] = value

    def store_f(a, t, value):
        cols = slice(128 * t, 128 * t + 128)
        ef[a, :, cols] = ef[a, :, cols] + value

    def coarse_parts(e):
        other = sub + 1 - 2 * half_a
        below = [jnp.where(half_a == 1, rows(e[7][t], other), 0.0) for t in range(2)]
        above = [jnp.where(half_a == 0, rows(e[0][t], other), 0.0) for t in range(2)]
        layers = [below] + e + [above]
        return [parts(*layers[a : a + 3], zero, (zero, zero)) for a in range(8)]

    assemble(2, perm_copies, store_q)
    assemble(0, sol_copies, store_0)
    for a, part in enumerate(coarse_parts(coarse)):
        for h, (x, flux, _) in enumerate(part):
            cols = slice(128 * h, 128 * h + 128)
            e0[a, :, cols] = x
            ef[a, :, cols] = REACTION * x + eq[a, :, cols] * flux
    assemble(1, res_copies, store_f)

    iterate = coarse
    for repeat in range(COARSE):
        after = []
        for a, part in enumerate(coarse_parts(iterate)):
            after.append([])
            for h, (x, flux, conduct) in enumerate(part):
                cols = slice(128 * h, 128 * h + 128)
                q = eq[a, :, cols]
                defect = ef[a, :, cols] - (REACTION * x + q * flux)
                after[a].append(x + defect * (DAMPING / (REACTION + q * conduct)))
        iterate = after

    parent_row = (pa // 8) * 2 + (pa % 8) // 4
    low_ob, low_oc = (pa // 2) % 2 == 0, pa % 2 == 0
    for a in range(8):
        one = rows(iterate[a][0] - e0[a, :, 0:128], parent_row)
        two = rows(iterate[a][1] - e0[a, :, 128:256], parent_row)
        value = jnp.where(low_ob, one, two)
        cor[a] = jnp.where(low_oc, value, roll(value, -8))
    spread = exact_dot(jnp.concatenate([cor[a] for a in range(8)], 0), upsample_m[...])
    for a in range(16):
        part = spread[8 * (a // 2) : 8 * (a // 2) + 8]
        va[a + 1] = vb[a + 1] + part

    copies2 = send_faces(2, va)
    own_faces(va, (va, vb))
    take_faces(asked(2), (va, vb), copies2)

    def into_result(a, h, value):
        both_v[0:8, 256 * a + 128 * h : 256 * a + 128 * h + 128] = value

    smooth(INNER - 1)
    jacobi(va, fr, qr, fine_ghosts, into_result, 16)

    for copy in (
        x_copies + msgs + [y_first, y_second] + copies0 + perm_copies + copies1 + sol_copies + res_copies + copies2
    ):
        copy.wait_send()


def body(*args):
    count = 30
    vmem = lambda *shape: pltpu.VMEM(shape, F32)
    any_space = pl.BlockSpec(memory_space=pl.ANY)
    both = pl.pallas_call(
        kernel,
        out_shape=pltpu.VMEM((16, 4096), F32),
        in_specs=[any_space] * 8,
        out_specs=pl.BlockSpec(memory_space=pltpu.VMEM),
        scratch_shapes=[
            vmem(3, 8, 4096), vmem(3, 8, 4096),
            pltpu.SMEM((8,), I32), pltpu.SMEM((8,), I32), pltpu.SMEM((8,), I32), pltpu.SMEM((8,), I32),
            pltpu.VMEM((8, 6), I32), vmem(16, 128), vmem(4, 16, 128),
            vmem(32, 2, 128), vmem(32, 2, 128), vmem(32, 4, 128), vmem(32, 4, 128),
            vmem(2, 18, 8, 256), vmem(16, 8, 256), vmem(16, 8, 256),
            vmem(16, 8, 128), vmem(16, 8, 256), vmem(16, 8, 128), vmem(16, 8, 256),
            vmem(6, 8, 256), vmem(4, 6, 8, 256), vmem(2, 4, 8, 256), vmem(2, 4, 8, 256),
            vmem(3, 4, 8, 128), vmem(3, 4, 8, 128), vmem(3, 4, 8, 128),
            vmem(3, 4, 2, 128), vmem(3, 4, 2, 128),
            vmem(8, 8, 256), vmem(8, 8, 256), vmem(8, 8, 256),
            vmem(8, 8, 128), vmem(3, 8, 8, 128),
            pltpu.VMEM((256, 128), BF16), pltpu.VMEM((128, 256), BF16),
            pltpu.SemaphoreType.REGULAR((4,)), pltpu.SemaphoreType.DMA((8,)), pltpu.SemaphoreType.DMA((count,)), pltpu.SemaphoreType.DMA((count,)),
        ],
        compiler_params=pltpu.CompilerParams(
            collective_id=0, has_side_effects=True, vmem_limit_bytes=32 * 1024 * 1024
        ),
    )(*[pltpu.with_memory_space_constraint(a, pltpu.HBM) for a in args])
    return both[:8], both[8:]


def solution(mesh):
    whole, flat = P(("gx", "gy"), None), P(("gx", "gy"))
    return jax.shard_map(
        body,
        mesh=mesh,
        in_specs=(whole, whole, whole, flat, flat, whole, flat, flat),
        out_specs=(whole, whole),
        check_vma=False,
    )
```

```python
import functools

import jax
import jax.numpy as jnp
from jax import lax
from jax.experimental import pallas as pl
from jax.experimental.pallas import tpu as pltpu
from jax.sharding import PartitionSpec as P

INNER = 3
COARSE = 4
REACTION = 0.25
DAMPING = 0.8
OPP = (1, 0, 3, 2)

F32 = jnp.float32
I32 = jnp.int32
BF16 = jnp.bfloat16

_ROWS = lax.GatherDimensionNumbers(
    offset_dims=(),
    collapsed_slice_dims=(0,),
    start_index_map=(0,),
    operand_batching_dims=(1,),
    start_indices_batching_dims=(1,),
)


def rows(x, index):
    return lax.gather(
        x, index[..., None], _ROWS, (1, 1), mode=lax.GatherScatterMode.PROMISE_IN_BOUNDS
    )


def roll(x, shift):
    return pltpu.roll(x, shift % 128, 1) if shift % 128 else x


def split3(x):
    high = x.astype(BF16)
    rest = x - high.astype(F32)
    mid = rest.astype(BF16)
    low = (rest - mid.astype(F32)).astype(BF16)
    return high, mid, low


def exact_dot(x, matrix):
    count = x.shape[0]
    out = jnp.dot(jnp.concatenate(split3(x), 0), matrix, preferred_element_type=F32)
    return out[:count] + (out[count : 2 * count] + out[2 * count :])


def pairwise(x):
    return ((x[0] + x[1]) + (x[2] + x[3])) + (x[4] + x[5])


def kernel(
    init_h, src_h, perm_h, mx_h, my_h, nb_h, ch_h, pa_h, both_v,
    own, px, t_mx, t_my, t_ch, t_pa, nbv, msg_s, msg_r, yi_s, yi_r, yf_s, yf_r,
    vv, fr, qr, sb, sc, gb, gc, every_s, every_r, gs, gr, ps, pxr, pyr, pd_s, pd_r,
    flux_v, squares_v, e0, ef, eq, cor, zz, restrict_m, upsample_m,
    ready, lsem, ssem, rsem,
):
    va, vb = vv.at[0], vv.at[1]
    i, j = lax.axis_index("gx"), lax.axis_index("gy")
    nx, ny = lax.axis_size("gx"), lax.axis_size("gy")
    xp = (i + 1 - 2 * (i % 2), j)
    yp = (i, j + 1 - 2 * (j % 2))
    diag = (xp[0], yp[1])
    beyond_x = ((i + nx - 1 + 2 * (i % 2)) % nx, j)
    beyond_y = (i, (j + ny - 1 + 2 * (j % 2)) % ny)
    around = (((i + nx - 1) % nx, j), ((i + 1) % nx, j), (i, (j + ny - 1) % ny), (i, (j + 1) % ny))

    tables = [
        pltpu.make_async_copy(a, b, lsem.at[n])
        for n, (a, b) in enumerate(
            ((mx_h, t_mx), (my_h, t_my), (ch_h, t_ch), (pa_h, t_pa), (nb_h, nbv))
        )
    ]
    for copy in tables:
        copy.start()
    fields = [
        pltpu.make_async_copy(a, own.at[n], lsem.at[5 + n])
        for n, a in enumerate((init_h, src_h, perm_h))
    ]
    for copy in fields:
        copy.start()

    even = (i + j) % 2 == 0
    odd = (i + j) % 2 == 1
    barrier = pltpu.get_barrier_semaphore()

    def signal(semaphore, peer):
        pl.semaphore_signal(semaphore, inc=1, device_id=peer, device_id_type=pl.DeviceIdType.MESH)

    @pl.when(even)
    def _():
        signal(barrier, beyond_x)
        signal(barrier, beyond_y)
        pl.semaphore_wait(barrier, 2)
        signal(ready.at[0], xp)
        signal(ready.at[1], yp)

    @pl.when(odd)
    def _():
        signal(barrier, xp)
        signal(barrier, yp)
        pl.semaphore_wait(ready.at[0], 1)

    used = [0]

    def push(source, target, peer):
        n = used[0]
        used[0] += 1
        return pltpu.make_async_remote_copy(
            src_ref=source,
            dst_ref=target,
            send_sem=ssem.at[n],
            recv_sem=rsem.at[n],
            device_id=peer,
            device_id_type=pl.DeviceIdType.MESH,
        )

    def push_around(sources, target):
        base = used[0]
        used[0] += 4
        return [
            pltpu.make_async_remote_copy(
                src_ref=sources(d),
                dst_ref=target(OPP[d]),
                send_sem=ssem.at[base + d],
                recv_sem=rsem.at[base + OPP[d]],
                device_id=around[d],
                device_id_type=pl.DeviceIdType.MESH,
            )
            for d in range(4)
        ]

    x_copies = [push(a, px.at[n], xp) for n, a in enumerate((init_h, src_h, perm_h))]
    for copy in x_copies:
        copy.start()

    lane = lax.broadcasted_iota(I32, (8, 128), 1)
    sub = lax.broadcasted_iota(I32, (8, 128), 0)
    zero = jnp.zeros((8, 128), F32)

    for copy in tables:
        copy.wait()

    def column(ref):
        out = jnp.full((8, 128), ref[0], I32)
        for k in range(1, 8):
            out = jnp.where(sub == k, ref[k], out)
        return out

    mx, my, ch, pa = column(t_mx), column(t_my), column(t_ch), column(t_pa)

    links = [jnp.broadcast_to(nbv[:, f : f + 1], (8, 128)) for f in range(6)]
    away = [jnp.where(c >= 0, c // 8, 7) for c in links]
    slot = [jnp.where(c >= 0, c % 8, 0) for c in links]
    named = sub == t_my[0]
    for k in range(1, 8):
        named = named | (sub == t_my[k])
    free = jnp.where(named, 8.0, sub.astype(F32))
    first = jnp.min(free, axis=0, keepdims=True)
    last = jnp.max(jnp.where(named, 0.0, sub.astype(F32)), axis=0, keepdims=True)
    leave = jnp.where(sub % 2 == 0, jnp.broadcast_to(first, (8, 128)), jnp.broadcast_to(last, (8, 128)))
    leave = jnp.minimum(leave, 7.0).astype(I32)
    leave_e = rows(mx, leave)
    leave_own, leave_row = leave_e < 8, leave_e % 8
    stay = my < 8
    final_e = rows(mx, my % 8)
    final_own, final_row = final_e < 8, final_e % 8
    order = jnp.zeros((8, 128), I32)
    for k in range(8):
        entry = t_my[k]
        order = order + jnp.where((entry >= 8) & (my > entry), 1, 0)
    final_first = order == 0

    def leaving(n, c):
        cols = pl.ds(128 * c, 128)
        return jnp.where(leave_own, rows(own[n, :, cols], leave_row), rows(px[n, :, cols], leave_row))

    fields[0].wait()
    x_copies[0].wait_recv()
    for c in range(32):
        yi_s[c] = leaving(0, c)[0:2]
    y_first = push(yi_s, yi_r, yp)

    @pl.when(odd)
    def _():
        pl.semaphore_wait(ready.at[1], 1)

    y_first.start()

    @pl.when(odd)
    def _():
        pl.semaphore_wait(barrier, 2)
        signal(ready.at[2], beyond_x)
        signal(ready.at[3], beyond_y)

    for n in (1, 2):
        fields[n].wait()
        x_copies[n].wait_recv()
    for c in range(32):
        yf_s[c] = jnp.where(sub < 2, leaving(1, c), leaving(2, c))[0:4]
    y_second = push(yf_s, yf_r, yp)
    y_second.start()

    def arrived(n, ref, top, c):
        cols = pl.ds(128 * c, 128)
        kept = jnp.where(final_own, rows(own[n, :, cols], final_row), rows(px[n, :, cols], final_row))
        one = jnp.broadcast_to(ref[c, top : top + 1, :], (8, 128))
        two = jnp.broadcast_to(ref[c, top + 1 : top + 2, :], (8, 128))
        return jnp.where(stay, kept, jnp.where(final_first, one, two))

    low_b, high_b = lane < 16, lane >= 112
    low_c, high_c = lane % 16 == 0, lane % 16 == 15
    left_half, left_c = lane < 64, lane % 16 < 8
    group, inside = lane // 16, lane % 16
    row_b = jnp.where(left_half, slot[2], slot[3])
    here_b = jnp.where(left_half, away[2], away[3]) == 0
    row_c = jnp.where(left_c, slot[4], slot[5])
    here_c = jnp.where(left_c, away[4], away[5]) == 0
    sent = [(d >= 1) & (d <= 4) for d in away]
    sent_b = (low_b & sent[2], high_b & sent[3])
    sent_c = (low_c & sent[4]) | (high_c & sent[5])

    def pack_faces(v):
        packed = [[v[1, :, 0:128], v[1, :, 128:256]], [v[16, :, 0:128], v[16, :, 128:256]]]
        for _ in range(4):
            packed.append([zero, zero])
        for a in range(16):
            both = jnp.where(left_half, roll(v[a + 1, :, 128:256], 16), roll(v[a + 1, :, 0:128], -16))
            sb[a] = both
            moved = roll(both, 16 * (a % 8))
            packed[3][a // 8] = jnp.where(group == a % 8, moved, packed[3][a // 8])
            packed[2][a // 8] = jnp.where(group == (a + 7) % 8, moved, packed[2][a // 8])
            for h in range(2):
                half = v[a + 1, :, 128 * h : 128 * h + 128]
                both = jnp.where(left_c, roll(half, -15), roll(half, 15))
                sc[a, :, 128 * h : 128 * h + 128] = both
                m, k = (2 * a + h) % 16, (2 * a + h) // 16
                moved = roll(both, m)
                packed[5][k] = jnp.where(inside == m, moved, packed[5][k])
                packed[4][k] = jnp.where(inside == (m + 15) % 16, moved, packed[4][k])
        return packed

    def send_faces(g, v):
        packed = pack_faces(v)
        for d in range(4):
            face, row = give[d]
            for k in range(2):
                out = rows(packed[0][k], row)
                for f in range(1, 6):
                    out = jnp.where(face == f, rows(packed[f][k], row), out)
                gs[g - 1, d, :, 128 * k : 128 * k + 128] = out
        copies = push_around(lambda d: gs.at[g - 1, d], lambda d: gr.at[g - 1, d])
        for copy in copies:
            copy.start()
        return copies

    def own_faces(v, ends):
        for k in range(2):
            cols = slice(128 * k, 128 * k + 128)
            low = jnp.where(away[0] == 0, rows(v[16, :, cols], slot[0]), 0.0)
            high = jnp.where(away[1] == 0, rows(v[1, :, cols], slot[1]), 0.0)
            for end in ends:
                end[0, :, cols] = low
                end[17, :, cols] = high
        for a in range(16):
            gb[a] = jnp.where(here_b, rows(sb[a], row_b), 0.0)
            for h in range(2):
                cols = slice(128 * h, 128 * h + 128)
                gc[a, :, cols] = jnp.where(here_c, rows(sc[a, :, cols], row_c), 0.0)

    def take_faces(got, ends, copies):
        for copy in copies:
            copy.wait_recv()
        came = [[zero, zero] for _ in range(6)]
        for f in range(6):
            for k in range(2):
                for d in range(4):
                    came[f][k] = jnp.where(away[f] == d + 1, got(d, f, slice(128 * k, 128 * k + 128)), came[f][k])
        for k in range(2):
            cols = slice(128 * k, 128 * k + 128)
            low = jnp.where(away[0] == 0, ends[0][0, :, cols], came[0][k])
            high = jnp.where(away[1] == 0, ends[0][17, :, cols], came[1][k])
            for end in ends:
                end[0, :, cols] = low
                end[17, :, cols] = high
        for a in range(16):
            both = jnp.where(group == a % 8, came[2][a // 8], came[3][a // 8])
            gb[a] = jnp.where(here_b, gb[a], roll(both, -16 * (a % 8)))
            for h in range(2):
                cols = slice(128 * h, 128 * h + 128)
                m, k = (2 * a + h) % 16, (2 * a + h) // 16
                both = jnp.where(inside == m, came[4][k], came[5][k])
                gc[a, :, cols] = jnp.where(here_c, gc[a, :, cols], roll(both, -m))

    def halves(v, a):
        return [v[a, :, 0:128], v[a, :, 128:256]]

    def parts(before, x, after, ghost_b, ghost_c):
        down, up = [roll(y, 16) for y in x], [roll(y, -16) for y in x]
        beside_b = (
            (jnp.where(low_b, ghost_b[0], down[0]), jnp.where(high_b, up[1], up[0])),
            (jnp.where(low_b, down[0], down[1]), jnp.where(high_b, ghost_b[1], up[1])),
        )
        out = []
        for h in range(2):
            beside = beside_b[h] + (
                jnp.where(low_c, ghost_c[h], roll(x[h], 1)),
                jnp.where(high_c, ghost_c[h], roll(x[h], -1)),
                before[h],
                after[h],
            )
            mobility = 1.0 + x[h] * x[h]
            square = [w * w for w in beside]
            term = [(mobility + y) * (x[h] - w) for y, w in zip(square, beside)]
            squares = 6.0 * mobility + pairwise(square)
            flux = pairwise(term)
            out.append((x[h], flux, squares))
        return out

    def stencil(v, a, ghost_b, ghost_c):
        return parts(halves(v, a), halves(v, a + 1), halves(v, a + 2), ghost_b, ghost_c)

    def whole(v, a):
        return stencil(v, a, (gb[a], gb[a]), (gc[a, :, 0:128], gc[a, :, 128:256]))

    def begin(v):
        for a in range(16):
            x = halves(v, a + 1)
            ends = [halves(v, a), halves(v, a + 2)]
            if a == 0:
                ends[0] = [jnp.where(sent[0], x[h], ends[0][h]) for h in range(2)]
            if a == 15:
                ends[1] = [jnp.where(sent[1], x[h], ends[1][h]) for h in range(2)]
            ghost_b = [jnp.where(sent_b[h], x[h], gb[a]) for h in range(2)]
            ghost_c = [jnp.where(sent_c, x[h], gc[a, :, 128 * h : 128 * h + 128]) for h in range(2)]
            for h, (_, flux, squares) in enumerate(parts(ends[0], x, ends[1], ghost_b, ghost_c)):
                flux_v[a, :, 128 * h : 128 * h + 128] = flux
                squares_v[a, :, 128 * h : 128 * h + 128] = squares

    def complete(v, a):
        out = []
        for h, x in enumerate(halves(v, a + 1)):
            cols = slice(128 * h, 128 * h + 128)
            ghosts = [(sent_b[h], gb[a]), (sent_c, gc[a, :, cols])]
            if a == 0:
                ghosts.append((sent[0], v[0, :, cols]))
            if a == 15:
                ghosts.append((sent[1], v[17, :, cols]))
            own_square = x * x
            mobility = 1.0 + own_square
            flux, squares = flux_v[a, :, cols], squares_v[a, :, cols]
            for mask, ghost in ghosts:
                w = jnp.where(mask, ghost, x)
                square = w * w
                flux = flux + (mobility + square) * (x - w)
                squares = squares + (square - own_square)
            out.append((x, flux, squares))
        return out

    def jacobi(v, force, coefficient, sums, store, count):
        for a in range(count):
            for h, (x, flux, conduct) in enumerate(sums(v, a)):
                cols = slice(128 * h, 128 * h + 128)
                q = coefficient[a, :, cols]
                defect = force[a, :, cols] - (REACTION * x + q * flux)
                store(a, h, x + defect * (DAMPING / (REACTION + q * conduct)))

    def into(ref):
        def store(a, h, value):
            ref[a + 1, :, 128 * h : 128 * h + 128] = value

        return store

    def smooth(sweeps):
        for n in range(sweeps):
            jacobi(vv.at[n % 2], fr, qr, whole if n else complete, into(vv.at[(n + 1) % 2]), 16)

    def shrink(n, layer):
        fold = jnp.concatenate([layer(2 * a) + layer(2 * a + 1) for a in range(8)], 0)
        out = exact_dot(fold, restrict_m[...])
        for a in range(8):
            zz[n, a] = out[8 * a : 8 * a + 8]
        for m in range(4):
            dense = jnp.where(left_c, out[16 * m : 16 * m + 8], out[16 * m + 8 : 16 * m + 16])
            ps[n, m] = dense
            pd_s[n, m] = rows(dense, outward)[0:2]
        copies = [
            push(ps.at[n], pxr.at[n], xp),
            push(ps.at[n], pyr.at[n], yp),
            push(pd_s.at[n], pd_r.at[n], diag),
        ]
        for copy in copies:
            copy.start()
        return copies

    slots = sub.astype(F32)
    to_x = jnp.sum(jnp.where(pa // 8 == 1, slots, 0.0), axis=0, keepdims=True)
    to_y = jnp.sum(jnp.where(pa // 8 == 2, slots, 0.0), axis=0, keepdims=True)
    outward = jnp.where(sub == 0, jnp.broadcast_to(to_x, (8, 128)), jnp.broadcast_to(to_y, (8, 128)))
    outward = outward.astype(I32)

    y_first.wait_recv()
    for c in range(32):
        va[1 + c // 2, :, 128 * (c % 2) : 128 * (c % 2) + 128] = arrived(0, yi_r, 0, c)
    packed = pack_faces(va)
    for f in range(6):
        for k in range(2):
            every_s[f, :, 128 * k : 128 * k + 128] = packed[f][k]

    @pl.when(even)
    def _():
        pl.semaphore_wait(ready.at[2], 1)
        pl.semaphore_wait(ready.at[3], 1)

    copies0 = push_around(lambda d: every_s, lambda d: every_r.at[d])
    for copy in copies0:
        copy.start()
    own_faces(va, (va, vb))
    begin(va)

    marks = jnp.concatenate([(lane == d).astype(F32) for d in away], 0)
    before = (
        lax.broadcasted_iota(I32, (48, 48), 1) < lax.broadcasted_iota(I32, (48, 48), 0)
    ).astype(F32)
    counts = jnp.dot(before, marks, preferred_element_type=F32)
    rank = []
    wanted = zero
    for f in range(6):
        mine = jnp.where(lane == away[f], counts[8 * f : 8 * f + 8], 0.0)
        place = jnp.broadcast_to(jnp.sum(mine, axis=1, keepdims=True), (8, 128)).astype(I32)
        place = jnp.minimum(place, 7)
        rank.append(place)
        remote = (away[f] >= 1) & (away[f] <= 4)
        hit = (lane == away[f] * 8 + place) & remote
        wanted = wanted + jnp.where(hit, ((f ^ 1) * 8 + slot[f]).astype(F32), 0.0)
    msg_s[0:8, :] = jnp.broadcast_to(jnp.sum(wanted, axis=0, keepdims=True), (8, 128))
    msg_s[8:16, :] = ch.astype(F32)

    msgs = push_around(lambda d: msg_s, lambda d: msg_r.at[d])
    for copy in msgs:
        copy.start()

    fine = lax.broadcasted_iota(I32, (256, 128), 0)
    small = lax.broadcasted_iota(I32, (256, 128), 1)
    same = (fine // 32 == small // 16) & ((fine % 16) // 2 == small % 8)
    restrict_m[...] = jnp.where(same, 0.125, 0.0).astype(BF16)
    fine = lax.broadcasted_iota(I32, (128, 256), 1)
    small = lax.broadcasted_iota(I32, (128, 256), 0)
    same = (fine // 32 == small // 16) & ((fine % 16) // 2 == small % 16)
    upsample_m[...] = jnp.where(same, 1.0, 0.0).astype(BF16)

    y_second.wait_recv()
    for c in range(32):
        cols = slice(128 * (c % 2), 128 * (c % 2) + 128)
        fr[c // 2, :, cols] = arrived(1, yf_r, 0, c)
        qr[c // 2, :, cols] = 0.5 * arrived(2, yf_r, 2, c)
    perm_copies = shrink(2, lambda a: qr[a])
    take_faces(lambda d, f, cols: rows(every_r[d, f ^ 1, :, cols], slot[f]), (va, vb), copies0)
    smooth(INNER)

    for copy in msgs:
        copy.wait_recv()
    give = []
    for d in range(4):
        code = jnp.where(lane == (OPP[d] + 1) * 8 + sub, msg_r[d, 0:8, :], 0.0)
        code = jnp.broadcast_to(jnp.sum(code, axis=1, keepdims=True), (8, 128)).astype(I32)
        give.append((code // 8, code % 8))
    ch_x = msg_r[1 - i % 2, 8:16, :].astype(I32)
    ch_y = msg_r[3 - j % 2, 8:16, :].astype(I32)

    def asked(g):
        return lambda d, f, cols: rows(gr[g - 1, d, :, cols], rank[f])

    copies1 = send_faces(1, vb)
    own_faces(vb, (vb,))
    begin(vb)
    sol_copies = shrink(0, lambda a: vb[a + 1])
    take_faces(asked(1), (vb,), copies1)

    layers = []
    for a in range(16):
        layers.append([])
        for h, (x, flux, _) in enumerate(complete(vb, a)):
            cols = slice(128 * h, 128 * h + 128)
            value = fr[a, :, cols] - (REACTION * x + qr[a, :, cols] * flux)
            both_v[8:16, 256 * a + 128 * h : 256 * a + 128 * h + 128] = value
            layers[a].append(value)
    res_copies = shrink(1, lambda a: jnp.concatenate(layers[a], 1))

    block, half_a = sub // 2, sub % 2
    side_c = (lane // 8) % 2
    codes = []
    for t in range(2):
        at = half_a * 4 + 2 * t + side_c
        code = jnp.where(block == 1, rows(ch_x, at), jnp.where(block == 2, rows(ch_y, at), rows(ch, at)))
        source = code // 8
        place = jnp.where(
            block == 1,
            jnp.where(source == 0, 1, jnp.where(source == 1, 0, 3)),
            jnp.where(block == 2, jnp.where(source == 0, 2, jnp.where(source == 1, 3, 0)), source),
        )
        codes.append((place, code % 8))

    def unpack(dense, odd):
        if odd:
            return jnp.where(left_c, roll(dense, -8), dense)
        return jnp.where(left_c, dense, roll(dense, 8))

    def assemble(n, copies, store):
        for copy in copies:
            copy.wait_recv()
        for a in range(8):
            from_x = unpack(pxr[n, a // 2], a % 2)
            from_y = unpack(pyr[n, a // 2], a % 2)
            one = jnp.broadcast_to(pd_r[n, a // 2, 0:1, :], (8, 128))
            two = jnp.broadcast_to(pd_r[n, a // 2, 1:2, :], (8, 128))
            from_d = unpack(jnp.where(block == 1, two, one), a % 2)
            for t in range(2):
                place, row = codes[t]
                value = jnp.where(place == 0, rows(zz[n, a], row), from_d)
                value = jnp.where(place == 1, rows(from_x, row), value)
                value = jnp.where(place == 2, rows(from_y, row), value)
                store(a, t, value)

    def store_q(a, t, value):
        eq[a, :, 128 * t : 128 * t + 128] = 0.25 * value

    coarse = [[None, None] for _ in range(8)]

    def store_0(a, t, value):
        coarse[a][t] = value

    def coarse_parts(e):
        other = sub + 1 - 2 * half_a
        below = [jnp.where(half_a == 1, rows(e[7][t], other), 0.0) for t in range(2)]
        above = [jnp.where(half_a == 0, rows(e[0][t], other), 0.0) for t in range(2)]
        layers = [below] + e + [above]
        return [parts(*layers[a : a + 3], (zero, zero), (zero, zero)) for a in range(8)]

    assemble(2, perm_copies, store_q)
    assemble(0, sol_copies, store_0)
    iterate = [[None, None] for _ in range(8)]
    pace = [[None, None] for _ in range(8)]
    for a, part in enumerate(coarse_parts(coarse)):
        for h, (x, flux, conduct) in enumerate(part):
            cols = slice(128 * h, 128 * h + 128)
            e0[a, :, cols] = x
            ef[a, :, cols] = REACTION * x + eq[a, :, cols] * flux
            pace[a][h] = DAMPING / (REACTION + eq[a, :, cols] * conduct)

    def store_f(a, t, value):
        cols = slice(128 * t, 128 * t + 128)
        ef[a, :, cols] = ef[a, :, cols] + value
        iterate[a][t] = coarse[a][t] + value * pace[a][t]

    assemble(1, res_copies, store_f)

    for repeat in range(COARSE - 1):
        after = []
        for a, part in enumerate(coarse_parts(iterate)):
            after.append([])
            for h, (x, flux, conduct) in enumerate(part):
                cols = slice(128 * h, 128 * h + 128)
                q = eq[a, :, cols]
                defect = ef[a, :, cols] - (REACTION * x + q * flux)
                after[a].append(x + defect * (DAMPING / (REACTION + q * conduct)))
        iterate = after

    parent_row = (pa // 8) * 2 + (pa % 8) // 4
    low_ob, low_oc = (pa // 2) % 2 == 0, pa % 2 == 0
    for a in range(8):
        one = rows(iterate[a][0] - e0[a, :, 0:128], parent_row)
        two = rows(iterate[a][1] - e0[a, :, 128:256], parent_row)
        value = jnp.where(low_ob, one, two)
        cor[a] = jnp.where(low_oc, value, roll(value, -8))
    spread = exact_dot(jnp.concatenate([cor[a] for a in range(8)], 0), upsample_m[...])
    for a in range(16):
        part = spread[8 * (a // 2) : 8 * (a // 2) + 8]
        va[a + 1] = vb[a + 1] + part

    copies2 = send_faces(2, va)
    own_faces(va, (va, vb))
    begin(va)
    take_faces(asked(2), (va, vb), copies2)

    def into_result(a, h, value):
        both_v[0:8, 256 * a + 128 * h : 256 * a + 128 * h + 128] = value

    smooth(INNER - 1)
    jacobi(va, fr, qr, whole, into_result, 16)

    for copy in (
        x_copies + msgs + [y_first, y_second] + copies0 + perm_copies + copies1 + sol_copies + res_copies + copies2
    ):
        copy.wait_send()


def body(*args):
    count = 30
    vmem = lambda *shape: pltpu.VMEM(shape, F32)
    any_space = pl.BlockSpec(memory_space=pl.ANY)
    both = pl.pallas_call(
        kernel,
        out_shape=pltpu.VMEM((16, 4096), F32),
        in_specs=[any_space] * 8,
        out_specs=pl.BlockSpec(memory_space=pltpu.VMEM),
        scratch_shapes=[
            vmem(3, 8, 4096), vmem(3, 8, 4096),
            pltpu.SMEM((8,), I32), pltpu.SMEM((8,), I32), pltpu.SMEM((8,), I32), pltpu.SMEM((8,), I32),
            pltpu.VMEM((8, 6), I32), vmem(16, 128), vmem(4, 16, 128),
            vmem(32, 2, 128), vmem(32, 2, 128), vmem(32, 4, 128), vmem(32, 4, 128),
            vmem(2, 18, 8, 256), vmem(16, 8, 256), vmem(16, 8, 256),
            vmem(16, 8, 128), vmem(16, 8, 256), vmem(16, 8, 128), vmem(16, 8, 256),
            vmem(6, 8, 256), vmem(4, 6, 8, 256), vmem(2, 4, 8, 256), vmem(2, 4, 8, 256),
            vmem(3, 4, 8, 128), vmem(3, 4, 8, 128), vmem(3, 4, 8, 128),
            vmem(3, 4, 2, 128), vmem(3, 4, 2, 128),
            vmem(16, 8, 256), vmem(16, 8, 256), vmem(8, 8, 256), vmem(8, 8, 256), vmem(8, 8, 256),
            vmem(8, 8, 128), vmem(3, 8, 8, 128),
            pltpu.VMEM((256, 128), BF16), pltpu.VMEM((128, 256), BF16),
            pltpu.SemaphoreType.REGULAR((4,)), pltpu.SemaphoreType.DMA((8,)), pltpu.SemaphoreType.DMA((count,)), pltpu.SemaphoreType.DMA((count,)),
        ],
        compiler_params=pltpu.CompilerParams(
            collective_id=0, has_side_effects=True, vmem_limit_bytes=32 * 1024 * 1024
        ),
    )(*[pltpu.with_memory_space_constraint(a, pltpu.HBM) for a in args])
    return both[:8], both[8:]


def solution(mesh):
    whole, flat = P(("gx", "gy"), None), P(("gx", "gy"))
    return jax.shard_map(
        body,
        mesh=mesh,
        in_specs=(whole, whole, whole, flat, flat, whole, flat, flat),
        out_specs=(whole, whole),
        check_vma=False,
    )
```

```python
import functools

import jax
import jax.numpy as jnp
from jax import lax
from jax.experimental import pallas as pl
from jax.experimental.pallas import tpu as pltpu
from jax.sharding import PartitionSpec as P

INNER = 3
COARSE = 4
REACTION = 0.25
DAMPING = 0.8
OPP = (1, 0, 3, 2)

F32 = jnp.float32
I32 = jnp.int32
BF16 = jnp.bfloat16

_ROWS = lax.GatherDimensionNumbers(
    offset_dims=(),
    collapsed_slice_dims=(0,),
    start_index_map=(0,),
    operand_batching_dims=(1,),
    start_indices_batching_dims=(1,),
)


def rows(x, index):
    return lax.gather(
        x, index[..., None], _ROWS, (1, 1), mode=lax.GatherScatterMode.PROMISE_IN_BOUNDS
    )


def roll(x, shift):
    return pltpu.roll(x, shift % 128, 1) if shift % 128 else x


def split3(x):
    high = x.astype(BF16)
    rest = x - high.astype(F32)
    mid = rest.astype(BF16)
    low = (rest - mid.astype(F32)).astype(BF16)
    return high, mid, low


def exact_dot(x, matrix):
    count = x.shape[0]
    out = jnp.dot(jnp.concatenate(split3(x), 0), matrix, preferred_element_type=F32)
    return out[:count] + (out[count : 2 * count] + out[2 * count :])


def pairwise(x):
    return ((x[0] + x[1]) + (x[2] + x[3])) + (x[4] + x[5])


def kernel(
    init_h, src_h, perm_h, mx_h, my_h, nb_h, ch_h, pa_h, both_v,
    own, px, t_mx, t_my, t_ch, t_pa, nbv, msg_s, msg_r, yi_s, yi_r, yf_s, yf_r,
    vv, fr, qr, sb, sc, gb, gc, every_s, every_r, gs, gr, ps, pxr, pyr, pd_s, pd_r,
    flux_v, squares_v, e0, ef, eq, cor, zz, restrict_m, upsample_m,
    ready, lsem, ssem, rsem,
):
    va, vb = vv.at[0], vv.at[1]
    i, j = lax.axis_index("gx"), lax.axis_index("gy")
    nx, ny = lax.axis_size("gx"), lax.axis_size("gy")
    xp = (i + 1 - 2 * (i % 2), j)
    yp = (i, j + 1 - 2 * (j % 2))
    diag = (xp[0], yp[1])
    beyond_x = ((i + nx - 1 + 2 * (i % 2)) % nx, j)
    beyond_y = (i, (j + ny - 1 + 2 * (j % 2)) % ny)
    around = (((i + nx - 1) % nx, j), ((i + 1) % nx, j), (i, (j + ny - 1) % ny), (i, (j + 1) % ny))

    tables = [
        pltpu.make_async_copy(a, b, lsem.at[n])
        for n, (a, b) in enumerate(
            ((mx_h, t_mx), (my_h, t_my), (ch_h, t_ch), (pa_h, t_pa), (nb_h, nbv))
        )
    ]
    for copy in tables:
        copy.start()
    fields = [
        pltpu.make_async_copy(a, own.at[n], lsem.at[5 + n])
        for n, a in enumerate((init_h, src_h, perm_h))
    ]
    for copy in fields:
        copy.start()

    even = (i + j) % 2 == 1
    odd = (i + j) % 2 == 0
    barrier = pltpu.get_barrier_semaphore()

    def signal(semaphore, peer):
        pl.semaphore_signal(semaphore, inc=1, device_id=peer, device_id_type=pl.DeviceIdType.MESH)

    @pl.when(even)
    def _():
        signal(barrier, beyond_x)
        signal(barrier, beyond_y)
        pl.semaphore_wait(barrier, 2)
        signal(ready.at[0], xp)
        signal(ready.at[1], yp)

    @pl.when(odd)
    def _():
        signal(barrier, xp)
        signal(barrier, yp)
        pl.semaphore_wait(ready.at[0], 1)

    used = [0]

    def push(source, target, peer):
        n = used[0]
        used[0] += 1
        return pltpu.make_async_remote_copy(
            src_ref=source,
            dst_ref=target,
            send_sem=ssem.at[n],
            recv_sem=rsem.at[n],
            device_id=peer,
            device_id_type=pl.DeviceIdType.MESH,
        )

    def push_around(sources, target):
        base = used[0]
        used[0] += 4
        return [
            pltpu.make_async_remote_copy(
                src_ref=sources(d),
                dst_ref=target(OPP[d]),
                send_sem=ssem.at[base + d],
                recv_sem=rsem.at[base + OPP[d]],
                device_id=around[d],
                device_id_type=pl.DeviceIdType.MESH,
            )
            for d in range(4)
        ]

    fields[0].wait()
    x_copies = [push(a, px.at[n], xp) for n, a in enumerate((own.at[0], src_h, perm_h))]
    for copy in x_copies:
        copy.start()

    lane = lax.broadcasted_iota(I32, (8, 128), 1)
    sub = lax.broadcasted_iota(I32, (8, 128), 0)
    zero = jnp.zeros((8, 128), F32)

    for copy in tables:
        copy.wait()

    def column(ref):
        out = jnp.full((8, 128), ref[0], I32)
        for k in range(1, 8):
            out = jnp.where(sub == k, ref[k], out)
        return out

    mx, my, ch, pa = column(t_mx), column(t_my), column(t_ch), column(t_pa)

    links = [jnp.broadcast_to(nbv[:, f : f + 1], (8, 128)) for f in range(6)]
    away = [jnp.where(c >= 0, c // 8, 7) for c in links]
    slot = [jnp.where(c >= 0, c % 8, 0) for c in links]
    named = sub == t_my[0]
    for k in range(1, 8):
        named = named | (sub == t_my[k])
    free = jnp.where(named, 8.0, sub.astype(F32))
    first = jnp.min(free, axis=0, keepdims=True)
    last = jnp.max(jnp.where(named, 0.0, sub.astype(F32)), axis=0, keepdims=True)
    leave = jnp.where(sub % 2 == 0, jnp.broadcast_to(first, (8, 128)), jnp.broadcast_to(last, (8, 128)))
    leave = jnp.minimum(leave, 7.0).astype(I32)
    leave_e = rows(mx, leave)
    leave_own, leave_row = leave_e < 8, leave_e % 8
    stay = my < 8
    final_e = rows(mx, my % 8)
    final_own, final_row = final_e < 8, final_e % 8
    order = jnp.zeros((8, 128), I32)
    for k in range(8):
        entry = t_my[k]
        order = order + jnp.where((entry >= 8) & (my > entry), 1, 0)
    final_first = order == 0

    def leaving(n, c):
        cols = pl.ds(128 * c, 128)
        return jnp.where(leave_own, rows(own[n, :, cols], leave_row), rows(px[n, :, cols], leave_row))

    x_copies[0].wait_recv()
    for c in range(32):
        yi_s[c] = leaving(0, c)[0:2]
    y_first = push(yi_s, yi_r, yp)

    @pl.when(odd)
    def _():
        pl.semaphore_wait(ready.at[1], 1)

    y_first.start()

    @pl.when(odd)
    def _():
        pl.semaphore_wait(barrier, 2)
        signal(ready.at[2], beyond_x)
        signal(ready.at[3], beyond_y)

    for n in (1, 2):
        fields[n].wait()
        x_copies[n].wait_recv()
    for c in range(32):
        yf_s[c] = jnp.where(sub < 2, leaving(1, c), leaving(2, c))[0:4]
    y_second = push(yf_s, yf_r, yp)
    y_second.start()

    def arrived(n, ref, top, c):
        cols = pl.ds(128 * c, 128)
        kept = jnp.where(final_own, rows(own[n, :, cols], final_row), rows(px[n, :, cols], final_row))
        one = jnp.broadcast_to(ref[c, top : top + 1, :], (8, 128))
        two = jnp.broadcast_to(ref[c, top + 1 : top + 2, :], (8, 128))
        return jnp.where(stay, kept, jnp.where(final_first, one, two))

    low_b, high_b = lane < 16, lane >= 112
    low_c, high_c = lane % 16 == 0, lane % 16 == 15
    left_half, left_c = lane < 64, lane % 16 < 8
    group, inside = lane // 16, lane % 16
    row_b = jnp.where(left_half, slot[2], slot[3])
    here_b = jnp.where(left_half, away[2], away[3]) == 0
    row_c = jnp.where(left_c, slot[4], slot[5])
    here_c = jnp.where(left_c, away[4], away[5]) == 0
    sent = [(d >= 1) & (d <= 4) for d in away]
    sent_b = (low_b & sent[2], high_b & sent[3])
    sent_c = (low_c & sent[4]) | (high_c & sent[5])

    def pack_faces(v):
        packed = [[v[1, :, 0:128], v[1, :, 128:256]], [v[16, :, 0:128], v[16, :, 128:256]]]
        for _ in range(4):
            packed.append([zero, zero])
        for a in range(16):
            both = jnp.where(left_half, roll(v[a + 1, :, 128:256], 16), roll(v[a + 1, :, 0:128], -16))
            sb[a] = both
            moved = roll(both, 16 * (a % 8))
            packed[3][a // 8] = jnp.where(group == a % 8, moved, packed[3][a // 8])
            packed[2][a // 8] = jnp.where(group == (a + 7) % 8, moved, packed[2][a // 8])
            for h in range(2):
                half = v[a + 1, :, 128 * h : 128 * h + 128]
                both = jnp.where(left_c, roll(half, -15), roll(half, 15))
                sc[a, :, 128 * h : 128 * h + 128] = both
                m, k = (2 * a + h) % 16, (2 * a + h) // 16
                moved = roll(both, m)
                packed[5][k] = jnp.where(inside == m, moved, packed[5][k])
                packed[4][k] = jnp.where(inside == (m + 15) % 16, moved, packed[4][k])
        return packed

    def send_faces(g, v):
        packed = pack_faces(v)
        for d in range(4):
            face, row = give[d]
            for k in range(2):
                out = rows(packed[0][k], row)
                for f in range(1, 6):
                    out = jnp.where(face == f, rows(packed[f][k], row), out)
                gs[g - 1, d, :, 128 * k : 128 * k + 128] = out
        copies = push_around(lambda d: gs.at[g - 1, d], lambda d: gr.at[g - 1, d])
        for copy in copies:
            copy.start()
        return copies

    def own_faces(v, ends):
        for k in range(2):
            cols = slice(128 * k, 128 * k + 128)
            low = jnp.where(away[0] == 0, rows(v[16, :, cols], slot[0]), 0.0)
            high = jnp.where(away[1] == 0, rows(v[1, :, cols], slot[1]), 0.0)
            for end in ends:
                end[0, :, cols] = low
                end[17, :, cols] = high
        for a in range(16):
            gb[a] = jnp.where(here_b, rows(sb[a], row_b), 0.0)
            for h in range(2):
                cols = slice(128 * h, 128 * h + 128)
                gc[a, :, cols] = jnp.where(here_c, rows(sc[a, :, cols], row_c), 0.0)

    def take_faces(got, ends, copies):
        for copy in copies:
            copy.wait_recv()
        came = [[zero, zero] for _ in range(6)]
        for f in range(6):
            for k in range(2):
                for d in range(4):
                    came[f][k] = jnp.where(away[f] == d + 1, got(d, f, slice(128 * k, 128 * k + 128)), came[f][k])
        for k in range(2):
            cols = slice(128 * k, 128 * k + 128)
            low = jnp.where(away[0] == 0, ends[0][0, :, cols], came[0][k])
            high = jnp.where(away[1] == 0, ends[0][17, :, cols], came[1][k])
            for end in ends:
                end[0, :, cols] = low
                end[17, :, cols] = high
        for a in range(16):
            both = jnp.where(group == a % 8, came[2][a // 8], came[3][a // 8])
            gb[a] = jnp.where(here_b, gb[a], roll(both, -16 * (a % 8)))
            for h in range(2):
                cols = slice(128 * h, 128 * h + 128)
                m, k = (2 * a + h) % 16, (2 * a + h) // 16
                both = jnp.where(inside == m, came[4][k], came[5][k])
                gc[a, :, cols] = jnp.where(here_c, gc[a, :, cols], roll(both, -m))

    def halves(v, a):
        return [v[a, :, 0:128], v[a, :, 128:256]]

    def parts(before, x, after, ghost_b, ghost_c):
        down, up = [roll(y, 16) for y in x], [roll(y, -16) for y in x]
        beside_b = (
            (jnp.where(low_b, ghost_b[0], down[0]), jnp.where(high_b, up[1], up[0])),
            (jnp.where(low_b, down[0], down[1]), jnp.where(high_b, ghost_b[1], up[1])),
        )
        out = []
        for h in range(2):
            beside = beside_b[h] + (
                jnp.where(low_c, ghost_c[h], roll(x[h], 1)),
                jnp.where(high_c, ghost_c[h], roll(x[h], -1)),
                before[h],
                after[h],
            )
            mobility = 1.0 + x[h] * x[h]
            square = [w * w for w in beside]
            term = [(mobility + y) * (x[h] - w) for y, w in zip(square, beside)]
            squares = 6.0 * mobility + pairwise(square)
            flux = pairwise(term)
            out.append((x[h], flux, squares))
        return out

    def stencil(v, a, ghost_b, ghost_c):
        return parts(halves(v, a), halves(v, a + 1), halves(v, a + 2), ghost_b, ghost_c)

    def whole(v, a):
        return stencil(v, a, (gb[a], gb[a]), (gc[a, :, 0:128], gc[a, :, 128:256]))

    def begin(v):
        for a in range(16):
            x = halves(v, a + 1)
            ends = [halves(v, a), halves(v, a + 2)]
            if a == 0:
                ends[0] = [jnp.where(sent[0], x[h], ends[0][h]) for h in range(2)]
            if a == 15:
                ends[1] = [jnp.where(sent[1], x[h], ends[1][h]) for h in range(2)]
            ghost_b = [jnp.where(sent_b[h], x[h], gb[a]) for h in range(2)]
            ghost_c = [jnp.where(sent_c, x[h], gc[a, :, 128 * h : 128 * h + 128]) for h in range(2)]
            for h, (_, flux, squares) in enumerate(parts(ends[0], x, ends[1], ghost_b, ghost_c)):
                flux_v[a, :, 128 * h : 128 * h + 128] = flux
                squares_v[a, :, 128 * h : 128 * h + 128] = squares

    def complete(v, a):
        out = []
        for h, x in enumerate(halves(v, a + 1)):
            cols = slice(128 * h, 128 * h + 128)
            ghosts = [(sent_b[h], gb[a]), (sent_c, gc[a, :, cols])]
            if a == 0:
                ghosts.append((sent[0], v[0, :, cols]))
            if a == 15:
                ghosts.append((sent[1], v[17, :, cols]))
            own_square = x * x
            mobility = 1.0 + own_square
            flux, squares = flux_v[a, :, cols], squares_v[a, :, cols]
            for mask, ghost in ghosts:
                w = jnp.where(mask, ghost, x)
                square = w * w
                flux = flux + (mobility + square) * (x - w)
                squares = squares + (square - own_square)
            out.append((x, flux, squares))
        return out

    def jacobi(v, force, coefficient, sums, store, count):
        for a in range(count):
            for h, (x, flux, conduct) in enumerate(sums(v, a)):
                cols = slice(128 * h, 128 * h + 128)
                q = coefficient[a, :, cols]
                defect = force[a, :, cols] - (REACTION * x + q * flux)
                store(a, h, x + defect * (DAMPING / (REACTION + q * conduct)))

    def into(ref):
        def store(a, h, value):
            ref[a + 1, :, 128 * h : 128 * h + 128] = value

        return store

    def smooth(sweeps):
        for n in range(sweeps):
            jacobi(vv.at[n % 2], fr, qr, whole if n else complete, into(vv.at[(n + 1) % 2]), 16)

    def shrink(n, layer):
        fold = jnp.concatenate([layer(2 * a) + layer(2 * a + 1) for a in range(8)], 0)
        out = exact_dot(fold, restrict_m[...])
        for a in range(8):
            zz[n, a] = out[8 * a : 8 * a + 8]
        for m in range(4):
            dense = jnp.where(left_c, out[16 * m : 16 * m + 8], out[16 * m + 8 : 16 * m + 16])
            ps[n, m] = dense
            pd_s[n, m] = rows(dense, outward)[0:2]
        copies = [
            push(ps.at[n], pxr.at[n], xp),
            push(ps.at[n], pyr.at[n], yp),
            push(pd_s.at[n], pd_r.at[n], diag),
        ]
        for copy in copies:
            copy.start()
        return copies

    slots = sub.astype(F32)
    to_x = jnp.sum(jnp.where(pa // 8 == 1, slots, 0.0), axis=0, keepdims=True)
    to_y = jnp.sum(jnp.where(pa // 8 == 2, slots, 0.0), axis=0, keepdims=True)
    outward = jnp.where(sub == 0, jnp.broadcast_to(to_x, (8, 128)), jnp.broadcast_to(to_y, (8, 128)))
    outward = outward.astype(I32)

    y_first.wait_recv()
    for c in range(32):
        va[1 + c // 2, :, 128 * (c % 2) : 128 * (c % 2) + 128] = arrived(0, yi_r, 0, c)
    packed = pack_faces(va)
    for f in range(6):
        for k in range(2):
            every_s[f, :, 128 * k : 128 * k + 128] = packed[f][k]

    @pl.when(even)
    def _():
        pl.semaphore_wait(ready.at[2], 1)
        pl.semaphore_wait(ready.at[3], 1)

    copies0 = push_around(lambda d: every_s, lambda d: every_r.at[d])
    for copy in copies0:
        copy.start()
    own_faces(va, (va, vb))
    begin(va)

    marks = jnp.concatenate([(lane == d).astype(F32) for d in away], 0)
    before = (
        lax.broadcasted_iota(I32, (48, 48), 1) < lax.broadcasted_iota(I32, (48, 48), 0)
    ).astype(F32)
    counts = jnp.dot(before, marks, preferred_element_type=F32)
    rank = []
    wanted = zero
    for f in range(6):
        mine = jnp.where(lane == away[f], counts[8 * f : 8 * f + 8], 0.0)
        place = jnp.broadcast_to(jnp.sum(mine, axis=1, keepdims=True), (8, 128)).astype(I32)
        place = jnp.minimum(place, 7)
        rank.append(place)
        remote = (away[f] >= 1) & (away[f] <= 4)
        hit = (lane == away[f] * 8 + place) & remote
        wanted = wanted + jnp.where(hit, ((f ^ 1) * 8 + slot[f]).astype(F32), 0.0)
    msg_s[0:8, :] = jnp.broadcast_to(jnp.sum(wanted, axis=0, keepdims=True), (8, 128))
    msg_s[8:16, :] = ch.astype(F32)

    msgs = push_around(lambda d: msg_s, lambda d: msg_r.at[d])
    for copy in msgs:
        copy.start()

    fine = lax.broadcasted_iota(I32, (256, 128), 0)
    small = lax.broadcasted_iota(I32, (256, 128), 1)
    same = (fine // 32 == small // 16) & ((fine % 16) // 2 == small % 8)
    restrict_m[...] = jnp.where(same, 0.125, 0.0).astype(BF16)
    fine = lax.broadcasted_iota(I32, (128, 256), 1)
    small = lax.broadcasted_iota(I32, (128, 256), 0)
    same = (fine // 32 == small // 16) & ((fine % 16) // 2 == small % 16)
    upsample_m[...] = jnp.where(same, 1.0, 0.0).astype(BF16)

    y_second.wait_recv()
    for c in range(32):
        cols = slice(128 * (c % 2), 128 * (c % 2) + 128)
        fr[c // 2, :, cols] = arrived(1, yf_r, 0, c)
        qr[c // 2, :, cols] = 0.5 * arrived(2, yf_r, 2, c)
    perm_copies = shrink(2, lambda a: qr[a])
    take_faces(lambda d, f, cols: rows(every_r[d, f ^ 1, :, cols], slot[f]), (va, vb), copies0)
    smooth(INNER)

    for copy in msgs:
        copy.wait_recv()
    give = []
    for d in range(4):
        code = jnp.where(lane == (OPP[d] + 1) * 8 + sub, msg_r[d, 0:8, :], 0.0)
        code = jnp.broadcast_to(jnp.sum(code, axis=1, keepdims=True), (8, 128)).astype(I32)
        give.append((code // 8, code % 8))
    ch_x = msg_r[1 - i % 2, 8:16, :].astype(I32)
    ch_y = msg_r[3 - j % 2, 8:16, :].astype(I32)

    def asked(g):
        return lambda d, f, cols: rows(gr[g - 1, d, :, cols], rank[f])

    copies1 = send_faces(1, vb)
    own_faces(vb, (vb,))
    begin(vb)
    sol_copies = shrink(0, lambda a: vb[a + 1])
    take_faces(asked(1), (vb,), copies1)

    layers = []
    for a in range(16):
        layers.append([])
        for h, (x, flux, _) in enumerate(complete(vb, a)):
            cols = slice(128 * h, 128 * h + 128)
            value = fr[a, :, cols] - (REACTION * x + qr[a, :, cols] * flux)
            both_v[8:16, 256 * a + 128 * h : 256 * a + 128 * h + 128] = value
            layers[a].append(value)
    res_copies = shrink(1, lambda a: jnp.concatenate(layers[a], 1))

    block, half_a = sub // 2, sub % 2
    side_c = (lane // 8) % 2
    codes = []
    for t in range(2):
        at = half_a * 4 + 2 * t + side_c
        code = jnp.where(block == 1, rows(ch_x, at), jnp.where(block == 2, rows(ch_y, at), rows(ch, at)))
        source = code // 8
        place = jnp.where(
            block == 1,
            jnp.where(source == 0, 1, jnp.where(source == 1, 0, 3)),
            jnp.where(block == 2, jnp.where(source == 0, 2, jnp.where(source == 1, 3, 0)), source),
        )
        codes.append((place, code % 8))

    def unpack(dense, odd):
        if odd:
            return jnp.where(left_c, roll(dense, -8), dense)
        return jnp.where(left_c, dense, roll(dense, 8))

    def assemble(n, copies, store):
        for copy in copies:
            copy.wait_recv()
        for a in range(8):
            from_x = unpack(pxr[n, a // 2], a % 2)
            from_y = unpack(pyr[n, a // 2], a % 2)
            one = jnp.broadcast_to(pd_r[n, a // 2, 0:1, :], (8, 128))
            two = jnp.broadcast_to(pd_r[n, a // 2, 1:2, :], (8, 128))
            from_d = unpack(jnp.where(block == 1, two, one), a % 2)
            for t in range(2):
                place, row = codes[t]
                value = jnp.where(place == 0, rows(zz[n, a], row), from_d)
                value = jnp.where(place == 1, rows(from_x, row), value)
                value = jnp.where(place == 2, rows(from_y, row), value)
                store(a, t, value)

    def store_q(a, t, value):
        eq[a, :, 128 * t : 128 * t + 128] = 0.25 * value

    coarse = [[None, None] for _ in range(8)]

    def store_0(a, t, value):
        coarse[a][t] = value

    def coarse_parts(e):
        other = sub + 1 - 2 * half_a
        below = [jnp.where(half_a == 1, rows(e[7][t], other), 0.0) for t in range(2)]
        above = [jnp.where(half_a == 0, rows(e[0][t], other), 0.0) for t in range(2)]
        layers = [below] + e + [above]
        return [parts(*layers[a : a + 3], (zero, zero), (zero, zero)) for a in range(8)]

    assemble(2, perm_copies, store_q)
    assemble(0, sol_copies, store_0)
    iterate = [[None, None] for _ in range(8)]
    pace = [[None, None] for _ in range(8)]
    for a, part in enumerate(coarse_parts(coarse)):
        for h, (x, flux, conduct) in enumerate(part):
            cols = slice(128 * h, 128 * h + 128)
            e0[a, :, cols] = x
            ef[a, :, cols] = REACTION * x + eq[a, :, cols] * flux
            pace[a][h] = DAMPING / (REACTION + eq[a, :, cols] * conduct)

    def store_f(a, t, value):
        cols = slice(128 * t, 128 * t + 128)
        ef[a, :, cols] = ef[a, :, cols] + value
        iterate[a][t] = coarse[a][t] + value * pace[a][t]

    assemble(1, res_copies, store_f)

    for repeat in range(COARSE - 1):
        after = []
        for a, part in enumerate(coarse_parts(iterate)):
            after.append([])
            for h, (x, flux, conduct) in enumerate(part):
                cols = slice(128 * h, 128 * h + 128)
                q = eq[a, :, cols]
                defect = ef[a, :, cols] - (REACTION * x + q * flux)
                after[a].append(x + defect * (DAMPING / (REACTION + q * conduct)))
        iterate = after

    parent_row = (pa // 8) * 2 + (pa % 8) // 4
    low_ob, low_oc = (pa // 2) % 2 == 0, pa % 2 == 0
    for a in range(8):
        one = rows(iterate[a][0] - e0[a, :, 0:128], parent_row)
        two = rows(iterate[a][1] - e0[a, :, 128:256], parent_row)
        value = jnp.where(low_ob, one, two)
        cor[a] = jnp.where(low_oc, value, roll(value, -8))
    spread = exact_dot(jnp.concatenate([cor[a] for a in range(8)], 0), upsample_m[...])
    for a in range(16):
        part = spread[8 * (a // 2) : 8 * (a // 2) + 8]
        va[a + 1] = vb[a + 1] + part

    copies2 = send_faces(2, va)
    own_faces(va, (va, vb))
    begin(va)
    take_faces(asked(2), (va, vb), copies2)

    def into_result(a, h, value):
        both_v[0:8, 256 * a + 128 * h : 256 * a + 128 * h + 128] = value

    smooth(INNER - 1)
    jacobi(va, fr, qr, whole, into_result, 16)

    for copy in (
        x_copies + msgs + [y_first, y_second] + copies0 + perm_copies + copies1 + sol_copies + res_copies + copies2
    ):
        copy.wait_send()


def body(*args):
    count = 30
    vmem = lambda *shape: pltpu.VMEM(shape, F32)
    any_space = pl.BlockSpec(memory_space=pl.ANY)
    both = pl.pallas_call(
        kernel,
        out_shape=pltpu.VMEM((16, 4096), F32),
        in_specs=[any_space] * 8,
        out_specs=pl.BlockSpec(memory_space=pltpu.VMEM),
        scratch_shapes=[
            vmem(3, 8, 4096), vmem(3, 8, 4096),
            pltpu.SMEM((8,), I32), pltpu.SMEM((8,), I32), pltpu.SMEM((8,), I32), pltpu.SMEM((8,), I32),
            pltpu.VMEM((8, 6), I32), vmem(16, 128), vmem(4, 16, 128),
            vmem(32, 2, 128), vmem(32, 2, 128), vmem(32, 4, 128), vmem(32, 4, 128),
            vmem(2, 18, 8, 256), vmem(16, 8, 256), vmem(16, 8, 256),
            vmem(16, 8, 128), vmem(16, 8, 256), vmem(16, 8, 128), vmem(16, 8, 256),
            vmem(6, 8, 256), vmem(4, 6, 8, 256), vmem(2, 4, 8, 256), vmem(2, 4, 8, 256),
            vmem(3, 4, 8, 128), vmem(3, 4, 8, 128), vmem(3, 4, 8, 128),
            vmem(3, 4, 2, 128), vmem(3, 4, 2, 128),
            vmem(16, 8, 256), vmem(16, 8, 256), vmem(8, 8, 256), vmem(8, 8, 256), vmem(8, 8, 256),
            vmem(8, 8, 128), vmem(3, 8, 8, 128),
            pltpu.VMEM((256, 128), BF16), pltpu.VMEM((128, 256), BF16),
            pltpu.SemaphoreType.REGULAR((4,)), pltpu.SemaphoreType.DMA((8,)), pltpu.SemaphoreType.DMA((count,)), pltpu.SemaphoreType.DMA((count,)),
        ],
        compiler_params=pltpu.CompilerParams(
            collective_id=0, has_side_effects=True, vmem_limit_bytes=32 * 1024 * 1024
        ),
    )(*[pltpu.with_memory_space_constraint(a, pltpu.HBM) for a in args])
    return both[:8], both[8:]


def solution(mesh):
    whole, flat = P(("gx", "gy"), None), P(("gx", "gy"))
    return jax.shard_map(
        body,
        mesh=mesh,
        in_specs=(whole, whole, whole, flat, flat, whole, flat, flat),
        out_specs=(whole, whole),
        check_vma=False,
    )
```

```python
import functools

import jax
import jax.numpy as jnp
from jax import lax
from jax.experimental import pallas as pl
from jax.experimental.pallas import tpu as pltpu
from jax.sharding import PartitionSpec as P

INNER = 3
COARSE = 4
REACTION = 0.25
DAMPING = 0.8
OPP = (1, 0, 3, 2)

F32 = jnp.float32
I32 = jnp.int32
BF16 = jnp.bfloat16

_ROWS = lax.GatherDimensionNumbers(
    offset_dims=(),
    collapsed_slice_dims=(0,),
    start_index_map=(0,),
    operand_batching_dims=(1,),
    start_indices_batching_dims=(1,),
)


def rows(x, index):
    return lax.gather(
        x, index[..., None], _ROWS, (1, 1), mode=lax.GatherScatterMode.PROMISE_IN_BOUNDS
    )


def roll(x, shift):
    return pltpu.roll(x, shift % 128, 1) if shift % 128 else x


def split3(x):
    high = x.astype(BF16)
    rest = x - high.astype(F32)
    mid = rest.astype(BF16)
    low = (rest - mid.astype(F32)).astype(BF16)
    return high, mid, low


def exact_dot(x, matrix):
    count = x.shape[0]
    out = jnp.dot(jnp.concatenate(split3(x), 0), matrix, preferred_element_type=F32)
    return out[:count] + (out[count : 2 * count] + out[2 * count :])


def pairwise(x):
    return ((x[0] + x[1]) + (x[2] + x[3])) + (x[4] + x[5])


def kernel(
    init_h, src_h, perm_h, mx_h, my_h, nb_h, ch_h, pa_h, both_v,
    own, px, t_mx, t_my, t_ch, t_pa, nbv, msg_s, msg_r, yi_s, yi_r, yf_s, yf_r,
    vv, fr, qr, sb, sc, gb, gc, every_s, every_r, gs, gr, ps, pxr, pyr, pd_s, pd_r,
    flux_v, squares_v, e0, ef, eq, cor, zz, restrict_m, upsample_m,
    ready, lsem, ssem, rsem,
):
    va, vb = vv.at[0], vv.at[1]
    i, j = lax.axis_index("gx"), lax.axis_index("gy")
    nx, ny = lax.axis_size("gx"), lax.axis_size("gy")
    xp = (i + 1 - 2 * (i % 2), j)
    yp = (i, j + 1 - 2 * (j % 2))
    diag = (xp[0], yp[1])
    beyond_x = ((i + nx - 1 + 2 * (i % 2)) % nx, j)
    beyond_y = (i, (j + ny - 1 + 2 * (j % 2)) % ny)
    around = (((i + nx - 1) % nx, j), ((i + 1) % nx, j), (i, (j + ny - 1) % ny), (i, (j + 1) % ny))

    tables = [
        pltpu.make_async_copy(a, b, lsem.at[n])
        for n, (a, b) in enumerate(
            ((mx_h, t_mx), (my_h, t_my), (ch_h, t_ch), (pa_h, t_pa), (nb_h, nbv))
        )
    ]
    for copy in tables:
        copy.start()
    fields = [
        pltpu.make_async_copy(a, own.at[n], lsem.at[5 + n])
        for n, a in enumerate((init_h, src_h, perm_h))
    ]
    for copy in fields:
        copy.start()

    even = (i + j) % 2 == 1
    odd = (i + j) % 2 == 0
    barrier = pltpu.get_barrier_semaphore()

    def signal(semaphore, peer):
        pl.semaphore_signal(semaphore, inc=1, device_id=peer, device_id_type=pl.DeviceIdType.MESH)

    @pl.when(even)
    def _():
        signal(barrier, beyond_x)
        signal(barrier, beyond_y)
        pl.semaphore_wait(barrier, 2)
        signal(ready.at[0], xp)
        signal(ready.at[1], yp)

    @pl.when(odd)
    def _():
        signal(barrier, xp)
        signal(barrier, yp)
        pl.semaphore_wait(ready.at[0], 1)

    used = [0]

    def push(source, target, peer):
        n = used[0]
        used[0] += 1
        return pltpu.make_async_remote_copy(
            src_ref=source,
            dst_ref=target,
            send_sem=ssem.at[n],
            recv_sem=rsem.at[n],
            device_id=peer,
            device_id_type=pl.DeviceIdType.MESH,
        )

    def push_around(sources, target):
        base = used[0]
        used[0] += 4
        return [
            pltpu.make_async_remote_copy(
                src_ref=sources(d),
                dst_ref=target(OPP[d]),
                send_sem=ssem.at[base + d],
                recv_sem=rsem.at[base + OPP[d]],
                device_id=around[d],
                device_id_type=pl.DeviceIdType.MESH,
            )
            for d in range(4)
        ]

    fields[0].wait()
    x_copies = [push(own.at[0], px.at[0], xp), push(own.at[1:3], px.at[1:3], xp)]
    x_copies[0].start()
    fields[1].wait()
    fields[2].wait()
    x_copies[1].start()

    lane = lax.broadcasted_iota(I32, (8, 128), 1)
    sub = lax.broadcasted_iota(I32, (8, 128), 0)
    zero = jnp.zeros((8, 128), F32)

    for copy in tables:
        copy.wait()

    def column(ref):
        out = jnp.full((8, 128), ref[0], I32)
        for k in range(1, 8):
            out = jnp.where(sub == k, ref[k], out)
        return out

    mx, my, ch, pa = column(t_mx), column(t_my), column(t_ch), column(t_pa)

    links = [jnp.broadcast_to(nbv[:, f : f + 1], (8, 128)) for f in range(6)]
    away = [jnp.where(c >= 0, c // 8, 7) for c in links]
    slot = [jnp.where(c >= 0, c % 8, 0) for c in links]
    named = sub == t_my[0]
    for k in range(1, 8):
        named = named | (sub == t_my[k])
    free = jnp.where(named, 8.0, sub.astype(F32))
    first = jnp.min(free, axis=0, keepdims=True)
    last = jnp.max(jnp.where(named, 0.0, sub.astype(F32)), axis=0, keepdims=True)
    leave = jnp.where(sub % 2 == 0, jnp.broadcast_to(first, (8, 128)), jnp.broadcast_to(last, (8, 128)))
    leave = jnp.minimum(leave, 7.0).astype(I32)
    leave_e = rows(mx, leave)
    leave_own, leave_row = leave_e < 8, leave_e % 8
    stay = my < 8
    final_e = rows(mx, my % 8)
    final_own, final_row = final_e < 8, final_e % 8
    order = jnp.zeros((8, 128), I32)
    for k in range(8):
        entry = t_my[k]
        order = order + jnp.where((entry >= 8) & (my > entry), 1, 0)
    final_first = order == 0

    def leaving(n, c):
        cols = pl.ds(128 * c, 128)
        return jnp.where(leave_own, rows(own[n, :, cols], leave_row), rows(px[n, :, cols], leave_row))

    x_copies[0].wait_recv()
    for c in range(32):
        yi_s[c] = leaving(0, c)[0:2]
    y_first = push(yi_s, yi_r, yp)

    @pl.when(odd)
    def _():
        pl.semaphore_wait(ready.at[1], 1)

    y_first.start()

    @pl.when(odd)
    def _():
        pl.semaphore_wait(barrier, 2)
        signal(ready.at[2], beyond_x)
        signal(ready.at[3], beyond_y)

    x_copies[1].wait_recv()
    for c in range(32):
        yf_s[c] = jnp.where(sub < 2, leaving(1, c), leaving(2, c))[0:4]
    y_second = push(yf_s, yf_r, yp)
    y_second.start()

    def arrived(n, ref, top, c):
        cols = pl.ds(128 * c, 128)
        kept = jnp.where(final_own, rows(own[n, :, cols], final_row), rows(px[n, :, cols], final_row))
        one = jnp.broadcast_to(ref[c, top : top + 1, :], (8, 128))
        two = jnp.broadcast_to(ref[c, top + 1 : top + 2, :], (8, 128))
        return jnp.where(stay, kept, jnp.where(final_first, one, two))

    low_b, high_b = lane < 16, lane >= 112
    low_c, high_c = lane % 16 == 0, lane % 16 == 15
    left_half, left_c = lane < 64, lane % 16 < 8
    group, inside = lane // 16, lane % 16
    row_b = jnp.where(left_half, slot[2], slot[3])
    here_b = jnp.where(left_half, away[2], away[3]) == 0
    row_c = jnp.where(left_c, slot[4], slot[5])
    here_c = jnp.where(left_c, away[4], away[5]) == 0
    sent = [(d >= 1) & (d <= 4) for d in away]
    sent_b = (low_b & sent[2], high_b & sent[3])
    sent_c = (low_c & sent[4]) | (high_c & sent[5])

    def pack_faces(v):
        packed = [[v[1, :, 0:128], v[1, :, 128:256]], [v[16, :, 0:128], v[16, :, 128:256]]]
        for _ in range(4):
            packed.append([zero, zero])
        for a in range(16):
            both = jnp.where(left_half, roll(v[a + 1, :, 128:256], 16), roll(v[a + 1, :, 0:128], -16))
            sb[a] = both
            moved = roll(both, 16 * (a % 8))
            packed[3][a // 8] = jnp.where(group == a % 8, moved, packed[3][a // 8])
            packed[2][a // 8] = jnp.where(group == (a + 7) % 8, moved, packed[2][a // 8])
            for h in range(2):
                half = v[a + 1, :, 128 * h : 128 * h + 128]
                both = jnp.where(left_c, roll(half, -15), roll(half, 15))
                sc[a, :, 128 * h : 128 * h + 128] = both
                m, k = (2 * a + h) % 16, (2 * a + h) // 16
                moved = roll(both, m)
                packed[5][k] = jnp.where(inside == m, moved, packed[5][k])
                packed[4][k] = jnp.where(inside == (m + 15) % 16, moved, packed[4][k])
        return packed

    def send_faces(g, v):
        packed = pack_faces(v)
        for d in range(4):
            face, row = give[d]
            for k in range(2):
                out = rows(packed[0][k], row)
                for f in range(1, 6):
                    out = jnp.where(face == f, rows(packed[f][k], row), out)
                gs[g - 1, d, :, 128 * k : 128 * k + 128] = out
        copies = push_around(lambda d: gs.at[g - 1, d], lambda d: gr.at[g - 1, d])
        for copy in copies:
            copy.start()
        return copies

    def own_faces(v, ends):
        for k in range(2):
            cols = slice(128 * k, 128 * k + 128)
            low = jnp.where(away[0] == 0, rows(v[16, :, cols], slot[0]), 0.0)
            high = jnp.where(away[1] == 0, rows(v[1, :, cols], slot[1]), 0.0)
            for end in ends:
                end[0, :, cols] = low
                end[17, :, cols] = high
        for a in range(16):
            gb[a] = jnp.where(here_b, rows(sb[a], row_b), 0.0)
            for h in range(2):
                cols = slice(128 * h, 128 * h + 128)
                gc[a, :, cols] = jnp.where(here_c, rows(sc[a, :, cols], row_c), 0.0)

    def take_faces(got, ends, copies):
        for copy in copies:
            copy.wait_recv()
        came = [[zero, zero] for _ in range(6)]
        for f in range(6):
            for k in range(2):
                for d in range(4):
                    came[f][k] = jnp.where(away[f] == d + 1, got(d, f, slice(128 * k, 128 * k + 128)), came[f][k])
        for k in range(2):
            cols = slice(128 * k, 128 * k + 128)
            low = jnp.where(away[0] == 0, ends[0][0, :, cols], came[0][k])
            high = jnp.where(away[1] == 0, ends[0][17, :, cols], came[1][k])
            for end in ends:
                end[0, :, cols] = low
                end[17, :, cols] = high
        for a in range(16):
            both = jnp.where(group == a % 8, came[2][a // 8], came[3][a // 8])
            gb[a] = jnp.where(here_b, gb[a], roll(both, -16 * (a % 8)))
            for h in range(2):
                cols = slice(128 * h, 128 * h + 128)
                m, k = (2 * a + h) % 16, (2 * a + h) // 16
                both = jnp.where(inside == m, came[4][k], came[5][k])
                gc[a, :, cols] = jnp.where(here_c, gc[a, :, cols], roll(both, -m))

    def halves(v, a):
        return [v[a, :, 0:128], v[a, :, 128:256]]

    def parts(before, x, after, ghost_b, ghost_c):
        down, up = [roll(y, 16) for y in x], [roll(y, -16) for y in x]
        beside_b = (
            (jnp.where(low_b, ghost_b[0], down[0]), jnp.where(high_b, up[1], up[0])),
            (jnp.where(low_b, down[0], down[1]), jnp.where(high_b, ghost_b[1], up[1])),
        )
        out = []
        for h in range(2):
            beside = beside_b[h] + (
                jnp.where(low_c, ghost_c[h], roll(x[h], 1)),
                jnp.where(high_c, ghost_c[h], roll(x[h], -1)),
                before[h],
                after[h],
            )
            mobility = 1.0 + x[h] * x[h]
            square = [w * w for w in beside]
            term = [(mobility + y) * (x[h] - w) for y, w in zip(square, beside)]
            squares = 6.0 * mobility + pairwise(square)
            flux = pairwise(term)
            out.append((x[h], flux, squares))
        return out

    def stencil(v, a, ghost_b, ghost_c):
        return parts(halves(v, a), halves(v, a + 1), halves(v, a + 2), ghost_b, ghost_c)

    def whole(v, a):
        return stencil(v, a, (gb[a], gb[a]), (gc[a, :, 0:128], gc[a, :, 128:256]))

    def begin(v):
        for a in range(16):
            x = halves(v, a + 1)
            ends = [halves(v, a), halves(v, a + 2)]
            if a == 0:
                ends[0] = [jnp.where(sent[0], x[h], ends[0][h]) for h in range(2)]
            if a == 15:
                ends[1] = [jnp.where(sent[1], x[h], ends[1][h]) for h in range(2)]
            ghost_b = [jnp.where(sent_b[h], x[h], gb[a]) for h in range(2)]
            ghost_c = [jnp.where(sent_c, x[h], gc[a, :, 128 * h : 128 * h + 128]) for h in range(2)]
            for h, (_, flux, squares) in enumerate(parts(ends[0], x, ends[1], ghost_b, ghost_c)):
                flux_v[a, :, 128 * h : 128 * h + 128] = flux
                squares_v[a, :, 128 * h : 128 * h + 128] = squares

    def complete(v, a):
        out = []
        for h, x in enumerate(halves(v, a + 1)):
            cols = slice(128 * h, 128 * h + 128)
            ghosts = [(sent_b[h], gb[a]), (sent_c, gc[a, :, cols])]
            if a == 0:
                ghosts.append((sent[0], v[0, :, cols]))
            if a == 15:
                ghosts.append((sent[1], v[17, :, cols]))
            own_square = x * x
            mobility = 1.0 + own_square
            flux, squares = flux_v[a, :, cols], squares_v[a, :, cols]
            for mask, ghost in ghosts:
                w = jnp.where(mask, ghost, x)
                square = w * w
                flux = flux + (mobility + square) * (x - w)
                squares = squares + (square - own_square)
            out.append((x, flux, squares))
        return out

    def jacobi(v, force, coefficient, sums, store, count):
        for a in range(count):
            for h, (x, flux, conduct) in enumerate(sums(v, a)):
                cols = slice(128 * h, 128 * h + 128)
                q = coefficient[a, :, cols]
                defect = force[a, :, cols] - (REACTION * x + q * flux)
                store(a, h, x + defect * (DAMPING / (REACTION + q * conduct)))

    def into(ref):
        def store(a, h, value):
            ref[a + 1, :, 128 * h : 128 * h + 128] = value

        return store

    def smooth(sweeps):
        for n in range(sweeps):
            jacobi(vv.at[n % 2], fr, qr, whole if n else complete, into(vv.at[(n + 1) % 2]), 16)

    def shrink(n, layer):
        fold = jnp.concatenate([layer(2 * a) + layer(2 * a + 1) for a in range(8)], 0)
        out = exact_dot(fold, restrict_m[...])
        for a in range(8):
            zz[n, a] = out[8 * a : 8 * a + 8]
        for m in range(4):
            dense = jnp.where(left_c, out[16 * m : 16 * m + 8], out[16 * m + 8 : 16 * m + 16])
            ps[n, m] = dense
            pd_s[n, m] = rows(dense, outward)[0:2]

    def send_pieces(which):
        copies = [
            push(ps.at[which], pxr.at[which], xp),
            push(ps.at[which], pyr.at[which], yp),
            push(pd_s.at[which], pd_r.at[which], diag),
        ]
        for copy in copies:
            copy.start()
        return copies

    slots = sub.astype(F32)
    to_x = jnp.sum(jnp.where(pa // 8 == 1, slots, 0.0), axis=0, keepdims=True)
    to_y = jnp.sum(jnp.where(pa // 8 == 2, slots, 0.0), axis=0, keepdims=True)
    outward = jnp.where(sub == 0, jnp.broadcast_to(to_x, (8, 128)), jnp.broadcast_to(to_y, (8, 128)))
    outward = outward.astype(I32)

    y_first.wait_recv()
    for c in range(32):
        va[1 + c // 2, :, 128 * (c % 2) : 128 * (c % 2) + 128] = arrived(0, yi_r, 0, c)
    packed = pack_faces(va)
    for f in range(6):
        for k in range(2):
            every_s[f, :, 128 * k : 128 * k + 128] = packed[f][k]

    @pl.when(even)
    def _():
        pl.semaphore_wait(ready.at[2], 1)
        pl.semaphore_wait(ready.at[3], 1)

    copies0 = push_around(lambda d: every_s, lambda d: every_r.at[d])
    for copy in copies0:
        copy.start()
    own_faces(va, (va, vb))
    begin(va)

    marks = jnp.concatenate([(lane == d).astype(F32) for d in away], 0)
    before = (
        lax.broadcasted_iota(I32, (48, 48), 1) < lax.broadcasted_iota(I32, (48, 48), 0)
    ).astype(F32)
    counts = jnp.dot(before, marks, preferred_element_type=F32)
    rank = []
    wanted = zero
    for f in range(6):
        mine = jnp.where(lane == away[f], counts[8 * f : 8 * f + 8], 0.0)
        place = jnp.broadcast_to(jnp.sum(mine, axis=1, keepdims=True), (8, 128)).astype(I32)
        place = jnp.minimum(place, 7)
        rank.append(place)
        remote = (away[f] >= 1) & (away[f] <= 4)
        hit = (lane == away[f] * 8 + place) & remote
        wanted = wanted + jnp.where(hit, ((f ^ 1) * 8 + slot[f]).astype(F32), 0.0)
    msg_s[0:8, :] = jnp.broadcast_to(jnp.sum(wanted, axis=0, keepdims=True), (8, 128))
    msg_s[8:16, :] = ch.astype(F32)

    msgs = push_around(lambda d: msg_s, lambda d: msg_r.at[d])
    for copy in msgs:
        copy.start()

    fine = lax.broadcasted_iota(I32, (256, 128), 0)
    small = lax.broadcasted_iota(I32, (256, 128), 1)
    same = (fine // 32 == small // 16) & ((fine % 16) // 2 == small % 8)
    restrict_m[...] = jnp.where(same, 0.125, 0.0).astype(BF16)
    fine = lax.broadcasted_iota(I32, (128, 256), 1)
    small = lax.broadcasted_iota(I32, (128, 256), 0)
    same = (fine // 32 == small // 16) & ((fine % 16) // 2 == small % 16)
    upsample_m[...] = jnp.where(same, 1.0, 0.0).astype(BF16)

    y_second.wait_recv()
    for c in range(32):
        cols = slice(128 * (c % 2), 128 * (c % 2) + 128)
        fr[c // 2, :, cols] = arrived(1, yf_r, 0, c)
        qr[c // 2, :, cols] = 0.5 * arrived(2, yf_r, 2, c)
    shrink(0, lambda a: qr[a])
    take_faces(lambda d, f, cols: rows(every_r[d, f ^ 1, :, cols], slot[f]), (va, vb), copies0)
    smooth(INNER)

    for copy in msgs:
        copy.wait_recv()
    give = []
    for d in range(4):
        code = jnp.where(lane == (OPP[d] + 1) * 8 + sub, msg_r[d, 0:8, :], 0.0)
        code = jnp.broadcast_to(jnp.sum(code, axis=1, keepdims=True), (8, 128)).astype(I32)
        give.append((code // 8, code % 8))
    ch_x = msg_r[1 - i % 2, 8:16, :].astype(I32)
    ch_y = msg_r[3 - j % 2, 8:16, :].astype(I32)

    def asked(g):
        return lambda d, f, cols: rows(gr[g - 1, d, :, cols], rank[f])

    copies1 = send_faces(1, vb)
    own_faces(vb, (vb,))
    begin(vb)
    shrink(1, lambda a: vb[a + 1])
    sol_copies = send_pieces(pl.ds(0, 2))
    take_faces(asked(1), (vb,), copies1)

    layers = []
    for a in range(16):
        layers.append([])
        for h, (x, flux, _) in enumerate(complete(vb, a)):
            cols = slice(128 * h, 128 * h + 128)
            value = fr[a, :, cols] - (REACTION * x + qr[a, :, cols] * flux)
            both_v[8:16, 256 * a + 128 * h : 256 * a + 128 * h + 128] = value
            layers[a].append(value)
    shrink(2, lambda a: jnp.concatenate(layers[a], 1))
    res_copies = send_pieces(2)

    block, half_a = sub // 2, sub % 2
    side_c = (lane // 8) % 2
    codes = []
    for t in range(2):
        at = half_a * 4 + 2 * t + side_c
        code = jnp.where(block == 1, rows(ch_x, at), jnp.where(block == 2, rows(ch_y, at), rows(ch, at)))
        source = code // 8
        place = jnp.where(
            block == 1,
            jnp.where(source == 0, 1, jnp.where(source == 1, 0, 3)),
            jnp.where(block == 2, jnp.where(source == 0, 2, jnp.where(source == 1, 3, 0)), source),
        )
        codes.append((place, code % 8))

    def unpack(dense, odd):
        if odd:
            return jnp.where(left_c, roll(dense, -8), dense)
        return jnp.where(left_c, dense, roll(dense, 8))

    def assemble(n, copies, store):
        for copy in copies:
            copy.wait_recv()
        for a in range(8):
            from_x = unpack(pxr[n, a // 2], a % 2)
            from_y = unpack(pyr[n, a // 2], a % 2)
            one = jnp.broadcast_to(pd_r[n, a // 2, 0:1, :], (8, 128))
            two = jnp.broadcast_to(pd_r[n, a // 2, 1:2, :], (8, 128))
            from_d = unpack(jnp.where(block == 1, two, one), a % 2)
            for t in range(2):
                place, row = codes[t]
                value = jnp.where(place == 0, rows(zz[n, a], row), from_d)
                value = jnp.where(place == 1, rows(from_x, row), value)
                value = jnp.where(place == 2, rows(from_y, row), value)
                store(a, t, value)

    def store_q(a, t, value):
        eq[a, :, 128 * t : 128 * t + 128] = 0.25 * value

    coarse = [[None, None] for _ in range(8)]

    def store_0(a, t, value):
        coarse[a][t] = value

    def coarse_parts(e):
        other = sub + 1 - 2 * half_a
        below = [jnp.where(half_a == 1, rows(e[7][t], other), 0.0) for t in range(2)]
        above = [jnp.where(half_a == 0, rows(e[0][t], other), 0.0) for t in range(2)]
        layers = [below] + e + [above]
        return [parts(*layers[a : a + 3], (zero, zero), (zero, zero)) for a in range(8)]

    assemble(0, sol_copies, store_q)
    assemble(1, [], store_0)
    iterate = [[None, None] for _ in range(8)]
    pace = [[None, None] for _ in range(8)]
    for a, part in enumerate(coarse_parts(coarse)):
        for h, (x, flux, conduct) in enumerate(part):
            cols = slice(128 * h, 128 * h + 128)
            e0[a, :, cols] = x
            ef[a, :, cols] = REACTION * x + eq[a, :, cols] * flux
            pace[a][h] = DAMPING / (REACTION + eq[a, :, cols] * conduct)

    def store_f(a, t, value):
        cols = slice(128 * t, 128 * t + 128)
        ef[a, :, cols] = ef[a, :, cols] + value
        iterate[a][t] = coarse[a][t] + value * pace[a][t]

    assemble(2, res_copies, store_f)

    for repeat in range(COARSE - 1):
        after = []
        for a, part in enumerate(coarse_parts(iterate)):
            after.append([])
            for h, (x, flux, conduct) in enumerate(part):
                cols = slice(128 * h, 128 * h + 128)
                q = eq[a, :, cols]
                defect = ef[a, :, cols] - (REACTION * x + q * flux)
                after[a].append(x + defect * (DAMPING / (REACTION + q * conduct)))
        iterate = after

    parent_row = (pa // 8) * 2 + (pa % 8) // 4
    low_ob, low_oc = (pa // 2) % 2 == 0, pa % 2 == 0
    for a in range(8):
        one = rows(iterate[a][0] - e0[a, :, 0:128], parent_row)
        two = rows(iterate[a][1] - e0[a, :, 128:256], parent_row)
        value = jnp.where(low_ob, one, two)
        cor[a] = jnp.where(low_oc, value, roll(value, -8))
    spread = exact_dot(jnp.concatenate([cor[a] for a in range(8)], 0), upsample_m[...])
    for a in range(16):
        part = spread[8 * (a // 2) : 8 * (a // 2) + 8]
        va[a + 1] = vb[a + 1] + part

    copies2 = send_faces(2, va)
    own_faces(va, (va, vb))
    begin(va)
    take_faces(asked(2), (va, vb), copies2)

    def into_result(a, h, value):
        both_v[0:8, 256 * a + 128 * h : 256 * a + 128 * h + 128] = value

    smooth(INNER - 1)
    jacobi(va, fr, qr, whole, into_result, 16)

    for copy in (
        x_copies + msgs + [y_first, y_second] + copies0 + copies1 + sol_copies + res_copies + copies2
    ):
        copy.wait_send()


def body(*args):
    count = 30
    vmem = lambda *shape: pltpu.VMEM(shape, F32)
    any_space = pl.BlockSpec(memory_space=pl.ANY)
    both = pl.pallas_call(
        kernel,
        out_shape=pltpu.VMEM((16, 4096), F32),
        in_specs=[any_space] * 8,
        out_specs=pl.BlockSpec(memory_space=pltpu.VMEM),
        scratch_shapes=[
            vmem(3, 8, 4096), vmem(3, 8, 4096),
            pltpu.SMEM((8,), I32), pltpu.SMEM((8,), I32), pltpu.SMEM((8,), I32), pltpu.SMEM((8,), I32),
            pltpu.VMEM((8, 6), I32), vmem(16, 128), vmem(4, 16, 128),
            vmem(32, 2, 128), vmem(32, 2, 128), vmem(32, 4, 128), vmem(32, 4, 128),
            vmem(2, 18, 8, 256), vmem(16, 8, 256), vmem(16, 8, 256),
            vmem(16, 8, 128), vmem(16, 8, 256), vmem(16, 8, 128), vmem(16, 8, 256),
            vmem(6, 8, 256), vmem(4, 6, 8, 256), vmem(2, 4, 8, 256), vmem(2, 4, 8, 256),
            vmem(3, 4, 8, 128), vmem(3, 4, 8, 128), vmem(3, 4, 8, 128),
            vmem(3, 4, 2, 128), vmem(3, 4, 2, 128),
            vmem(16, 8, 256), vmem(16, 8, 256), vmem(8, 8, 256), vmem(8, 8, 256), vmem(8, 8, 256),
            vmem(8, 8, 128), vmem(3, 8, 8, 128),
            pltpu.VMEM((256, 128), BF16), pltpu.VMEM((128, 256), BF16),
            pltpu.SemaphoreType.REGULAR((4,)), pltpu.SemaphoreType.DMA((8,)), pltpu.SemaphoreType.DMA((count,)), pltpu.SemaphoreType.DMA((count,)),
        ],
        compiler_params=pltpu.CompilerParams(
            collective_id=0, has_side_effects=True, vmem_limit_bytes=32 * 1024 * 1024
        ),
    )(*[pltpu.with_memory_space_constraint(a, pltpu.HBM) for a in args])
    return both[:8], both[8:]


def solution(mesh):
    whole, flat = P(("gx", "gy"), None), P(("gx", "gy"))
    return jax.shard_map(
        body,
        mesh=mesh,
        in_specs=(whole, whole, whole, flat, flat, whole, flat, flat),
        out_specs=(whole, whole),
        check_vma=False,
    )
```

```python
import functools

import jax
import jax.numpy as jnp
from jax import lax
from jax.experimental import pallas as pl
from jax.experimental.pallas import tpu as pltpu
from jax.sharding import PartitionSpec as P

INNER = 3
COARSE = 4
REACTION = 0.25
DAMPING = 0.8
OPP = (1, 0, 3, 2)

F32 = jnp.float32
I32 = jnp.int32
BF16 = jnp.bfloat16

_ROWS = lax.GatherDimensionNumbers(
    offset_dims=(),
    collapsed_slice_dims=(0,),
    start_index_map=(0,),
    operand_batching_dims=(1,),
    start_indices_batching_dims=(1,),
)


def rows(x, index):
    return lax.gather(
        x, index[..., None], _ROWS, (1, 1), mode=lax.GatherScatterMode.PROMISE_IN_BOUNDS
    )


def roll(x, shift):
    return pltpu.roll(x, shift % 128, 1) if shift % 128 else x


def split3(x):
    high = x.astype(BF16)
    rest = x - high.astype(F32)
    mid = rest.astype(BF16)
    low = (rest - mid.astype(F32)).astype(BF16)
    return high, mid, low


def exact_dot(x, matrix):
    count = x.shape[0]
    out = jnp.dot(jnp.concatenate(split3(x), 0), matrix, preferred_element_type=F32)
    return out[:count] + (out[count : 2 * count] + out[2 * count :])


def pairwise(x):
    return ((x[0] + x[1]) + (x[2] + x[3])) + (x[4] + x[5])


def kernel(
    init_h, src_h, perm_h, mx_h, my_h, nb_h, ch_h, pa_h, both_v,
    own, px, t_mx, t_my, t_ch, t_pa, nbv, msg_s, msg_r, yi_s, yi_r, yf_s, yf_r,
    vv, fr, qr, sb, sc, gb, gc, every_s, every_r, gs, gr, ps, pxr, pyr, pd_s, pd_r,
    flux_v, squares_v, e0, ef, eq, cor, zz, restrict_m, upsample_m,
    ready, lsem, ssem, rsem,
):
    va, vb = vv.at[0], vv.at[1]
    i, j = lax.axis_index("gx"), lax.axis_index("gy")
    nx, ny = lax.axis_size("gx"), lax.axis_size("gy")
    xp = (i + 1 - 2 * (i % 2), j)
    yp = (i, j + 1 - 2 * (j % 2))
    diag = (xp[0], yp[1])
    beyond_x = ((i + nx - 1 + 2 * (i % 2)) % nx, j)
    beyond_y = (i, (j + ny - 1 + 2 * (j % 2)) % ny)
    around = (((i + nx - 1) % nx, j), ((i + 1) % nx, j), (i, (j + ny - 1) % ny), (i, (j + 1) % ny))

    tables = [
        pltpu.make_async_copy(a, b, lsem.at[n])
        for n, (a, b) in enumerate(
            ((mx_h, t_mx), (my_h, t_my), (ch_h, t_ch), (pa_h, t_pa), (nb_h, nbv))
        )
    ]
    for copy in tables:
        copy.start()
    fields = [
        pltpu.make_async_copy(a, own.at[n], lsem.at[5 + n])
        for n, a in enumerate((init_h, src_h, perm_h))
    ]
    for copy in fields:
        copy.start()

    even = (i + j) % 2 == 1
    odd = (i + j) % 2 == 0
    barrier = pltpu.get_barrier_semaphore()

    def signal(semaphore, peer):
        pl.semaphore_signal(semaphore, inc=1, device_id=peer, device_id_type=pl.DeviceIdType.MESH)

    @pl.when(even)
    def _():
        signal(barrier, beyond_x)
        signal(barrier, beyond_y)
        pl.semaphore_wait(barrier, 2)
        signal(ready.at[0], xp)
        signal(ready.at[1], yp)

    @pl.when(odd)
    def _():
        signal(barrier, xp)
        signal(barrier, yp)
        pl.semaphore_wait(ready.at[0], 1)

    used = [0]

    def push(source, target, peer):
        n = used[0]
        used[0] += 1
        return pltpu.make_async_remote_copy(
            src_ref=source,
            dst_ref=target,
            send_sem=ssem.at[n],
            recv_sem=rsem.at[n],
            device_id=peer,
            device_id_type=pl.DeviceIdType.MESH,
        )

    def push_around(sources, target):
        base = used[0]
        used[0] += 4
        return [
            pltpu.make_async_remote_copy(
                src_ref=sources(d),
                dst_ref=target(OPP[d]),
                send_sem=ssem.at[base + d],
                recv_sem=rsem.at[base + OPP[d]],
                device_id=around[d],
                device_id_type=pl.DeviceIdType.MESH,
            )
            for d in range(4)
        ]

    fields[0].wait()
    x_copies = [push(own.at[0], px.at[0], xp), push(own.at[1:3], px.at[1:3], xp)]
    x_copies[0].start()
    fields[1].wait()
    fields[2].wait()
    x_copies[1].start()

    lane = lax.broadcasted_iota(I32, (8, 128), 1)
    sub = lax.broadcasted_iota(I32, (8, 128), 0)
    zero = jnp.zeros((8, 128), F32)

    for copy in tables:
        copy.wait()

    def column(ref):
        out = jnp.full((8, 128), ref[0], I32)
        for k in range(1, 8):
            out = jnp.where(sub == k, ref[k], out)
        return out

    mx, my, ch, pa = column(t_mx), column(t_my), column(t_ch), column(t_pa)

    links = [jnp.broadcast_to(nbv[:, f : f + 1], (8, 128)) for f in range(6)]
    away = [jnp.where(c >= 0, c // 8, 7) for c in links]
    slot = [jnp.where(c >= 0, c % 8, 0) for c in links]
    named = sub == t_my[0]
    for k in range(1, 8):
        named = named | (sub == t_my[k])
    free = jnp.where(named, 8.0, sub.astype(F32))
    first = jnp.min(free, axis=0, keepdims=True)
    last = jnp.max(jnp.where(named, 0.0, sub.astype(F32)), axis=0, keepdims=True)
    leave = jnp.where(sub % 2 == 0, jnp.broadcast_to(first, (8, 128)), jnp.broadcast_to(last, (8, 128)))
    leave = jnp.minimum(leave, 7.0).astype(I32)
    leave_e = rows(mx, leave)
    leave_own, leave_row = leave_e < 8, leave_e % 8
    stay = my < 8
    final_e = rows(mx, my % 8)
    final_own, final_row = final_e < 8, final_e % 8
    order = jnp.zeros((8, 128), I32)
    for k in range(8):
        entry = t_my[k]
        order = order + jnp.where((entry >= 8) & (my > entry), 1, 0)
    final_first = order == 0

    def leaving(n, c):
        cols = pl.ds(128 * c, 128)
        return jnp.where(leave_own, rows(own[n, :, cols], leave_row), rows(px[n, :, cols], leave_row))

    x_copies[0].wait_recv()
    for c in range(32):
        yi_s[c] = leaving(0, c)[0:2]
    y_first = push(yi_s, yi_r, yp)

    @pl.when(odd)
    def _():
        pl.semaphore_wait(ready.at[1], 1)

    y_first.start()

    @pl.when(odd)
    def _():
        pl.semaphore_wait(barrier, 2)
        signal(ready.at[2], beyond_x)
        signal(ready.at[3], beyond_y)

    x_copies[1].wait_recv()
    for c in range(32):
        yf_s[c] = jnp.where(sub < 2, leaving(1, c), leaving(2, c))[0:4]
    y_second = push(yf_s, yf_r, yp)
    y_second.start()

    def arrived(n, ref, top, c):
        cols = pl.ds(128 * c, 128)
        kept = jnp.where(final_own, rows(own[n, :, cols], final_row), rows(px[n, :, cols], final_row))
        one = jnp.broadcast_to(ref[c, top : top + 1, :], (8, 128))
        two = jnp.broadcast_to(ref[c, top + 1 : top + 2, :], (8, 128))
        return jnp.where(stay, kept, jnp.where(final_first, one, two))

    low_b, high_b = lane < 16, lane >= 112
    low_c, high_c = lane % 16 == 0, lane % 16 == 15
    left_half, left_c = lane < 64, lane % 16 < 8
    group, inside = lane // 16, lane % 16
    row_b = jnp.where(left_half, slot[2], slot[3])
    here_b = jnp.where(left_half, away[2], away[3]) == 0
    row_c = jnp.where(left_c, slot[4], slot[5])
    here_c = jnp.where(left_c, away[4], away[5]) == 0
    sent = [(d >= 1) & (d <= 4) for d in away]
    sent_b = (low_b & sent[2], high_b & sent[3])
    sent_c = (low_c & sent[4]) | (high_c & sent[5])

    def pack_faces(v):
        packed = [[v[1, :, 0:128], v[1, :, 128:256]], [v[16, :, 0:128], v[16, :, 128:256]]]
        for _ in range(4):
            packed.append([zero, zero])
        for a in range(16):
            both = jnp.where(left_half, roll(v[a + 1, :, 128:256], 16), roll(v[a + 1, :, 0:128], -16))
            sb[a] = both
            moved = roll(both, 16 * (a % 8))
            packed[3][a // 8] = jnp.where(group == a % 8, moved, packed[3][a // 8])
            packed[2][a // 8] = jnp.where(group == (a + 7) % 8, moved, packed[2][a // 8])
            for h in range(2):
                half = v[a + 1, :, 128 * h : 128 * h + 128]
                both = jnp.where(left_c, roll(half, -15), roll(half, 15))
                sc[a, :, 128 * h : 128 * h + 128] = both
                m, k = (2 * a + h) % 16, (2 * a + h) // 16
                moved = roll(both, m)
                packed[5][k] = jnp.where(inside == m, moved, packed[5][k])
                packed[4][k] = jnp.where(inside == (m + 15) % 16, moved, packed[4][k])
        return packed

    def send_faces(g, v):
        packed = pack_faces(v)
        for d in range(4):
            face, row = give[d]
            for k in range(2):
                out = rows(packed[0][k], row)
                for f in range(1, 6):
                    out = jnp.where(face == f, rows(packed[f][k], row), out)
                gs[g - 1, d, :, 128 * k : 128 * k + 128] = out
        copies = push_around(lambda d: gs.at[g - 1, d], lambda d: gr.at[g - 1, d])
        for copy in copies:
            copy.start()
        return copies

    def own_faces(v, ends):
        for k in range(2):
            cols = slice(128 * k, 128 * k + 128)
            low = jnp.where(away[0] == 0, rows(v[16, :, cols], slot[0]), 0.0)
            high = jnp.where(away[1] == 0, rows(v[1, :, cols], slot[1]), 0.0)
            for end in ends:
                end[0, :, cols] = low
                end[17, :, cols] = high
        for a in range(16):
            gb[a] = jnp.where(here_b, rows(sb[a], row_b), 0.0)
            for h in range(2):
                cols = slice(128 * h, 128 * h + 128)
                gc[a, :, cols] = jnp.where(here_c, rows(sc[a, :, cols], row_c), 0.0)

    def take_faces(got, ends, copies):
        for copy in copies:
            copy.wait_recv()
        came = [[zero, zero] for _ in range(6)]
        for f in range(6):
            for k in range(2):
                for d in range(4):
                    came[f][k] = jnp.where(away[f] == d + 1, got(d, f, slice(128 * k, 128 * k + 128)), came[f][k])
        for k in range(2):
            cols = slice(128 * k, 128 * k + 128)
            low = jnp.where(away[0] == 0, ends[0][0, :, cols], came[0][k])
            high = jnp.where(away[1] == 0, ends[0][17, :, cols], came[1][k])
            for end in ends:
                end[0, :, cols] = low
                end[17, :, cols] = high
        for a in range(16):
            both = jnp.where(group == a % 8, came[2][a // 8], came[3][a // 8])
            gb[a] = jnp.where(here_b, gb[a], roll(both, -16 * (a % 8)))
            for h in range(2):
                cols = slice(128 * h, 128 * h + 128)
                m, k = (2 * a + h) % 16, (2 * a + h) // 16
                both = jnp.where(inside == m, came[4][k], came[5][k])
                gc[a, :, cols] = jnp.where(here_c, gc[a, :, cols], roll(both, -m))

    def halves(v, a):
        return [v[a, :, 0:128], v[a, :, 128:256]]

    def parts(before, x, after, ghost_b, ghost_c, shared=None):
        down, up = [roll(y, 16) for y in x], [roll(y, -16) for y in x]
        beside_b = (
            (jnp.where(low_b, ghost_b[0], down[0]), jnp.where(high_b, up[1], up[0])),
            (jnp.where(low_b, down[0], down[1]), jnp.where(high_b, ghost_b[1], up[1])),
        )
        out = []
        for h in range(2):
            beside = beside_b[h] + (
                jnp.where(low_c, ghost_c[h], roll(x[h], 1)),
                jnp.where(high_c, ghost_c[h], roll(x[h], -1)),
                before[h],
                after[h],
            )
            last = shared.get(h) if shared is not None else None
            own_square = last[1] if last else x[h] * x[h]
            mobility = 1.0 + own_square
            square = [w * w for w in beside[:4]] + [last[2] if last else before[h] * before[h], after[h] * after[h]]
            term = [(mobility + y) * (x[h] - w) for y, w in zip(square[:4], beside)]
            above = (mobility + square[5]) * (x[h] - after[h])
            ends = above - last[0] if last else above + (mobility + square[4]) * (x[h] - before[h])
            if shared is not None:
                shared[h] = (above, square[5], own_square)
            squares = 6.0 * mobility + pairwise(square)
            flux = ((term[0] + term[1]) + (term[2] + term[3])) + ends
            out.append((x[h], flux, squares))
        return out

    def stencil(v, a, ghost_b, ghost_c, shared):
        return parts(halves(v, a), halves(v, a + 1), halves(v, a + 2), ghost_b, ghost_c, shared)

    edges = {}

    def whole(v, a):
        if a == 0:
            edges.clear()
        return stencil(v, a, (gb[a], gb[a]), (gc[a, :, 0:128], gc[a, :, 128:256]), edges)

    def begin(v):
        for a in range(16):
            x = halves(v, a + 1)
            ends = [halves(v, a), halves(v, a + 2)]
            if a == 0:
                ends[0] = [jnp.where(sent[0], x[h], ends[0][h]) for h in range(2)]
            if a == 15:
                ends[1] = [jnp.where(sent[1], x[h], ends[1][h]) for h in range(2)]
            ghost_b = [jnp.where(sent_b[h], x[h], gb[a]) for h in range(2)]
            ghost_c = [jnp.where(sent_c, x[h], gc[a, :, 128 * h : 128 * h + 128]) for h in range(2)]
            for h, (_, flux, squares) in enumerate(parts(ends[0], x, ends[1], ghost_b, ghost_c)):
                flux_v[a, :, 128 * h : 128 * h + 128] = flux
                squares_v[a, :, 128 * h : 128 * h + 128] = squares

    def complete(v, a):
        out = []
        for h, x in enumerate(halves(v, a + 1)):
            cols = slice(128 * h, 128 * h + 128)
            ghosts = [(sent_b[h], gb[a]), (sent_c, gc[a, :, cols])]
            if a == 0:
                ghosts.append((sent[0], v[0, :, cols]))
            if a == 15:
                ghosts.append((sent[1], v[17, :, cols]))
            own_square = x * x
            mobility = 1.0 + own_square
            flux, squares = flux_v[a, :, cols], squares_v[a, :, cols]
            for mask, ghost in ghosts:
                w = jnp.where(mask, ghost, x)
                square = w * w
                flux = flux + (mobility + square) * (x - w)
                squares = squares + (square - own_square)
            out.append((x, flux, squares))
        return out

    def jacobi(v, force, coefficient, sums, store, count):
        for a in range(count):
            for h, (x, flux, conduct) in enumerate(sums(v, a)):
                cols = slice(128 * h, 128 * h + 128)
                q = coefficient[a, :, cols]
                defect = force[a, :, cols] - (REACTION * x + q * flux)
                store(a, h, x + defect * (DAMPING / (REACTION + q * conduct)))

    def into(ref):
        def store(a, h, value):
            ref[a + 1, :, 128 * h : 128 * h + 128] = value

        return store

    def smooth(sweeps):
        for n in range(sweeps):
            jacobi(vv.at[n % 2], fr, qr, whole if n else complete, into(vv.at[(n + 1) % 2]), 16)

    def shrink(n, layer):
        fold = jnp.concatenate([layer(2 * a) + layer(2 * a + 1) for a in range(8)], 0)
        out = exact_dot(fold, restrict_m[...])
        for a in range(8):
            zz[n, a] = out[8 * a : 8 * a + 8]
        for m in range(4):
            dense = jnp.where(left_c, out[16 * m : 16 * m + 8], out[16 * m + 8 : 16 * m + 16])
            ps[n, m] = dense
            pd_s[n, m] = rows(dense, outward)[0:2]

    def send_pieces(which):
        copies = [
            push(ps.at[which], pxr.at[which], xp),
            push(ps.at[which], pyr.at[which], yp),
            push(pd_s.at[which], pd_r.at[which], diag),
        ]
        for copy in copies:
            copy.start()
        return copies

    slots = sub.astype(F32)
    to_x = jnp.sum(jnp.where(pa // 8 == 1, slots, 0.0), axis=0, keepdims=True)
    to_y = jnp.sum(jnp.where(pa // 8 == 2, slots, 0.0), axis=0, keepdims=True)
    outward = jnp.where(sub == 0, jnp.broadcast_to(to_x, (8, 128)), jnp.broadcast_to(to_y, (8, 128)))
    outward = outward.astype(I32)

    y_first.wait_recv()
    for c in range(32):
        va[1 + c // 2, :, 128 * (c % 2) : 128 * (c % 2) + 128] = arrived(0, yi_r, 0, c)
    packed = pack_faces(va)
    for f in range(6):
        for k in range(2):
            every_s[f, :, 128 * k : 128 * k + 128] = packed[f][k]

    @pl.when(even)
    def _():
        pl.semaphore_wait(ready.at[2], 1)
        pl.semaphore_wait(ready.at[3], 1)

    copies0 = push_around(lambda d: every_s, lambda d: every_r.at[d])
    for copy in copies0:
        copy.start()
    own_faces(va, (va, vb))
    begin(va)

    marks = jnp.concatenate([(lane == d).astype(F32) for d in away], 0)
    before = (
        lax.broadcasted_iota(I32, (48, 48), 1) < lax.broadcasted_iota(I32, (48, 48), 0)
    ).astype(F32)
    counts = jnp.dot(before, marks, preferred_element_type=F32)
    rank = []
    wanted = zero
    for f in range(6):
        mine = jnp.where(lane == away[f], counts[8 * f : 8 * f + 8], 0.0)
        place = jnp.broadcast_to(jnp.sum(mine, axis=1, keepdims=True), (8, 128)).astype(I32)
        place = jnp.minimum(place, 7)
        rank.append(place)
        remote = (away[f] >= 1) & (away[f] <= 4)
        hit = (lane == away[f] * 8 + place) & remote
        wanted = wanted + jnp.where(hit, ((f ^ 1) * 8 + slot[f]).astype(F32), 0.0)
    msg_s[0:8, :] = jnp.broadcast_to(jnp.sum(wanted, axis=0, keepdims=True), (8, 128))
    msg_s[8:16, :] = ch.astype(F32)

    msgs = push_around(lambda d: msg_s, lambda d: msg_r.at[d])
    for copy in msgs:
        copy.start()

    fine = lax.broadcasted_iota(I32, (256, 128), 0)
    small = lax.broadcasted_iota(I32, (256, 128), 1)
    same = (fine // 32 == small // 16) & ((fine % 16) // 2 == small % 8)
    restrict_m[...] = jnp.where(same, 0.125, 0.0).astype(BF16)
    fine = lax.broadcasted_iota(I32, (128, 256), 1)
    small = lax.broadcasted_iota(I32, (128, 256), 0)
    same = (fine // 32 == small // 16) & ((fine % 16) // 2 == small % 16)
    upsample_m[...] = jnp.where(same, 1.0, 0.0).astype(BF16)

    y_second.wait_recv()
    for c in range(32):
        cols = slice(128 * (c % 2), 128 * (c % 2) + 128)
        fr[c // 2, :, cols] = arrived(1, yf_r, 0, c)
        qr[c // 2, :, cols] = 0.5 * arrived(2, yf_r, 2, c)
    shrink(0, lambda a: qr[a])
    take_faces(lambda d, f, cols: rows(every_r[d, f ^ 1, :, cols], slot[f]), (va, vb), copies0)
    smooth(INNER)

    for copy in msgs:
        copy.wait_recv()
    give = []
    for d in range(4):
        code = jnp.where(lane == (OPP[d] + 1) * 8 + sub, msg_r[d, 0:8, :], 0.0)
        code = jnp.broadcast_to(jnp.sum(code, axis=1, keepdims=True), (8, 128)).astype(I32)
        give.append((code // 8, code % 8))
    ch_x = msg_r[1 - i % 2, 8:16, :].astype(I32)
    ch_y = msg_r[3 - j % 2, 8:16, :].astype(I32)

    def asked(g):
        return lambda d, f, cols: rows(gr[g - 1, d, :, cols], rank[f])

    copies1 = send_faces(1, vb)
    own_faces(vb, (vb,))
    begin(vb)
    shrink(1, lambda a: vb[a + 1])
    sol_copies = send_pieces(pl.ds(0, 2))
    take_faces(asked(1), (vb,), copies1)

    layers = []
    for a in range(16):
        layers.append([])
        for h, (x, flux, _) in enumerate(complete(vb, a)):
            cols = slice(128 * h, 128 * h + 128)
            value = fr[a, :, cols] - (REACTION * x + qr[a, :, cols] * flux)
            both_v[8:16, 256 * a + 128 * h : 256 * a + 128 * h + 128] = value
            layers[a].append(value)
    shrink(2, lambda a: jnp.concatenate(layers[a], 1))
    res_copies = send_pieces(2)

    block, half_a = sub // 2, sub % 2
    side_c = (lane // 8) % 2
    codes = []
    for t in range(2):
        at = half_a * 4 + 2 * t + side_c
        code = jnp.where(block == 1, rows(ch_x, at), jnp.where(block == 2, rows(ch_y, at), rows(ch, at)))
        source = code // 8
        place = jnp.where(
            block == 1,
            jnp.where(source == 0, 1, jnp.where(source == 1, 0, 3)),
            jnp.where(block == 2, jnp.where(source == 0, 2, jnp.where(source == 1, 3, 0)), source),
        )
        codes.append((place, code % 8))

    def unpack(dense, odd):
        if odd:
            return jnp.where(left_c, roll(dense, -8), dense)
        return jnp.where(left_c, dense, roll(dense, 8))

    def assemble(n, copies, store):
        for copy in copies:
            copy.wait_recv()
        for a in range(8):
            from_x = unpack(pxr[n, a // 2], a % 2)
            from_y = unpack(pyr[n, a // 2], a % 2)
            one = jnp.broadcast_to(pd_r[n, a // 2, 0:1, :], (8, 128))
            two = jnp.broadcast_to(pd_r[n, a // 2, 1:2, :], (8, 128))
            from_d = unpack(jnp.where(block == 1, two, one), a % 2)
            for t in range(2):
                place, row = codes[t]
                value = jnp.where(place == 0, rows(zz[n, a], row), from_d)
                value = jnp.where(place == 1, rows(from_x, row), value)
                value = jnp.where(place == 2, rows(from_y, row), value)
                store(a, t, value)

    def store_q(a, t, value):
        eq[a, :, 128 * t : 128 * t + 128] = 0.25 * value

    coarse = [[None, None] for _ in range(8)]

    def store_0(a, t, value):
        coarse[a][t] = value

    def coarse_parts(e):
        other = sub + 1 - 2 * half_a
        below = [jnp.where(half_a == 1, rows(e[7][t], other), 0.0) for t in range(2)]
        above = [jnp.where(half_a == 0, rows(e[0][t], other), 0.0) for t in range(2)]
        layers = [below] + e + [above]
        shared = {}
        return [parts(*layers[a : a + 3], (zero, zero), (zero, zero), shared) for a in range(8)]

    assemble(0, sol_copies, store_q)
    assemble(1, [], store_0)
    iterate = [[None, None] for _ in range(8)]
    pace = [[None, None] for _ in range(8)]
    for a, part in enumerate(coarse_parts(coarse)):
        for h, (x, flux, conduct) in enumerate(part):
            cols = slice(128 * h, 128 * h + 128)
            e0[a, :, cols] = x
            ef[a, :, cols] = REACTION * x + eq[a, :, cols] * flux
            pace[a][h] = DAMPING / (REACTION + eq[a, :, cols] * conduct)

    def store_f(a, t, value):
        cols = slice(128 * t, 128 * t + 128)
        ef[a, :, cols] = ef[a, :, cols] + value
        iterate[a][t] = coarse[a][t] + value * pace[a][t]

    assemble(2, res_copies, store_f)

    for repeat in range(COARSE - 1):
        after = []
        for a, part in enumerate(coarse_parts(iterate)):
            after.append([])
            for h, (x, flux, conduct) in enumerate(part):
                cols = slice(128 * h, 128 * h + 128)
                q = eq[a, :, cols]
                defect = ef[a, :, cols] - (REACTION * x + q * flux)
                after[a].append(x + defect * (DAMPING / (REACTION + q * conduct)))
        iterate = after

    parent_row = (pa // 8) * 2 + (pa % 8) // 4
    low_ob, low_oc = (pa // 2) % 2 == 0, pa % 2 == 0
    for a in range(8):
        one = rows(iterate[a][0] - e0[a, :, 0:128], parent_row)
        two = rows(iterate[a][1] - e0[a, :, 128:256], parent_row)
        value = jnp.where(low_ob, one, two)
        cor[a] = jnp.where(low_oc, value, roll(value, -8))
    spread = exact_dot(jnp.concatenate([cor[a] for a in range(8)], 0), upsample_m[...])
    for a in range(16):
        part = spread[8 * (a // 2) : 8 * (a // 2) + 8]
        va[a + 1] = vb[a + 1] + part

    copies2 = send_faces(2, va)
    own_faces(va, (va, vb))
    begin(va)
    take_faces(asked(2), (va, vb), copies2)

    def into_result(a, h, value):
        both_v[0:8, 256 * a + 128 * h : 256 * a + 128 * h + 128] = value

    smooth(INNER - 1)
    jacobi(va, fr, qr, whole, into_result, 16)

    for copy in (
        x_copies + msgs + [y_first, y_second] + copies0 + copies1 + sol_copies + res_copies + copies2
    ):
        copy.wait_send()


def body(*args):
    count = 30
    vmem = lambda *shape: pltpu.VMEM(shape, F32)
    any_space = pl.BlockSpec(memory_space=pl.ANY)
    both = pl.pallas_call(
        kernel,
        out_shape=pltpu.VMEM((16, 4096), F32),
        in_specs=[any_space] * 8,
        out_specs=pl.BlockSpec(memory_space=pltpu.VMEM),
        scratch_shapes=[
            vmem(3, 8, 4096), vmem(3, 8, 4096),
            pltpu.SMEM((8,), I32), pltpu.SMEM((8,), I32), pltpu.SMEM((8,), I32), pltpu.SMEM((8,), I32),
            pltpu.VMEM((8, 6), I32), vmem(16, 128), vmem(4, 16, 128),
            vmem(32, 2, 128), vmem(32, 2, 128), vmem(32, 4, 128), vmem(32, 4, 128),
            vmem(2, 18, 8, 256), vmem(16, 8, 256), vmem(16, 8, 256),
            vmem(16, 8, 128), vmem(16, 8, 256), vmem(16, 8, 128), vmem(16, 8, 256),
            vmem(6, 8, 256), vmem(4, 6, 8, 256), vmem(2, 4, 8, 256), vmem(2, 4, 8, 256),
            vmem(3, 4, 8, 128), vmem(3, 4, 8, 128), vmem(3, 4, 8, 128),
            vmem(3, 4, 2, 128), vmem(3, 4, 2, 128),
            vmem(16, 8, 256), vmem(16, 8, 256), vmem(8, 8, 256), vmem(8, 8, 256), vmem(8, 8, 256),
            vmem(8, 8, 128), vmem(3, 8, 8, 128),
            pltpu.VMEM((256, 128), BF16), pltpu.VMEM((128, 256), BF16),
            pltpu.SemaphoreType.REGULAR((4,)), pltpu.SemaphoreType.DMA((8,)), pltpu.SemaphoreType.DMA((count,)), pltpu.SemaphoreType.DMA((count,)),
        ],
        compiler_params=pltpu.CompilerParams(
            collective_id=0, has_side_effects=True, vmem_limit_bytes=32 * 1024 * 1024
        ),
    )(*[pltpu.with_memory_space_constraint(a, pltpu.HBM) for a in args])
    return both[:8], both[8:]


def solution(mesh):
    whole, flat = P(("gx", "gy"), None), P(("gx", "gy"))
    return jax.shard_map(
        body,
        mesh=mesh,
        in_specs=(whole, whole, whole, flat, flat, whole, flat, flat),
        out_specs=(whole, whole),
        check_vma=False,
    )
```
